32 devices in a mesh: fsdp: 16 (over z, y, x), dp: 2 (over core).
Axes of the slice: x: 2, y: 2, z: 4, core: 2. Of those that a mesh axis runs over, the one named last changes fastest.
Arguments:
- long_inputs: bfloat16 [128, 128, 768], P(('fsdp', 'dp')), may hold values from -6 to 6
- short_inputs: bfloat16 [128, 64, 768], P(('fsdp', 'dp')), may hold values from -6 to 6
- long_lengths: int32 [128], P(('fsdp', 'dp')), may hold values from 32 to 128, as said below
- short_lengths: int32 [128], P(('fsdp', 'dp')), may hold values from 16 to 64, as said below
- long_cotangent: bfloat16 [128, 128, 768], P(('fsdp', 'dp')), may hold values from -6 to 6
- short_cotangent: bfloat16 [128, 64, 768], P(('fsdp', 'dp')), may hold values from -6 to 6
- query_weight: bfloat16 [768, 768], P('fsdp'), may hold values from -0.3125 to 0.3125
- query_bias: bfloat16 [768], P('fsdp'), may hold values from -1.796875 to 1.796875
- key_weight: bfloat16 [768, 768], P('fsdp'), may hold values from -0.3125 to 0.3125
- value_weight: bfloat16 [768, 768], P('fsdp'), may hold values from -0.21875 to 0.21875
- value_bias: bfloat16 [768], P('fsdp'), may hold values from -1.796875 to 1.796875
- out_weight: bfloat16 [768, 768], P('fsdp'), may hold values from -0.875 to 0.875
- out_bias: bfloat16 [768], P('fsdp'), may hold values from -1.796875 to 1.796875
- first_gain: bfloat16 [768], P('fsdp'), may hold values from 0.5 to 1.5
- first_shift: bfloat16 [768], P('fsdp'), may hold values from -1.796875 to 1.796875
- up_weight: bfloat16 [768, 3072], P('fsdp'), may hold values from -0.21875 to 0.21875
- up_bias: bfloat16 [3072], P('fsdp'), may hold values from -1.796875 to 1.796875
- down_weight: bfloat16 [3072, 768], P('fsdp'), may hold values from -0.109375 to 0.109375
- down_bias: bfloat16 [768], P('fsdp'), may hold values from -1.796875 to 1.796875
- second_gain: bfloat16 [768], P('fsdp'), may hold values from 0.5 to 1.5
- second_shift: bfloat16 [768], P('fsdp'), may hold values from -1.796875 to 1.796875
Outputs:
- long_output: bfloat16 [128, 128, 768], P(('fsdp', 'dp'))
- short_output: bfloat16 [128, 64, 768], P(('fsdp', 'dp'))
- long_input_grad: float32 [128, 128, 768], P(('fsdp', 'dp'))
- short_input_grad: float32 [128, 64, 768], P(('fsdp', 'dp'))
- query_weight_grad: float32 [768, 768], P('fsdp')
- query_bias_grad: float32 [768], P('fsdp')
- key_weight_grad: float32 [768, 768], P('fsdp')
- value_weight_grad: float32 [768, 768], P('fsdp')
- value_bias_grad: float32 [768], P('fsdp')
- out_weight_grad: float32 [768, 768], P('fsdp')
- out_bias_grad: float32 [768], P('fsdp')
- first_gain_grad: float32 [768], P('fsdp')
- first_shift_grad: float32 [768], P('fsdp')
- up_weight_grad: float32 [768, 3072], P('fsdp')
- up_bias_grad: float32 [3072], P('fsdp')
- down_weight_grad: float32 [3072, 768], P('fsdp')
- down_bias_grad: float32 [768], P('fsdp')
- second_gain_grad: float32 [768], P('fsdp')
- second_shift_grad: float32 [768], P('fsdp')
The draws below stay inside these ranges and needn't reach their ends.
Inputs may be any that keep to these rules, and one draw needn't show every extreme that they name: `long_lengths`: real length of each sequence of the first group; at least one sequence has length 128. `short_lengths`: real length of each sequence of the second group; at least one sequence has length 64.
All inputs are finite; a program needn't handle non-finite values.
Results may differ from the reference program's by a relative error of at most 0.015.
The reference program's roundings to bfloat16 on the way count: a program that leaves them out, or rounds other values in their place, can miss the bound.
Values may be sent and summed in bfloat16 or wider, within the bound.
A program may use at most 192 MiB of HBM per device.

```python
import math
import jax
import jax.numpy as jnp
from jax import lax

D = 768
HEADS = 12
HEAD_DIM = 64
FF = 3072
LEN_LONG = 128
LEN_SHORT = 64
LONG_SEQS = 128
SHORT_SEQS = 128


def lengths_for(key, count, longest):
    first_key, second_key = jax.random.split(key)
    drawn = jax.random.randint(first_key, (count,), longest // 4, longest + 1, dtype=jnp.int32)
    chosen = jax.random.randint(second_key, (), 0, count, dtype=jnp.int32)
    placed = jnp.arange(count, dtype=jnp.int32) == chosen
    return jnp.where(placed, jnp.int32(longest), drawn).astype(jnp.int32)


def draw_long_lengths(key, part):
    key = jax.random.fold_in(key, 11)
    return lengths_for(key, LONG_SEQS, LEN_LONG)


def draw_short_lengths(key, part):
    key = jax.random.fold_in(key, 23)
    return lengths_for(key, SHORT_SEQS, LEN_SHORT)


def strengthened(values, own_key, source, target, parts, factor):
    def block_of(position):
        return (jnp.arange(values.shape[position]) // (values.shape[position] // parts)).reshape((-1,) + (1,) * (values.ndim - 1 - position))

    near = jax.random.permutation(own_key, parts)[block_of(target)]
    other_side = (block_of(target) + parts // 2) % parts
    return jnp.where((block_of(source) == near) | (block_of(source) == other_side), factor * values, values)


def level_of(stream_key, extent, cuts, low, high):
    def one(axis_at, blocks):
        heights = jax.random.uniform(jax.random.fold_in(jax.random.fold_in(stream_key, 6), axis_at), (blocks,), jnp.float32, low / len(cuts), high / len(cuts))
        return jnp.repeat(jnp.exp(heights), extent[axis_at] // blocks).reshape((-1,) + (1,) * (len(extent) - axis_at - 1))

    level = one(*cuts[0])
    for cut in cuts[1:]:
        level = level * one(*cut)
    return level


def gaussian(stream_key, shape, deviation, limit, cuts=(), kind=jnp.bfloat16):
    result = deviation * jax.random.normal(stream_key, shape, jnp.float32)
    if cuts:
        result = result * level_of(stream_key, shape, cuts, -0.22, 0.18)
    return jnp.clip(result, -limit, limit).astype(kind)


def heavy_noise(key, extent, deviation, most, cuts, heavy, kind=jnp.bfloat16):
    values = deviation * jax.random.normal(key, extent, jnp.float32)
    if cuts:
        values = values * level_of(key, extent, cuts, -0.22, 0.18)
    return jnp.clip(strengthened(values, jax.random.fold_in(key, 3), *heavy), -most, most).astype(kind)


def setup_inputs(seed: int = 0) -> dict:
    splits = jax.random.split(jax.random.key(seed), 22)
    long_inputs = heavy_noise(splits[0], (LONG_SEQS, LEN_LONG, D), 1.0, 6.0, ((0, 32),), (0, 2, 32, 2.75))
    short_inputs = heavy_noise(splits[1], (SHORT_SEQS, LEN_SHORT, D), 1.0, 6.0, ((0, 32),), (0, 2, 32, 2.75))
    long_lengths = draw_long_lengths(jax.random.fold_in(splits[21], 71), 0)
    short_lengths = draw_short_lengths(jax.random.fold_in(splits[21], 71), 0)
    long_cotangent = gaussian(splits[4], (LONG_SEQS, LEN_LONG, D), 1.0, 6.0, ((0, 32),))
    short_cotangent = gaussian(splits[5], (SHORT_SEQS, LEN_SHORT, D), 1.0, 6.0, ((0, 32),))
    query_weight = gaussian(splits[6], (D, D), (D // 2) ** -0.5, 0.3125, ((0, 16),))
    query_bias = gaussian(splits[7], (D,), 0.3, 1.796875, ((0, 16),))
    key_weight = gaussian(splits[8], (D, D), (D // 2) ** -0.5, 0.3125, ((0, 16),))
    value_weight = gaussian(splits[9], (D, D), D ** -0.5, 0.21875, ((0, 16),))
    value_bias = gaussian(splits[10], (D,), 0.3, 1.796875, ((0, 16),))
    out_weight = gaussian(splits[11], (D, D), (D // 16) ** -0.5, 0.875, ((0, 16),))
    out_bias = gaussian(splits[12], (D,), 0.3, 1.796875, ((0, 16),))
    first_gain = jnp.clip(1.0 + 0.1 * jax.random.normal(splits[13], (D,), jnp.float32), 0.5, 1.5).astype(jnp.bfloat16)
    first_shift = gaussian(splits[14], (D,), 0.3, 1.796875, ((0, 16),))
    up_weight = gaussian(splits[15], (D, FF), D ** -0.5, 0.21875, ((0, 16),))
    up_bias = gaussian(splits[16], (FF,), 0.3, 1.796875, ((0, 16),))
    down_weight = gaussian(splits[17], (FF, D), FF ** -0.5, 0.109375, ((0, 16),))
    down_bias = gaussian(splits[18], (D,), 0.3, 1.796875, ((0, 16),))
    second_gain = jnp.clip(1.0 + 0.1 * jax.random.normal(splits[19], (D,), jnp.float32), 0.5, 1.5).astype(jnp.bfloat16)
    second_shift = gaussian(splits[20], (D,), 0.3, 1.796875, ((0, 16),))
    return {"long_inputs": long_inputs, "short_inputs": short_inputs, "long_lengths": long_lengths, "short_lengths": short_lengths, "long_cotangent": long_cotangent, "short_cotangent": short_cotangent, "query_weight": query_weight, "query_bias": query_bias, "key_weight": key_weight, "value_weight": value_weight, "value_bias": value_bias, "out_weight": out_weight, "out_bias": out_bias, "first_gain": first_gain, "first_shift": first_shift, "up_weight": up_weight, "up_bias": up_bias, "down_weight": down_weight, "down_bias": down_bias, "second_gain": second_gain, "second_shift": second_shift}


@jax.custom_vjp
def low(v):
    return lax.optimization_barrier(v.astype(jnp.bfloat16)).astype(jnp.float32)

@jax.custom_vjp
def low_back(v):
    return v

def low_keep(v):
    return (low(v), None)

def low_pass(kept, grad):
    return (grad,)

def back_keep(v):
    return (v, None)

def back_low(kept, grad):
    return (low(grad),)
low.defvjp(low_keep, low_pass)
low_back.defvjp(back_keep, back_low)
epsilon = 1e-05
masked_score = -1000000000.0

def product(left, right):
    return jnp.dot(left, right, precision=lax.Precision.HIGHEST, preferred_element_type=jnp.float32)

def layer_norm(tensor, scales, offsets):
    centre = lax.optimization_barrier(jnp.mean(tensor, axis=-1, keepdims=True))
    centred = tensor - centre
    spread = lax.optimization_barrier(jnp.mean(centred * centred, axis=-1, keepdims=True))
    return centred * lax.rsqrt(spread + epsilon) * scales + offsets

def block_layer(params, inputs, lengths):
    query_weight, query_bias, key_weight, value_weight, value_bias, out_weight, out_bias, first_gain, first_shift, up_weight, up_bias, down_weight, down_bias, second_gain, second_shift = params
    count, length, width = inputs.shape
    heads_shape = (count, length, HEADS, HEAD_DIM)
    rows = inputs.reshape(count * length, width)
    queries = low(low_back(product(rows, query_weight) + query_bias)).reshape(heads_shape)
    key_rows = low(low_back(product(rows, key_weight))).reshape(heads_shape)
    value_rows = low(low_back(product(rows, value_weight) + value_bias)).reshape(heads_shape)
    score_scale = HEAD_DIM ** (-0.5)
    scores = jnp.einsum('bqhd,bkhd->bhqk', queries, key_rows, precision=lax.Precision.HIGHEST) * score_scale
    scores = low_back(scores)
    live = lax.broadcasted_iota(jnp.int32, (count, length), 1) < lengths[:, None]
    scores = jnp.where(live[:, None, None, :], scores, masked_score)
    highest = lax.optimization_barrier(jnp.max(scores, axis=-1, keepdims=True))
    raised = jnp.exp(scores - highest)
    attention = low(raised / lax.optimization_barrier(jnp.sum(raised, axis=-1, keepdims=True)))
    mixed = jnp.einsum('bhqk,bkhd->bqhd', attention, value_rows, precision=lax.Precision.HIGHEST)
    mixed = low(low_back(mixed.reshape(count * length, width)))
    branch = low_back(product(mixed, out_weight) + out_bias)
    normed = layer_norm(rows + branch, first_gain, first_shift)
    inner = low_back(product(low(normed), up_weight) + up_bias)
    hidden = low(jax.nn.gelu(inner, approximate=False))
    update = low_back(product(hidden, down_weight) + down_bias)
    final = layer_norm(normed + update, second_gain, second_shift)
    return final.reshape(count, length, width)

def group_forward(params, inputs, lengths):
    count, length, width = inputs.shape
    per_block = math.gcd(count, max(1, 4096 // length))
    blocks = inputs.reshape(count // per_block, per_block, length, width)
    lengths_blocked = lengths.reshape(count // per_block, per_block)
    stepper = jax.checkpoint(block_layer)
    outputs = lax.map(lambda pair: stepper(params, pair[0], pair[1]), (blocks, lengths_blocked))
    return outputs.reshape(count, length, width)

def reference(long_inputs, short_inputs, long_lengths, short_lengths, long_cotangent, short_cotangent, query_weight, query_bias, key_weight, value_weight, value_bias, out_weight, out_bias, first_gain, first_shift, up_weight, up_bias, down_weight, down_bias, second_gain, second_shift):
    params = tuple((entry.astype(jnp.float32) for entry in (query_weight, query_bias, key_weight, value_weight, value_bias, out_weight, out_bias, first_gain, first_shift, up_weight, up_bias, down_weight, down_bias, second_gain, second_shift)))

    def forward(weights, long_rows, short_rows):
        return (group_forward(weights, long_rows, long_lengths), group_forward(weights, short_rows, short_lengths))
    outputs, pullback = jax.vjp(forward, params, long_inputs.astype(jnp.float32), short_inputs.astype(jnp.float32))
    grads, long_grad, short_grad = pullback((long_cotangent.astype(jnp.float32), short_cotangent.astype(jnp.float32)))
    return (outputs[0].astype(jnp.bfloat16), outputs[1].astype(jnp.bfloat16), long_grad, short_grad, grads[0], grads[1], grads[2], grads[3], grads[4], grads[5], grads[6], grads[7], grads[8], grads[9], grads[10], grads[11], grads[12], grads[13], grads[14])
```

```python
import functools
import math

import jax
import jax.numpy as jnp
from jax import lax
from jax.experimental import pallas as pl
from jax.experimental.pallas import tpu as pltpu
from jax.sharding import PartitionSpec as P

HEADS = 12
HEAD_DIM = 64
MESH = pl.DeviceIdType.MESH
DMA = pltpu.SemaphoreType.DMA
f32 = jnp.float32
bf16 = jnp.bfloat16

epsilon = 1e-05
masked_score = -1000000000.0


def matmul(left, right):
    return jnp.dot(left, right, preferred_element_type=f32)


def transposed(left, right):
    return lax.dot_general(left, right, (((0,), (0,)), ((), ())), preferred_element_type=f32)


def against(left, right):
    return lax.dot_general(left, right, (((1,), (1,)), ((), ())), preferred_element_type=f32)


def norm_forward(tensor, scales, offsets):
    centre = jnp.mean(tensor, axis=-1, keepdims=True)
    centred = tensor - centre
    inverse = lax.rsqrt(jnp.mean(centred * centred, axis=-1, keepdims=True) + epsilon)
    scaled = centred * inverse
    return (scaled * scales + offsets, scaled, inverse)


def norm_backward(upstream, scaled, inverse, scales):
    delta_scaled = upstream * scales
    plain_mean = jnp.mean(delta_scaled, axis=-1, keepdims=True)
    cross_mean = jnp.mean(delta_scaled * scaled, axis=-1, keepdims=True)
    delta_input = inverse * (delta_scaled - plain_mean - scaled * cross_mean)
    return (delta_input, jnp.sum(upstream * scaled, axis=0), jnp.sum(upstream, axis=0))


def layer_pass(weights, inputs, lengths):
    (
        query_weight,
        query_bias,
        key_weight,
        value_weight,
        value_bias,
        out_weight,
        out_bias,
        first_gain,
        first_shift,
        up_weight,
        up_bias,
        down_weight,
        down_bias,
        second_gain,
        second_shift,
    ) = weights
    count, length, width = inputs.shape
    heads_shape = (count, length, HEADS, HEAD_DIM)
    rows = inputs.reshape(count * length, width)
    queries = (matmul(rows, query_weight) + query_bias).astype(bf16).reshape(heads_shape)
    key_rows = matmul(rows, key_weight).astype(bf16).reshape(heads_shape)
    value_rows = (matmul(rows, value_weight) + value_bias).astype(bf16).reshape(heads_shape)
    score_scale = HEAD_DIM ** (-0.5)
    scores = jnp.einsum("bqhd,bkhd->bhqk", queries, key_rows, preferred_element_type=f32) * score_scale
    live = lax.broadcasted_iota(jnp.int32, (count, length), 1) < lengths[:, None]
    scores = jnp.where(live[:, None, None, :], scores, masked_score)
    highest = jnp.max(scores, axis=-1, keepdims=True)
    raised = jnp.exp(scores - highest)
    attention = raised / jnp.sum(raised, axis=-1, keepdims=True)
    attention_low = attention.astype(bf16)
    mixed = jnp.einsum("bhqk,bkhd->bqhd", attention_low, value_rows, preferred_element_type=f32)
    mixed = mixed.reshape(count * length, width).astype(bf16)
    branch = matmul(mixed, out_weight) + out_bias
    normed, scaled_one, inverse_one = norm_forward(rows.astype(f32) + branch, first_gain, first_shift)
    normed_low = normed.astype(bf16)
    inner = matmul(normed_low, up_weight) + up_bias
    hidden = jax.nn.gelu(inner, approximate=False).astype(bf16)
    update = matmul(hidden, down_weight) + down_bias
    final, scaled_two, inverse_two = norm_forward(normed + update, second_gain, second_shift)
    saved = (
        rows,
        queries,
        key_rows,
        value_rows,
        attention,
        attention_low,
        mixed,
        scaled_one,
        inverse_one,
        normed_low,
        inner,
        hidden,
        scaled_two,
        inverse_two,
    )
    return (final.reshape(count, length, width), saved)


def layer_back(weights, saved, cotangent):
    (
        query_weight,
        query_bias,
        key_weight,
        value_weight,
        value_bias,
        out_weight,
        out_bias,
        first_gain,
        first_shift,
        up_weight,
        up_bias,
        down_weight,
        down_bias,
        second_gain,
        second_shift,
    ) = weights
    (
        rows,
        queries,
        key_rows,
        value_rows,
        attention,
        attention_low,
        mixed,
        scaled_one,
        inverse_one,
        normed_low,
        inner,
        hidden,
        scaled_two,
        inverse_two,
    ) = saved
    count, length, width = cotangent.shape
    heads_shape = (count, length, HEADS, HEAD_DIM)
    score_scale = HEAD_DIM ** (-0.5)
    upstream = cotangent.reshape(count * length, width).astype(f32)
    grad_two, second_gain_term, second_shift_term = norm_backward(upstream, scaled_two, inverse_two, second_gain)
    delta_update = grad_two.astype(bf16)
    down_weight_term = transposed(hidden, delta_update)
    down_bias_term = jnp.sum(delta_update.astype(f32), axis=0)
    _, gelu_pull = jax.vjp(functools.partial(jax.nn.gelu, approximate=False), inner)
    delta_inner = gelu_pull(against(delta_update, down_weight))[0].astype(bf16)
    up_weight_term = transposed(normed_low, delta_inner)
    up_bias_term = jnp.sum(delta_inner.astype(f32), axis=0)
    grad_normed = against(delta_inner, up_weight) + grad_two
    grad_one, first_gain_term, first_shift_term = norm_backward(grad_normed, scaled_one, inverse_one, first_gain)
    delta_branch = grad_one.astype(bf16)
    out_weight_term = transposed(mixed, delta_branch)
    out_bias_term = jnp.sum(delta_branch.astype(f32), axis=0)
    delta_mixed = against(delta_branch, out_weight).astype(bf16).reshape(heads_shape)
    delta_values = jnp.einsum("bhqk,bqhd->bkhd", attention_low, delta_mixed, preferred_element_type=f32)
    delta_values = delta_values.astype(bf16).reshape(count * length, width)
    grad_attention = jnp.einsum("bqhd,bkhd->bhqk", delta_mixed, value_rows, preferred_element_type=f32)
    row_total = jnp.sum(attention * grad_attention, axis=-1, keepdims=True)
    delta_scores = (attention * (grad_attention - row_total)).astype(bf16)
    delta_queries = jnp.einsum("bhqk,bkhd->bqhd", delta_scores, key_rows, preferred_element_type=f32) * score_scale
    delta_queries = delta_queries.astype(bf16).reshape(count * length, width)
    delta_keys = jnp.einsum("bhqk,bqhd->bkhd", delta_scores, queries, preferred_element_type=f32) * score_scale
    delta_keys = delta_keys.astype(bf16).reshape(count * length, width)
    query_weight_term = transposed(rows, delta_queries)
    query_bias_term = jnp.sum(delta_queries.astype(f32), axis=0)
    key_weight_term = transposed(rows, delta_keys)
    value_weight_term = transposed(rows, delta_values)
    value_bias_term = jnp.sum(delta_values.astype(f32), axis=0)
    input_grad = (
        grad_one
        + against(delta_queries, query_weight)
        + against(delta_keys, key_weight)
        + against(delta_values, value_weight)
    )
    terms = (
        query_weight_term,
        query_bias_term,
        key_weight_term,
        value_weight_term,
        value_bias_term,
        out_weight_term,
        out_bias_term,
        first_gain_term,
        first_shift_term,
        up_weight_term,
        up_bias_term,
        down_weight_term,
        down_bias_term,
        second_gain_term,
        second_shift_term,
    )
    return (input_grad.reshape(count, length, width), terms)


class Place:
    def __init__(self):
        chip = lax.axis_index("fsdp")
        core = lax.axis_index("dp")
        z, y, x = chip // 4, (chip // 2) % 2, chip % 2
        self.z, self.y, self.x, self.core = z, y, x, core
        first = 1 - core
        self.own = (y, x)
        self.near = (jnp.where(core == 0, y, 1 - y), jnp.where(core == 0, 1 - x, x))
        self.far = (jnp.where(core == 0, 1 - y, y), jnp.where(core == 0, x, 1 - x))
        self.across = (1 - y, 1 - x)
        self.up = [(z + d) % 4 for d in (1, 2, 3)]
        self.down = [(z + 4 - d) % 4 for d in (1, 2, 3)]
        self.column = [self.device(q, y, x, core) for q in self.up]
        self.near_device = self.device(z, *self.near, core)
        self.far_device = self.device(z, *self.far, core)
        self.partner = self.device(z, y, x, 1 - core)

    def device(self, z, y, x, core):
        return (z * 4 + y * 2 + x, core)

    def greet(self):
        barrier = pltpu.get_barrier_semaphore()
        for peer in self.column + [self.near_device, self.far_device, self.partner]:
            pl.semaphore_signal(barrier, 1, device_id=peer, device_id_type=MESH)
        return barrier


def half(kind, core):
    if kind == "w":
        return (slice(None), pl.ds(pl.multiple_of(core * 384, 128), 384))
    if kind == "d":
        return (slice(None), pl.ds(pl.multiple_of(core * 128, 128), 128))
    return (pl.ds(pl.multiple_of(core * 8, 8), 8), slice(None))


UNIT = {"w": (48, 768), "d": (192, 256), "v": (16, 128)}
HALF = {"w": (48, 384), "d": (192, 128), "v": (8, 128)}
TYPE = {"w": bf16, "d": bf16, "v": f32}
COUNT = {"w": 8, "d": 3, "v": 1}
GATHER = [("v", 0)] + [("w", i) for i in range(8)] + [("d", i) for i in range(3)]
REDUCE = [("d", i) for i in range(3)] + [("w", i) for i in (4, 5, 6, 7, 3, 2, 1, 0)] + [("v", 0)]


class Sender:
    def __init__(self, place):
        self.place = place
        self.started = []

    def copy(self, source, target, send, receive, device):
        return pltpu.make_async_remote_copy(
            source, target, send, receive, device_id=device, device_id_type=MESH
        )

    def send(self, source, target, send, receive, device):
        copy = self.copy(source, target, send, receive, device)
        copy.start()
        self.started.append(copy)

    def arrived(self, target, send, receive):
        self.copy(target, target, send, receive, self.place.partner).wait_recv()

    def finish(self):
        for copy in self.started:
            copy.wait_send()


def gather_kernel(w_in, d_in, v_in, w_out, d_out, v_out, own_s, z_s, z_r, h_s, h_r, p_s, p_r):
    place = Place()
    barrier = place.greet()
    sender = Sender(place)
    whole = {"w": w_out, "d": d_out, "v": v_out}
    given = {"w": w_in, "d": d_in, "v": v_in}
    z, core = place.z, place.core
    local = [
        pltpu.make_async_copy(
            given[kind].at[(i, *half(kind, core))],
            whole[kind].at[(i, z, *place.own, *half(kind, core))],
            own_s.at[n],
        )
        for n, (kind, i) in enumerate(GATHER)
    ]
    for copy in local:
        copy.start()
    pl.semaphore_wait(barrier, 6)

    def unit(n, q):
        kind, i = GATHER[n]
        return whole[kind].at[(i, q, *place.own, *half(kind, core))]

    def column(n, spot, core=core):
        kind, i = GATHER[n]
        return whole[kind].at[(i, slice(None), *spot, *half(kind, core))]

    def first(n):
        local[n].wait()
        for j in range(3):
            sender.send(unit(n, z), unit(n, z), z_s.at[n, j], z_r.at[n, j], place.column[j])

    def pass_on(n, spot, j, to):
        part = column(n, spot)
        sender.send(part, part, h_s.at[n, j], h_r.at[n, j], to)

    def share(n, spot, j):
        part = column(n, spot)
        sender.send(part, part, p_s.at[n, j], p_r.at[n, j], place.partner)

    def second(n):
        for j in range(3):
            sender.arrived(unit(n, place.down[j]), z_s.at[n, j], z_r.at[n, j])
        pass_on(n, place.own, 0, place.near_device)
        pass_on(n, place.own, 1, place.far_device)
        share(n, place.own, 0)

    def third(n):
        sender.arrived(column(n, place.near), h_s.at[n, 0], h_r.at[n, 0])
        pass_on(n, place.near, 2, place.far_device)
        share(n, place.near, 1)
        sender.arrived(column(n, place.far), h_s.at[n, 1], h_r.at[n, 1])
        share(n, place.far, 2)

    def fourth(n):
        sender.arrived(column(n, place.across), h_s.at[n, 2], h_r.at[n, 2])
        share(n, place.across, 3)

    def complete(n):
        for j, spot in enumerate((place.own, place.far, place.near, place.across)):
            sender.arrived(column(n, spot, 1 - core), p_s.at[n, j], p_r.at[n, j])

    count = len(GATHER)
    for step in range(count + 7):
        for late, stage in ((0, first), (1, second), (3, third), (6, fourth), (7, complete)):
            if 0 <= step - late < count:
                stage(step - late)
    sender.finish()


def whole_shape(kind):
    return (COUNT[kind], 4, 2, 2, *UNIT[kind])


def gather(w, d, v):
    n = len(GATHER)
    anywhere = pl.BlockSpec(memory_space=pl.ANY)
    return pl.pallas_call(
        gather_kernel,
        out_shape=[jax.ShapeDtypeStruct(whole_shape(kind), TYPE[kind]) for kind in "wdv"],
        in_specs=[anywhere] * 3,
        out_specs=[anywhere] * 3,
        scratch_shapes=[
            DMA((n,)),
            DMA((n, 3)),
            DMA((n, 3)),
            DMA((n, 3)),
            DMA((n, 3)),
            DMA((n, 4)),
            DMA((n, 4)),
        ],
        compiler_params=pltpu.CompilerParams(
            collective_id=0, has_side_effects=True, vmem_limit_bytes=8 << 20
        ),
        name="gather",
    )(w, d, v)


def static_half(kind, core):
    if kind == "w":
        return (slice(None), slice(384 * core, 384 * core + 384))
    if kind == "d":
        return (slice(None), slice(128 * core, 128 * core + 128))
    return (slice(8 * core, 8 * core + 8), slice(None))


def reduce_kernel(w_in, d_in, v_in, w_out, d_out, v_out, *scratch):
    place = Place()
    barrier = place.greet()
    sender = Sender(place)
    z, core = place.z, place.core
    given = {"w": w_in, "d": d_in, "v": v_in}
    out = {"w": w_out, "d": d_out, "v": v_out}
    total, shared, far, near, high, final = (dict(zip("wdv", scratch[3 * i : 3 * i + 3])) for i in range(6))
    in_s, p_s, p_r, h_s, h_r, z_s, z_r, f_s, f_r, o_s = scratch[18:]
    loads = [
        [
            pltpu.make_async_copy(
                given[kind].at[(i, slice(None), slice(None), slice(None), *static_half(kind, side))],
                total[kind].at[i, side],
                in_s.at[n, side],
            )
            for side in range(2)
        ]
        for n, (kind, i) in enumerate(REDUCE)
    ]
    for pair in loads:
        for load in pair:
            load.start()
    pl.semaphore_wait(barrier, 6)

    def column(n, spot):
        kind, i = REDUCE[n]
        return total[kind].at[(i, core, slice(None), *spot)]

    def add(n, spot, more):
        kind, i = REDUCE[n]
        for q in range(4):
            at = (i, core, q, *spot)
            total[kind][at] = (total[kind][at].astype(f32) + more[q].astype(f32)).astype(TYPE[kind])

    def give(n):
        for load in loads[n]:
            load.wait()
        kind, i = REDUCE[n]
        sender.send(total[kind].at[i, 1 - core], shared[kind].at[i], p_s.at[n], p_r.at[n], place.partner)

    def first(n):
        kind, i = REDUCE[n]
        sender.arrived(shared[kind].at[i], p_s.at[n], p_r.at[n])
        for j, spot in enumerate((place.across, place.far)):
            add(n, spot, shared[kind].at[(i, slice(None), *spot)])
            sender.send(column(n, spot), far[kind].at[i, j], h_s.at[n, j], h_r.at[n, j], place.far_device)
        for spot in (place.near, place.own):
            add(n, spot, shared[kind].at[(i, slice(None), *spot)])

    def second(n):
        kind, i = REDUCE[n]
        sender.arrived(far[kind].at[i, 0], h_s.at[n, 0], h_r.at[n, 0])
        add(n, place.near, far[kind].at[i, 0])
        sender.send(column(n, place.near), near[kind].at[i], h_s.at[n, 2], h_r.at[n, 2], place.near_device)
        sender.arrived(far[kind].at[i, 1], h_s.at[n, 1], h_r.at[n, 1])
        add(n, place.own, far[kind].at[i, 1])

    def third(n):
        kind, i = REDUCE[n]
        sender.arrived(near[kind].at[i], h_s.at[n, 2], h_r.at[n, 2])
        add(n, place.own, near[kind].at[i])
        for j in range(3):
            part = total[kind].at[(i, core, place.up[j], *place.own)]
            sender.send(part, high[kind].at[i, j], z_s.at[n, j], z_r.at[n, j], place.column[j])

    def fourth(n):
        kind, i = REDUCE[n]
        mine = total[kind][(i, core, z, *place.own)].astype(f32)
        for j in range(3):
            sender.arrived(high[kind].at[i, j], z_s.at[n, j], z_r.at[n, j])
            mine = mine + high[kind][i, j].astype(f32)
        final[kind][i, core] = mine
        part = final[kind].at[i, core]
        sender.send(part, part, f_s.at[n], f_r.at[n], place.partner)

    def stores(n):
        kind, i = REDUCE[n]
        return [
            pltpu.make_async_copy(
                final[kind].at[i, side], out[kind].at[(i, *static_half(kind, side))], o_s.at[n, side]
            )
            for side in range(2)
        ]

    def complete(n):
        kind, i = REDUCE[n]
        sender.arrived(final[kind].at[i, 1 - core], f_s.at[n], f_r.at[n])
        for store in stores(n):
            store.start()

    count = len(REDUCE)
    for step in range(count + 5):
        for late, stage in ((0, give), (1, first), (2, second), (3, third), (4, fourth), (5, complete)):
            if 0 <= step - late < count:
                stage(step - late)
    sender.finish()
    for n in range(count):
        for store in stores(n):
            store.wait()


def reduce(w, d, v):
    n = len(REDUCE)
    anywhere = pl.BlockSpec(memory_space=pl.ANY)
    buffers = []
    for lead in ((2, 4, 2, 2), (4, 2, 2), (2, 4), (4,), (3,)):
        buffers += [pltpu.VMEM((COUNT[kind], *lead, *HALF[kind]), TYPE[kind]) for kind in "wdv"]
    buffers += [pltpu.VMEM((COUNT[kind], 2, *HALF[kind]), f32) for kind in "wdv"]
    return pl.pallas_call(
        reduce_kernel,
        out_shape=[jax.ShapeDtypeStruct((COUNT[kind], *UNIT[kind]), f32) for kind in "wdv"],
        in_specs=[anywhere] * 3,
        out_specs=[anywhere] * 3,
        scratch_shapes=buffers
        + [
            DMA((n, 2)),
            DMA((n,)),
            DMA((n,)),
            DMA((n, 3)),
            DMA((n, 3)),
            DMA((n, 3)),
            DMA((n, 3)),
            DMA((n,)),
            DMA((n,)),
            DMA((n, 2)),
        ],
        compiler_params=pltpu.CompilerParams(
            collective_id=1, has_side_effects=True, vmem_limit_bytes=48 << 20
        ),
        name="reduce",
    )(w, d, v)


SMALL = (1, 4, 6, 7, 8, 12, 13, 14)


def gathered_by_kernel(shards):
    wq, wk, wv, wo, up, down = (shards[i] for i in (0, 2, 3, 5, 9, 11))
    w = jnp.concatenate([jnp.stack([wq, wk, wv, wo]), up.reshape(48, 4, 768).transpose(1, 0, 2)])
    d = down.reshape(192, 3, 256).transpose(1, 0, 2)
    small = jnp.pad(jnp.stack([shards[i] for i in SMALL]), ((0, 0), (0, 80)))
    tail = jnp.pad(shards[10], (0, 64)).reshape(2, 128)
    v = jnp.pad(jnp.concatenate([small, tail]), ((0, 6), (0, 0))).astype(f32)[None]
    w, d, v = gather(w, d, v)
    w = w.reshape(8, 768, 768)
    up = w[4:].transpose(1, 0, 2).reshape(768, 3072)
    down = d.reshape(3, 3072, 256).transpose(1, 0, 2).reshape(3072, 768)
    v = v.reshape(16, 16, 128)
    rows = v[:, :8, :48].transpose(1, 0, 2).reshape(8, 768)
    up_bias = v[:, 8:10].reshape(16, 256)[:, :192].reshape(3072)
    vectors = dict(zip(SMALL, rows))
    vectors[10] = up_bias
    matrices = {0: w[0], 2: w[1], 3: w[2], 5: w[3], 9: up, 11: down}
    return tuple((matrices | vectors)[i] for i in range(15))


def reduced_by_kernel(terms):
    parts = [terms[i].astype(bf16) for i in (0, 2, 3, 5)]
    up = terms[9].astype(bf16).reshape(768, 4, 768).transpose(1, 0, 2)
    w = jnp.concatenate([jnp.stack(parts), up]).reshape(whole_shape("w"))
    d = terms[11].astype(bf16).reshape(3072, 3, 256).transpose(1, 0, 2).reshape(whole_shape("d"))
    small = jnp.stack([terms[i] for i in SMALL]).reshape(8, 16, 48).transpose(1, 0, 2)
    small = jnp.pad(small, ((0, 0), (0, 0), (0, 80)))
    tail = jnp.pad(terms[10].reshape(16, 192), ((0, 0), (0, 64))).reshape(16, 2, 128)
    v = jnp.pad(jnp.concatenate([small, tail], axis=1), ((0, 0), (0, 6), (0, 0))).reshape(whole_shape("v"))
    w, d, v = reduce(w, d, v)
    done = {0: w[0], 2: w[1], 3: w[2], 5: w[3]}
    done[9] = w[4:].transpose(1, 0, 2).reshape(48, 3072)
    done[11] = d.transpose(1, 0, 2).reshape(192, 768)
    for at, i in enumerate(SMALL):
        done[i] = v[0, at, :48]
    done[10] = v[0, 8:10].reshape(256)[:192]
    return tuple(done[i] for i in range(15))


def gathered_by_collectives(shards):
    full = tuple(lax.all_gather(shard, "fsdp", axis=0, tiled=True) for shard in shards)
    return tuple(a.astype(f32) if a.ndim == 1 else a for a in full)


def reduced_by_collectives(totals):
    reduced = lax.psum_scatter(totals, "fsdp", scatter_dimension=0, tiled=True)
    low = jax.tree.map(lambda a: a.astype(bf16), reduced)
    return jax.tree.map(lambda a: a.astype(f32), lax.psum(low, "dp"))


def on_device(
    by_kernel,
    long_inputs,
    short_inputs,
    long_lengths,
    short_lengths,
    long_cotangent,
    short_cotangent,
    *shards,
):
    weights = gathered_by_kernel(shards) if by_kernel else gathered_by_collectives(shards)
    long_output, long_saved = layer_pass(weights, long_inputs, long_lengths)
    short_output, short_saved = layer_pass(weights, short_inputs, short_lengths)
    long_grad, long_terms = layer_back(weights, long_saved, long_cotangent)
    short_grad, short_terms = layer_back(weights, short_saved, short_cotangent)
    totals = tuple((first + second for first, second in zip(long_terms, short_terms)))
    reduced = reduced_by_kernel(totals) if by_kernel else reduced_by_collectives(totals)
    return (long_output.astype(bf16), short_output.astype(bf16), long_grad, short_grad, *reduced)


def solution(mesh):
    rows = P(("fsdp", "dp"), None, None)
    count = P(("fsdp", "dp"))
    matrix, vector = P("fsdp", None), P("fsdp")
    params = tuple(matrix if i in (0, 2, 3, 5, 9, 11) else vector for i in range(15))
    by_kernel = mesh.shape["fsdp"] == 16 and mesh.shape["dp"] == 2
    return jax.shard_map(
        functools.partial(on_device, by_kernel),
        mesh=mesh,
        in_specs=(rows, rows, count, count, rows, rows, *params),
        out_specs=(rows, rows, rows, rows, *params),
        check_vma=False,
    )
```

```python
import functools
import math

import jax
import jax.numpy as jnp
from jax import lax
from jax.experimental import pallas as pl
from jax.experimental.pallas import tpu as pltpu
from jax.sharding import PartitionSpec as P

HEADS = 12
HEAD_DIM = 64
MESH = pl.DeviceIdType.MESH
DMA = pltpu.SemaphoreType.DMA
f32 = jnp.float32
bf16 = jnp.bfloat16

epsilon = 1e-05
masked_score = -1000000000.0


def matmul(left, right):
    return jnp.dot(left, right, preferred_element_type=f32)


def transposed(left, right):
    return lax.dot_general(left, right, (((0,), (0,)), ((), ())), preferred_element_type=f32)


def against(left, right):
    return lax.dot_general(left, right, (((1,), (1,)), ((), ())), preferred_element_type=f32)


def norm_forward(tensor, scales, offsets):
    centre = jnp.mean(tensor, axis=-1, keepdims=True)
    centred = tensor - centre
    inverse = lax.rsqrt(jnp.mean(centred * centred, axis=-1, keepdims=True) + epsilon)
    scaled = centred * inverse
    return (scaled * scales + offsets, scaled, inverse)


def norm_backward(upstream, scaled, inverse, scales):
    delta_scaled = upstream * scales
    plain_mean = jnp.mean(delta_scaled, axis=-1, keepdims=True)
    cross_mean = jnp.mean(delta_scaled * scaled, axis=-1, keepdims=True)
    delta_input = inverse * (delta_scaled - plain_mean - scaled * cross_mean)
    return (delta_input, jnp.sum(upstream * scaled, axis=0), jnp.sum(upstream, axis=0))


def layer_pass(weights, inputs, lengths):
    (
        query_weight,
        query_bias,
        key_weight,
        value_weight,
        value_bias,
        out_weight,
        out_bias,
        first_gain,
        first_shift,
        up_weight,
        up_bias,
        down_weight,
        down_bias,
        second_gain,
        second_shift,
    ) = weights
    count, length, width = inputs.shape
    heads_shape = (count, length, HEADS, HEAD_DIM)
    rows = inputs.reshape(count * length, width)
    queries = (matmul(rows, query_weight) + query_bias).astype(bf16).reshape(heads_shape)
    key_rows = matmul(rows, key_weight).astype(bf16).reshape(heads_shape)
    value_rows = (matmul(rows, value_weight) + value_bias).astype(bf16).reshape(heads_shape)
    score_scale = HEAD_DIM ** (-0.5)
    scores = jnp.einsum("bqhd,bkhd->bhqk", queries, key_rows, preferred_element_type=f32) * score_scale
    live = lax.broadcasted_iota(jnp.int32, (count, length), 1) < lengths[:, None]
    scores = jnp.where(live[:, None, None, :], scores, masked_score)
    highest = jnp.max(scores, axis=-1, keepdims=True)
    raised = jnp.exp(scores - highest)
    attention = raised / jnp.sum(raised, axis=-1, keepdims=True)
    attention_low = attention.astype(bf16)
    mixed = jnp.einsum("bhqk,bkhd->bqhd", attention_low, value_rows, preferred_element_type=f32)
    mixed = mixed.reshape(count * length, width).astype(bf16)
    branch = matmul(mixed, out_weight) + out_bias
    normed, scaled_one, inverse_one = norm_forward(rows.astype(f32) + branch, first_gain, first_shift)
    normed_low = normed.astype(bf16)
    inner = matmul(normed_low, up_weight) + up_bias
    hidden = jax.nn.gelu(inner, approximate=False).astype(bf16)
    update = matmul(hidden, down_weight) + down_bias
    final, scaled_two, inverse_two = norm_forward(normed + update, second_gain, second_shift)
    saved = (
        rows,
        queries,
        key_rows,
        value_rows,
        attention,
        attention_low,
        mixed,
        scaled_one,
        inverse_one,
        normed_low,
        inner,
        hidden,
        scaled_two,
        inverse_two,
    )
    return (final.reshape(count, length, width), saved)


def layer_back(weights, saved, cotangent):
    (
        query_weight,
        query_bias,
        key_weight,
        value_weight,
        value_bias,
        out_weight,
        out_bias,
        first_gain,
        first_shift,
        up_weight,
        up_bias,
        down_weight,
        down_bias,
        second_gain,
        second_shift,
    ) = weights
    (
        rows,
        queries,
        key_rows,
        value_rows,
        attention,
        attention_low,
        mixed,
        scaled_one,
        inverse_one,
        normed_low,
        inner,
        hidden,
        scaled_two,
        inverse_two,
    ) = saved
    count, length, width = cotangent.shape
    heads_shape = (count, length, HEADS, HEAD_DIM)
    score_scale = HEAD_DIM ** (-0.5)
    upstream = cotangent.reshape(count * length, width).astype(f32)
    grad_two, second_gain_term, second_shift_term = norm_backward(upstream, scaled_two, inverse_two, second_gain)
    delta_update = grad_two.astype(bf16)
    down_weight_term = transposed(hidden, delta_update)
    down_bias_term = jnp.sum(delta_update.astype(f32), axis=0)
    _, gelu_pull = jax.vjp(functools.partial(jax.nn.gelu, approximate=False), inner)
    delta_inner = gelu_pull(against(delta_update, down_weight))[0].astype(bf16)
    up_weight_term = transposed(normed_low, delta_inner)
    up_bias_term = jnp.sum(delta_inner.astype(f32), axis=0)
    grad_normed = against(delta_inner, up_weight) + grad_two
    grad_one, first_gain_term, first_shift_term = norm_backward(grad_normed, scaled_one, inverse_one, first_gain)
    delta_branch = grad_one.astype(bf16)
    out_weight_term = transposed(mixed, delta_branch)
    out_bias_term = jnp.sum(delta_branch.astype(f32), axis=0)
    delta_mixed = against(delta_branch, out_weight).astype(bf16).reshape(heads_shape)
    delta_values = jnp.einsum("bhqk,bqhd->bkhd", attention_low, delta_mixed, preferred_element_type=f32)
    delta_values = delta_values.astype(bf16).reshape(count * length, width)
    grad_attention = jnp.einsum("bqhd,bkhd->bhqk", delta_mixed, value_rows, preferred_element_type=f32)
    row_total = jnp.sum(attention * grad_attention, axis=-1, keepdims=True)
    delta_scores = (attention * (grad_attention - row_total)).astype(bf16)
    delta_queries = jnp.einsum("bhqk,bkhd->bqhd", delta_scores, key_rows, preferred_element_type=f32) * score_scale
    delta_queries = delta_queries.astype(bf16).reshape(count * length, width)
    delta_keys = jnp.einsum("bhqk,bqhd->bkhd", delta_scores, queries, preferred_element_type=f32) * score_scale
    delta_keys = delta_keys.astype(bf16).reshape(count * length, width)
    query_weight_term = transposed(rows, delta_queries)
    query_bias_term = jnp.sum(delta_queries.astype(f32), axis=0)
    key_weight_term = transposed(rows, delta_keys)
    value_weight_term = transposed(rows, delta_values)
    value_bias_term = jnp.sum(delta_values.astype(f32), axis=0)
    input_grad = (
        grad_one
        + against(delta_queries, query_weight)
        + against(delta_keys, key_weight)
        + against(delta_values, value_weight)
    )
    terms = (
        query_weight_term,
        query_bias_term,
        key_weight_term,
        value_weight_term,
        value_bias_term,
        out_weight_term,
        out_bias_term,
        first_gain_term,
        first_shift_term,
        up_weight_term,
        up_bias_term,
        down_weight_term,
        down_bias_term,
        second_gain_term,
        second_shift_term,
    )
    return (input_grad.reshape(count, length, width), terms)


class Place:
    def __init__(self):
        chip = lax.axis_index("fsdp")
        core = lax.axis_index("dp")
        z, y, x = chip // 4, (chip // 2) % 2, chip % 2
        self.z, self.y, self.x, self.core = z, y, x, core
        first = 1 - core
        self.own = (y, x)
        self.near = (jnp.where(core == 0, y, 1 - y), jnp.where(core == 0, 1 - x, x))
        self.far = (jnp.where(core == 0, 1 - y, y), jnp.where(core == 0, x, 1 - x))
        self.across = (1 - y, 1 - x)
        self.up = [(z + d) % 4 for d in (1, 2, 3)]
        self.down = [(z + 4 - d) % 4 for d in (1, 2, 3)]
        self.column = [self.device(q, y, x, core) for q in self.up]
        self.near_device = self.device(z, *self.near, core)
        self.far_device = self.device(z, *self.far, core)
        self.partner = self.device(z, y, x, 1 - core)

    def device(self, z, y, x, core):
        return (z * 4 + y * 2 + x, core)

    def greet(self):
        barrier = pltpu.get_barrier_semaphore()
        for peer in self.column + [self.near_device, self.far_device, self.partner]:
            pl.semaphore_signal(barrier, 1, device_id=peer, device_id_type=MESH)
        return barrier


def half(kind, core):
    if kind == "w":
        return (slice(None), pl.ds(pl.multiple_of(core * 384, 128), 384))
    if kind == "d":
        return (slice(None), pl.ds(pl.multiple_of(core * 128, 128), 128))
    return (pl.ds(pl.multiple_of(core * 8, 8), 8), slice(None))


UNIT = {"w": (48, 768), "d": (192, 256), "v": (16, 128)}
HALF = {"w": (48, 384), "d": (192, 128), "v": (8, 128)}
TYPE = {"w": bf16, "d": bf16, "v": f32}
COUNT = {"w": 8, "d": 3, "v": 1}
GATHER = [("v", 0)] + [("w", i) for i in range(8)] + [("d", i) for i in range(3)]
REDUCE = [("d", i) for i in range(3)] + [("w", i) for i in (4, 5, 6, 7, 3, 2, 1, 0)] + [("v", 0)]
JOBS = len(GATHER)
SMALL = (1, 4, 6, 7, 8, 12, 13, 14)
QUERY_BIAS, VALUE_BIAS, OUT_BIAS, FIRST_GAIN, FIRST_SHIFT, DOWN_BIAS, SECOND_GAIN, SECOND_SHIFT = range(8)
D = 768
TILE = 192
PAIRS = HEADS // 2
BLOCK = 128


class Sender:
    def __init__(self, place):
        self.place = place
        self.started = []

    def copy(self, source, target, send, receive, device):
        return pltpu.make_async_remote_copy(
            source, target, send, receive, device_id=device, device_id_type=MESH
        )

    def send(self, source, target, send, receive, device):
        copy = self.copy(source, target, send, receive, device)
        copy.start()
        self.started.append(copy)

    def arrived(self, target, send, receive):
        self.copy(target, target, send, receive, self.place.partner).wait_recv()

    def finish(self):
        for copy in self.started:
            copy.wait_send()


class Script:
    def __init__(self, stages):
        self.events = []
        for step in range(JOBS + max(late for late, _ in stages)):
            for at, (late, stage) in enumerate(stages):
                if 0 <= step - late < JOBS:
                    self.events.append((at, step - late, stage))

    def until(self, stage, job):
        while any(at == stage and n == job for at, n, _ in self.events):
            self.one()

    def one(self):
        if self.events:
            _, job, stage = self.events.pop(0)
            stage(job)

    def some(self, count):
        for _ in range(count):
            self.one()

    def rest(self):
        while self.events:
            self.one()


def gather_script(place, sender, given, whole, own_s, z_s, z_r, h_s, h_r, p_s, p_r):
    z, core = place.z, place.core
    local = [
        pltpu.make_async_copy(
            given(kind, i, half(kind, core)),
            whole[kind].at[(i, z, *place.own, *half(kind, core))],
            own_s.at[n],
        )
        for n, (kind, i) in enumerate(GATHER)
    ]
    for copy in local:
        copy.start()

    def unit(n, q):
        kind, i = GATHER[n]
        return whole[kind].at[(i, q, *place.own, *half(kind, core))]

    def column(n, spot, core=core):
        kind, i = GATHER[n]
        return whole[kind].at[(i, slice(None), *spot, *half(kind, core))]

    def pass_on(n, spot, j, to):
        part = column(n, spot)
        sender.send(part, part, h_s.at[n, j], h_r.at[n, j], to)

    def share(n, spot, j):
        part = column(n, spot)
        sender.send(part, part, p_s.at[n, j], p_r.at[n, j], place.partner)

    def first(n):
        local[n].wait()
        for j in range(3):
            sender.send(unit(n, z), unit(n, z), z_s.at[n, j], z_r.at[n, j], place.column[j])

    def second(n):
        for j in range(3):
            sender.arrived(unit(n, place.down[j]), z_s.at[n, j], z_r.at[n, j])
        pass_on(n, place.own, 0, place.near_device)
        pass_on(n, place.own, 1, place.far_device)
        share(n, place.own, 0)

    def third(n):
        sender.arrived(column(n, place.near), h_s.at[n, 0], h_r.at[n, 0])
        pass_on(n, place.near, 2, place.far_device)
        share(n, place.near, 1)
        sender.arrived(column(n, place.far), h_s.at[n, 1], h_r.at[n, 1])
        share(n, place.far, 2)

    def fourth(n):
        sender.arrived(column(n, place.across), h_s.at[n, 2], h_r.at[n, 2])
        share(n, place.across, 3)

    def complete(n):
        for j, spot in enumerate((place.own, place.far, place.near, place.across)):
            sender.arrived(column(n, spot, 1 - core), p_s.at[n, j], p_r.at[n, j])

    return Script(((0, first), (1, second), (2, third), (3, fourth), (4, complete)))


def static_half(kind, core):
    if kind == "w":
        return (slice(None), slice(384 * core, 384 * core + 384))
    if kind == "d":
        return (slice(None), slice(128 * core, 128 * core + 128))
    return (slice(8 * core, 8 * core + 8), slice(None))


def reduce_script(place, sender, total, shared, far, near, high, final, out, p_s, p_r, h_s, h_r, z_s, z_r, f_s, f_r, o_s):
    z, core = place.z, place.core

    def add(n, spot, more):
        kind, i = REDUCE[n]
        ref = total(kind, i)

        def one(q, _):
            at = (core, q, *spot)
            ref[at] = (ref[at].astype(f32) + more[q].astype(f32)).astype(TYPE[kind])
            return 0

        lax.fori_loop(0, 4, one, 0)

    def column(n, spot):
        return total(*REDUCE[n]).at[(core, slice(None), *spot)]

    def give(n):
        kind, i = REDUCE[n]
        sender.send(total(kind, i).at[1 - core], shared[kind].at[i], p_s.at[n], p_r.at[n], place.partner)

    def first(n):
        kind, i = REDUCE[n]
        sender.arrived(shared[kind].at[i], p_s.at[n], p_r.at[n])
        for j, spot in enumerate((place.across, place.far)):
            add(n, spot, shared[kind].at[(i, slice(None), *spot)])
            sender.send(column(n, spot), far[kind].at[i, j], h_s.at[n, j], h_r.at[n, j], place.far_device)
        for spot in (place.near, place.own):
            add(n, spot, shared[kind].at[(i, slice(None), *spot)])

    def second(n):
        kind, i = REDUCE[n]
        sender.arrived(far[kind].at[i, 0], h_s.at[n, 0], h_r.at[n, 0])
        add(n, place.near, far[kind].at[i, 0])
        sender.send(column(n, place.near), near[kind].at[i], h_s.at[n, 2], h_r.at[n, 2], place.near_device)
        sender.arrived(far[kind].at[i, 1], h_s.at[n, 1], h_r.at[n, 1])
        add(n, place.own, far[kind].at[i, 1])

    def third(n):
        kind, i = REDUCE[n]
        sender.arrived(near[kind].at[i], h_s.at[n, 2], h_r.at[n, 2])
        add(n, place.own, near[kind].at[i])
        for j in range(3):
            part = total(kind, i).at[(core, place.up[j], *place.own)]
            sender.send(part, high[kind].at[i, j], z_s.at[n, j], z_r.at[n, j], place.column[j])

    def fourth(n):
        kind, i = REDUCE[n]
        mine = total(kind, i)[(core, z, *place.own)].astype(f32)
        for j in range(3):
            sender.arrived(high[kind].at[i, j], z_s.at[n, j], z_r.at[n, j])
            mine = mine + high[kind][i, j].astype(f32)
        final[kind][i, core] = mine
        part = final[kind].at[i, core]
        sender.send(part, part, f_s.at[n], f_r.at[n], place.partner)

    def stores(n):
        kind, i = REDUCE[n]
        return [
            pltpu.make_async_copy(
                final[kind].at[i, side], out(kind, i, static_half(kind, side)), o_s.at[n, side]
            )
            for side in range(2)
        ]

    def complete(n):
        kind, i = REDUCE[n]
        sender.arrived(final[kind].at[i, 1 - core], f_s.at[n], f_r.at[n])
        for store in stores(n):
            store.start()

    script = Script(((0, give), (1, first), (2, second), (3, third), (4, fourth), (5, complete)))
    script.stores = stores
    return script


def iota(shape, axis):
    return lax.broadcasted_iota(jnp.int32, shape, axis)


def loop(count, body):
    def step(i, _):
        body(i)
        return 0

    lax.fori_loop(0, count, step, 0)


def tile_rows(i):
    return pl.ds(pl.multiple_of(i * TILE, TILE), TILE)


def flat(value):
    return value.reshape(math.prod(value.shape[:-1]), value.shape[-1])


def spread_table():
    return jnp.where(iota((128, D), 1) % 48 == iota((128, D), 0), 1.0, 0.0)


def spread_tables_wide():
    l = iota((128, D), 1) % 192
    j = iota((128, D), 0)
    return jnp.where(l == j, 1.0, 0.0), jnp.where(l == j + 128, 1.0, 0.0)


def wide_rows():
    row = iota((64, D), 0)
    mine = iota((64, D), 1) // 192 == row // 16
    return mine & (row % 16 == 8), mine & (row % 16 == 9)


def total_over(mask, value):
    return jnp.sum(jnp.where(mask, value, 0.0), axis=0, keepdims=True)


def fused_kernel(
    long_lengths,
    short_lengths,
    long_inputs,
    short_inputs,
    long_cotangent,
    short_cotangent,
    wq_in,
    wk_in,
    wv_in,
    wo_in,
    up_in,
    down_in,
    v_in,
    long_output,
    short_output,
    long_grad,
    short_grad,
    wq_out,
    wk_out,
    wv_out,
    wo_out,
    up_out,
    down_out,
    v_out,
    w,
    d,
    v,
    shared_w,
    shared_d,
    shared_v,
    far_w,
    far_d,
    far_v,
    near_w,
    near_d,
    near_v,
    high_w,
    high_d,
    high_v,
    final_w,
    final_d,
    final_v,
    total_d,
    total_v,
    x,
    c,
    q,
    k,
    vl,
    mixed,
    xhat,
    inverse,
    low,
    hidden,
    slope,
    acc,
    delta,
    vec,
    up_bias,
    small,
    up_bias_sum,
    own_s,
    gz_s,
    gz_r,
    gh_s,
    gh_r,
    gp_s,
    gp_r,
    p_s,
    p_r,
    h_s,
    h_r,
    z_s,
    z_r,
    f_s,
    f_r,
    o_s,
    in_s,
    out_s,
):
    place = Place()
    barrier = place.greet()
    sender = Sender(place)
    matrices_in = (wq_in, wk_in, wv_in, wo_in)
    matrices_out = (wq_out, wk_out, wv_out, wo_out)

    def given(kind, i, at):
        rows, cols = at
        if kind == "v":
            return v_in.at[rows, cols]
        core = place.core
        if kind == "d":
            return down_in.at[:, pl.ds(pl.multiple_of(256 * i + core * 128, 128), 128)]
        if i < 4:
            return matrices_in[i].at[rows, cols]
        return up_in.at[:, pl.ds(pl.multiple_of(D * (i - 4) + core * 384, 128), 384)]

    def out(kind, i, at):
        rows, cols = at
        if kind == "v":
            return v_out.at[rows, cols]
        if kind == "d":
            return down_out.at[:, 256 * i + cols.start : 256 * i + cols.stop]
        if i < 4:
            return matrices_out[i].at[rows, cols]
        return up_out.at[:, D * (i - 4) + cols.start : D * (i - 4) + cols.stop]

    def total(kind, i):
        if kind == "d":
            return total_d.at[i]
        if kind == "v":
            return total_v
        return hidden.at[i - 4] if i >= 4 else slope.at[i]

    gathering = gather_script(
        place, sender, given, {"w": w, "d": d, "v": v}, own_s, gz_s, gz_r, gh_s, gh_r, gp_s, gp_r
    )
    reducing = reduce_script(
        place,
        sender,
        total,
        {"w": shared_w, "d": shared_d, "v": shared_v},
        {"w": far_w, "d": far_d, "v": far_v},
        {"w": near_w, "d": near_d, "v": near_v},
        {"w": high_w, "d": high_d, "v": high_v},
        {"w": final_w, "d": final_d, "v": final_v},
        out,
        p_s,
        p_r,
        h_s,
        h_r,
        z_s,
        z_r,
        f_s,
        f_r,
        o_s,
    )

    count, length, _ = long_inputs.shape
    short = short_inputs.shape[1]

    def groups(buffer, long_ref, short_ref, outward, s):
        copies = []
        for i in range(count):
            copies.append((buffer.at[i * length : (i + 1) * length], long_ref.at[i]))
        for i in range(count):
            start = count * length + i * short
            copies.append((buffer.at[start : start + short], short_ref.at[i]))
        return [
            pltpu.make_async_copy(*((a, b) if outward else (b, a)), s.at[i]) for i, (a, b) in enumerate(copies)
        ]

    x_copies = groups(x, long_inputs, short_inputs, False, in_s.at[0])
    c_copies = groups(c, long_cotangent, short_cotangent, False, in_s.at[1])
    for copy in x_copies + c_copies:
        copy.start()
    small[...] = jnp.zeros_like(small)
    up_bias_sum[...] = jnp.zeros_like(up_bias_sum)
    total_v[...] = jnp.zeros_like(total_v)
    pl.semaphore_wait(barrier, 6)

    def weight(i):
        return flat(w[i])

    def row(at):
        return vec[at : at + 1, :]


    def spread():
        wide = matmul(flat(v[0]).astype(bf16), spread_table().astype(bf16))
        mine = iota((256, D), 1) // 48 == iota((256, D), 0) // 16
        vec[...] = jnp.sum(jnp.where(mine, wide, 0.0).reshape(16, 16, D), axis=0)
        table_a, table_b = spread_tables_wide()
        mask_a, mask_b = wide_rows()
        for j in range(4):
            unit = flat(v[0, j]).astype(bf16)
            up_bias[j : j + 1, :] = total_over(mask_a, matmul(unit, table_a.astype(bf16))) + total_over(
                mask_b, matmul(unit, table_b.astype(bf16))
            )

    def project(i, target, bias):
        def one(t):
            rows = tile_rows(t)
            result = matmul(x[rows, :], weight(i))
            if bias is not None:
                result = result + row(bias)
            result = result.astype(bf16)
            for p in range(PAIRS):
                target[p, rows, :] = result[:, 128 * p : 128 * p + 128]

        loop(4, one)

    left_lanes = iota((BLOCK, BLOCK), 1) < HEAD_DIM

    def stacked(value):
        none = jnp.zeros_like(value)
        return jnp.concatenate([jnp.where(left_lanes, value, none), jnp.where(left_lanes, none, value)], axis=0)

    def picked(value):
        return jnp.where(left_lanes, value[:BLOCK], value[BLOCK:])

    def live_keys(b, is_long):
        key = iota((BLOCK, BLOCK), 1)
        if is_long:
            return key < long_lengths[b]
        left = key < short
        limit = jnp.where(left, short_lengths[2 * b], short + short_lengths[2 * b + 1])
        return (key < limit) & (left == (iota((BLOCK, BLOCK), 0) < short))

    def block_rows(b, is_long):
        start = b * BLOCK if is_long else count * length + b * BLOCK
        return pl.ds(pl.multiple_of(start, BLOCK), BLOCK)

    def attention(p, rows, live):
        scores = against(q[p, rows, :], stacked(k[p, rows, :]))
        result = []
        for head in range(2):
            part = jnp.where(live, scores[:, BLOCK * head : BLOCK * head + BLOCK] * HEAD_DIM**-0.5, masked_score)
            raised = jnp.exp(part - jnp.max(part, axis=-1, keepdims=True))
            result.append(raised / jnp.sum(raised, axis=-1, keepdims=True))
        return result

    def attend(b, is_long):
        rows = block_rows(b, is_long)
        live = live_keys(b, is_long)
        for p in range(PAIRS):
            both = jnp.concatenate(attention(p, rows, live), axis=1).astype(bf16)
            mixed[rows, 128 * p : 128 * p + 128] = matmul(both, stacked(vl[p, rows, :])).astype(bf16)

    def first_norm(t):
        rows = tile_rows(t)
        branch = matmul(mixed[rows, :], weight(3)) + row(OUT_BIAS)
        normed, scaled, inv = norm_forward(x[rows, :].astype(f32) + branch, row(FIRST_GAIN), row(FIRST_SHIFT))
        xhat[rows, :] = scaled
        inverse[rows, :] = inv
        low[rows, :] = normed.astype(bf16)

    def put(buffer, j, t, value):
        for side in range(2):
            buffer[j, side, t] = value[:, 384 * side : 384 * side + 384].reshape(2, 2, 48, 384)

    def take(buffer, j, t):
        return jnp.concatenate([flat(buffer[j, side, t]) for side in range(2)], axis=1)

    def take_all(buffer, j):
        return jnp.concatenate([flat(buffer[j, side]) for side in range(2)], axis=1)

    def expand(j):
        def one(t):
            inner = matmul(low[tile_rows(t), :], weight(4 + j)) + up_bias[j : j + 1, :]
            phi = 0.5 + 0.5 * lax.erf(inner * 0.5**0.5)
            put(hidden, j, t, (inner * phi).astype(bf16))
            density = jnp.exp(-0.5 * inner * inner) * (2 * math.pi) ** -0.5
            put(slope, j, t, (phi + inner * density).astype(bf16))

        loop(4, one)

    def contract(n):
        def one(t):
            update = row(DOWN_BIAS)[:, 256 * n : 256 * n + 256]
            for j in range(4):
                update = update + matmul(take(hidden, j, t), flat(d[n, j]))
            acc[tile_rows(t), 256 * n : 256 * n + 256] = update

        loop(4, one)

    def tally(at, value):
        small[at : at + 1, :] += jnp.sum(value, axis=0, keepdims=True)

    def norm_pull(upstream, scaled, inv, gain):
        g = upstream * gain
        plain = jnp.mean(g, axis=-1, keepdims=True)
        cross = jnp.mean(g * scaled, axis=-1, keepdims=True)
        return inv * (g - plain - scaled * cross)

    def second_norm(t):
        rows = tile_rows(t)
        normed = xhat[rows, :] * row(FIRST_GAIN) + row(FIRST_SHIFT)
        final, scaled, inv = norm_forward(normed + acc[rows, :], row(SECOND_GAIN), row(SECOND_SHIFT))
        upstream = c[rows, :].astype(f32)
        c[rows, :] = final.astype(bf16)
        tally(SECOND_GAIN, upstream * scaled)
        tally(SECOND_SHIFT, upstream)
        grad = norm_pull(upstream, scaled, inv, row(SECOND_GAIN))
        acc[rows, :] = grad
        lowered = grad.astype(bf16)
        delta[rows, :] = lowered
        tally(DOWN_BIAS, lowered.astype(f32))


    def down_grad(n):
        def one(j):
            grad = transposed(take_all(hidden, j), delta[:, 256 * n : 256 * n + 256]).astype(bf16)
            for side in range(2):
                total_d[n, side, j] = grad[:, 128 * side : 128 * side + 128].reshape(2, 2, 192, 128)

        loop(4, one)

    def inner_grad(j):
        def one(t):
            rows = tile_rows(t)
            pulled = against(delta[rows, 0:256], flat(d[0, j]))
            for n in (1, 2):
                pulled = pulled + against(delta[rows, 256 * n : 256 * n + 256], flat(d[n, j]))
            inner = (pulled * take(slope, j, t).astype(f32)).astype(bf16)
            put(slope, j, t, inner)
            up_bias_sum[j : j + 1, :] += jnp.sum(inner.astype(f32), axis=0, keepdims=True)

        loop(4, one)

    def weight_grad(left, right, buffer, slot):
        for m in range(2):
            grad = transposed(left[:, 384 * m : 384 * m + 384], right()).astype(bf16)
            for side in range(2):
                part = grad[:, 384 * side : 384 * side + 384]
                buffer[slot, side, 2 * m : 2 * m + 2] = part.reshape(2, 2, 2, 48, 384)

    def up_pull(j):
        def one(t):
            acc[tile_rows(t), :] += against(take(slope, j, t), weight(4 + j))

        loop(4, one)

    def first_pull(t):
        rows = tile_rows(t)
        upstream = acc[rows, :]
        scaled = xhat[rows, :]
        tally(FIRST_GAIN, upstream * scaled)
        tally(FIRST_SHIFT, upstream)
        grad = norm_pull(upstream, scaled, inverse[rows, :], row(FIRST_GAIN))
        acc[rows, :] = grad
        lowered = grad.astype(bf16)
        delta[rows, :] = lowered
        tally(OUT_BIAS, lowered.astype(f32))

    def mixed_pull(t):
        rows = tile_rows(t)
        mixed[rows, :] = against(delta[rows, :], weight(3)).astype(bf16)

    def attend_pull(b, is_long):
        rows = block_rows(b, is_long)
        live = live_keys(b, is_long)
        for p in range(PAIRS):
            probs = attention(p, rows, live)
            down = mixed[rows, 128 * p : 128 * p + 128]
            both = jnp.concatenate(probs, axis=1).astype(bf16)
            grad_values = picked(transposed(both, down))
            grad_probs = against(down, stacked(vl[p, rows, :]))
            parts = []
            for head in range(2):
                part = grad_probs[:, BLOCK * head : BLOCK * head + BLOCK]
                mean = jnp.sum(probs[head] * part, axis=-1, keepdims=True)
                parts.append((probs[head] * (part - mean)).astype(bf16))
            grad_scores = jnp.concatenate(parts, axis=1)
            grad_queries = matmul(grad_scores, stacked(k[p, rows, :])) * HEAD_DIM**-0.5
            grad_keys = picked(transposed(grad_scores, q[p, rows, :])) * HEAD_DIM**-0.5
            q[p, rows, :] = grad_queries.astype(bf16)
            k[p, rows, :] = grad_keys.astype(bf16)
            vl[p, rows, :] = grad_values.astype(bf16)

    def joined(heads):
        return lambda: jnp.concatenate([heads[p] for p in range(PAIRS)], axis=1)

    def head_sum(at, heads):
        for p in range(PAIRS):
            small[at : at + 1, 128 * p : 128 * p + 128] = jnp.sum(heads[p].astype(f32), axis=0, keepdims=True)

    def input_pull(t):
        rows = tile_rows(t)
        grad = acc[rows, :]
        for i, heads in enumerate((q, k, vl)):
            grad = grad + against(jnp.concatenate([heads[p, rows, :] for p in range(PAIRS)], axis=1), weight(i))
        acc[rows, :] = grad

    def exact(left, right):
        return lax.dot_general(
            left, right, (((1,), (1,)), ((), ())), precision=lax.Precision.HIGHEST, preferred_element_type=f32
        )

    def vectors_out():
        mine = iota((16, 8, D), 2) // 48 == iota((16, 8, D), 0)
        pieces = jnp.where(mine, jnp.broadcast_to(small[...][None], (16, 8, D)), 0.0).reshape(128, D)
        total_v[0] = exact(pieces, spread_table()).reshape(4, 2, 2, 8, 128)
        table_a, table_b = spread_tables_wide()
        mask_a, mask_b = wide_rows()
        for j in range(4):
            sums = jnp.broadcast_to(up_bias_sum[j : j + 1, :], (64, D))
            wide = exact(jnp.where(mask_a, sums, 0.0), table_a) + exact(jnp.where(mask_b, sums, 0.0), table_b)
            total_v[1, j] = wide.reshape(2, 2, 16, 128)[:, :, 8:, :]


    complete = 4
    for copy in x_copies:
        copy.wait()
    gathering.until(complete, 0)
    spread()
    for i, (target, bias) in enumerate(((q, QUERY_BIAS), (k, None), (vl, VALUE_BIAS))):
        gathering.until(complete, 1 + i)
        project(i, target, bias)
    for b in range(0, count, 2):
        loop(2, lambda i, b=b: attend(b + i, True))
        gathering.some(2)
    loop(count // 2, lambda b: attend(b, False))
    gathering.until(complete, 4)
    loop(4, first_norm)
    for j in range(4):
        gathering.until(complete, 5 + j)
        expand(j)
    for copy in c_copies:
        copy.wait()
    for n in range(3):
        gathering.until(complete, 9 + n)
        contract(n)
    gathering.rest()
    loop(4, second_norm)
    final_copies = groups(c, long_output, short_output, True, out_s.at[0])
    for copy in final_copies:
        copy.start()

    give, summed = 0, 5
    for n in range(3):
        down_grad(n)
        reducing.until(give, n)
    for j in range(4):
        inner_grad(j)
        weight_grad(low, lambda: take_all(slope, j), hidden, j)
        reducing.until(give, 3 + j)
        up_pull(j)
    loop(4, first_pull)
    weight_grad(mixed, lambda: delta[...], slope, 3)
    reducing.until(give, 7)
    loop(4, mixed_pull)
    for b in range(0, count, 2):
        loop(2, lambda i, b=b: attend_pull(b + i, True))
        reducing.some(2)
    loop(count // 2, lambda b: attend_pull(b, False))
    for i, heads in ((2, vl), (1, k), (0, q)):
        weight_grad(x, joined(heads), slope, i)
        reducing.until(give, 10 - i)
    head_sum(QUERY_BIAS, q)
    head_sum(VALUE_BIAS, vl)
    vectors_out()
    reducing.until(give, 11)
    loop(4, input_pull)
    grad_copies = groups(acc, long_grad, short_grad, True, out_s.at[1])
    for copy in grad_copies:
        copy.start()
    reducing.rest()
    sender.finish()
    for copy in final_copies + grad_copies:
        copy.wait()
    for n in range(JOBS):
        for store in reducing.stores(n):
            store.wait()


def fused(lengths, rows, matrices, vectors):
    long_inputs, short_inputs = rows[:2]
    count = long_inputs.shape[0]
    tokens = count * (long_inputs.shape[1] + short_inputs.shape[1])
    n = JOBS
    anywhere = pl.BlockSpec(memory_space=pl.ANY)
    scalar = pl.BlockSpec(memory_space=pltpu.SMEM)
    spots = (4, 2, 2)
    scratch = [pltpu.VMEM((COUNT[kind], *spots, *UNIT[kind]), TYPE[kind]) for kind in "wdv"]
    for lead in (spots, (2, 4), (4,), (3,)):
        scratch += [pltpu.VMEM((COUNT[kind], *lead, *HALF[kind]), TYPE[kind]) for kind in "wdv"]
    scratch += [pltpu.VMEM((COUNT[kind], 2, *HALF[kind]), f32) for kind in "wdv"]
    scratch += [pltpu.VMEM((3, 2, *spots, *HALF["d"]), bf16), pltpu.VMEM((2, *spots, *HALF["v"]), f32)]
    heads = pltpu.VMEM((PAIRS, tokens, 128), bf16)
    low = pltpu.VMEM((tokens, D), bf16)
    high = pltpu.VMEM((tokens, D), f32)
    wide = pltpu.VMEM((4, 2, *spots, *HALF["w"]), bf16)
    scratch += [low, low, heads, heads, heads, low, high, pltpu.VMEM((tokens, 1), f32), low, wide, wide, high, low]
    scratch += [pltpu.VMEM((16, D), f32), pltpu.VMEM((4, D), f32), pltpu.VMEM((8, D), f32), pltpu.VMEM((4, D), f32)]
    scratch += [DMA((n,))] + [DMA((n, 3))] * 4 + [DMA((n, 4))] * 2
    scratch += [DMA((n,))] * 2 + [DMA((n, 3))] * 4 + [DMA((n,))] * 2 + [DMA((n, 2)), DMA((2, 2 * count)), DMA((2, 2 * count))]
    results = [jax.ShapeDtypeStruct(a.shape, bf16) for a in rows[:2]]
    results += [jax.ShapeDtypeStruct(a.shape, f32) for a in rows[:2]]
    results += [jax.ShapeDtypeStruct(a.shape, f32) for a in matrices]
    results += [jax.ShapeDtypeStruct((16, 128), f32)]
    return pl.pallas_call(
        fused_kernel,
        out_shape=results,
        in_specs=[scalar] * 2 + [anywhere] * 11,
        out_specs=[anywhere] * 11,
        scratch_shapes=scratch,
        compiler_params=pltpu.CompilerParams(
            collective_id=0, has_side_effects=True, vmem_limit_bytes=61 << 20
        ),
        name="layer",
    )(*lengths, *rows, *matrices, vectors)


def layer_by_kernel(long_inputs, short_inputs, long_lengths, short_lengths, long_cotangent, short_cotangent, *shards):
    small = jnp.pad(jnp.stack([shards[i] for i in SMALL]), ((0, 0), (0, 80)))
    tail = jnp.pad(shards[10], (0, 64)).reshape(2, 128)
    vectors = jnp.pad(jnp.concatenate([small, tail]), ((0, 6), (0, 0))).astype(f32)
    *results, wq, wk, wv, wo, up, down, v = fused(
        (long_lengths, short_lengths),
        (long_inputs, short_inputs, long_cotangent, short_cotangent),
        tuple(shards[i] for i in (0, 2, 3, 5, 9, 11)),
        vectors,
    )
    done = {0: wq, 2: wk, 3: wv, 5: wo, 9: up, 11: down}
    for at, i in enumerate(SMALL):
        done[i] = v[at, :48]
    done[10] = v[8:10].reshape(256)[:192]
    return (*results, *(done[i] for i in range(15)))


def gathered_by_collectives(shards):
    full = tuple(lax.all_gather(shard, "fsdp", axis=0, tiled=True) for shard in shards)
    return tuple(a.astype(f32) if a.ndim == 1 else a for a in full)


def reduced_by_collectives(totals):
    reduced = lax.psum_scatter(totals, "fsdp", scatter_dimension=0, tiled=True)
    low = jax.tree.map(lambda a: a.astype(bf16), reduced)
    return jax.tree.map(lambda a: a.astype(f32), lax.psum(low, "dp"))


def layer_by_collectives(
    long_inputs, short_inputs, long_lengths, short_lengths, long_cotangent, short_cotangent, *shards
):
    weights = gathered_by_collectives(shards)
    long_output, long_saved = layer_pass(weights, long_inputs, long_lengths)
    short_output, short_saved = layer_pass(weights, short_inputs, short_lengths)
    long_grad, long_terms = layer_back(weights, long_saved, long_cotangent)
    short_grad, short_terms = layer_back(weights, short_saved, short_cotangent)
    totals = tuple((first + second for first, second in zip(long_terms, short_terms)))
    reduced = reduced_by_collectives(totals)
    return (long_output.astype(bf16), short_output.astype(bf16), long_grad, short_grad, *reduced)


def solution(mesh):
    rows = P(("fsdp", "dp"), None, None)
    count = P(("fsdp", "dp"))
    matrix, vector = P("fsdp", None), P("fsdp")
    params = tuple(matrix if i in (0, 2, 3, 5, 9, 11) else vector for i in range(15))
    by_kernel = mesh.shape["fsdp"] == 16 and mesh.shape["dp"] == 2
    return jax.shard_map(
        layer_by_kernel if by_kernel else layer_by_collectives,
        mesh=mesh,
        in_specs=(rows, rows, count, count, rows, rows, *params),
        out_specs=(rows, rows, rows, rows, *params),
        check_vma=False,
    )
```

```python
import functools
import math

import jax
import jax.numpy as jnp
from jax import lax
from jax.experimental import pallas as pl
from jax.experimental.pallas import tpu as pltpu
from jax.sharding import PartitionSpec as P

HEADS = 12
HEAD_DIM = 64
MESH = pl.DeviceIdType.MESH
DMA = pltpu.SemaphoreType.DMA
f32 = jnp.float32
bf16 = jnp.bfloat16

epsilon = 1e-05
masked_score = -1000000000.0


def matmul(left, right):
    return jnp.dot(left, right, preferred_element_type=f32)


def transposed(left, right):
    return lax.dot_general(left, right, (((0,), (0,)), ((), ())), preferred_element_type=f32)


def against(left, right):
    return lax.dot_general(left, right, (((1,), (1,)), ((), ())), preferred_element_type=f32)


def norm_forward(tensor, scales, offsets):
    centre = jnp.mean(tensor, axis=-1, keepdims=True)
    centred = tensor - centre
    inverse = lax.rsqrt(jnp.mean(centred * centred, axis=-1, keepdims=True) + epsilon)
    scaled = centred * inverse
    return (scaled * scales + offsets, scaled, inverse)


def norm_backward(upstream, scaled, inverse, scales):
    delta_scaled = upstream * scales
    plain_mean = jnp.mean(delta_scaled, axis=-1, keepdims=True)
    cross_mean = jnp.mean(delta_scaled * scaled, axis=-1, keepdims=True)
    delta_input = inverse * (delta_scaled - plain_mean - scaled * cross_mean)
    return (delta_input, jnp.sum(upstream * scaled, axis=0), jnp.sum(upstream, axis=0))


def layer_pass(weights, inputs, lengths):
    (
        query_weight,
        query_bias,
        key_weight,
        value_weight,
        value_bias,
        out_weight,
        out_bias,
        first_gain,
        first_shift,
        up_weight,
        up_bias,
        down_weight,
        down_bias,
        second_gain,
        second_shift,
    ) = weights
    count, length, width = inputs.shape
    heads_shape = (count, length, HEADS, HEAD_DIM)
    rows = inputs.reshape(count * length, width)
    queries = (matmul(rows, query_weight) + query_bias).astype(bf16).reshape(heads_shape)
    key_rows = matmul(rows, key_weight).astype(bf16).reshape(heads_shape)
    value_rows = (matmul(rows, value_weight) + value_bias).astype(bf16).reshape(heads_shape)
    score_scale = HEAD_DIM ** (-0.5)
    scores = jnp.einsum("bqhd,bkhd->bhqk", queries, key_rows, preferred_element_type=f32) * score_scale
    live = lax.broadcasted_iota(jnp.int32, (count, length), 1) < lengths[:, None]
    scores = jnp.where(live[:, None, None, :], scores, masked_score)
    highest = jnp.max(scores, axis=-1, keepdims=True)
    raised = jnp.exp(scores - highest)
    attention = raised / jnp.sum(raised, axis=-1, keepdims=True)
    attention_low = attention.astype(bf16)
    mixed = jnp.einsum("bhqk,bkhd->bqhd", attention_low, value_rows, preferred_element_type=f32)
    mixed = mixed.reshape(count * length, width).astype(bf16)
    branch = matmul(mixed, out_weight) + out_bias
    normed, scaled_one, inverse_one = norm_forward(rows.astype(f32) + branch, first_gain, first_shift)
    normed_low = normed.astype(bf16)
    inner = matmul(normed_low, up_weight) + up_bias
    hidden = jax.nn.gelu(inner, approximate=False).astype(bf16)
    update = matmul(hidden, down_weight) + down_bias
    final, scaled_two, inverse_two = norm_forward(normed + update, second_gain, second_shift)
    saved = (
        rows,
        queries,
        key_rows,
        value_rows,
        attention,
        attention_low,
        mixed,
        scaled_one,
        inverse_one,
        normed_low,
        inner,
        hidden,
        scaled_two,
        inverse_two,
    )
    return (final.reshape(count, length, width), saved)


def layer_back(weights, saved, cotangent):
    (
        query_weight,
        query_bias,
        key_weight,
        value_weight,
        value_bias,
        out_weight,
        out_bias,
        first_gain,
        first_shift,
        up_weight,
        up_bias,
        down_weight,
        down_bias,
        second_gain,
        second_shift,
    ) = weights
    (
        rows,
        queries,
        key_rows,
        value_rows,
        attention,
        attention_low,
        mixed,
        scaled_one,
        inverse_one,
        normed_low,
        inner,
        hidden,
        scaled_two,
        inverse_two,
    ) = saved
    count, length, width = cotangent.shape
    heads_shape = (count, length, HEADS, HEAD_DIM)
    score_scale = HEAD_DIM ** (-0.5)
    upstream = cotangent.reshape(count * length, width).astype(f32)
    grad_two, second_gain_term, second_shift_term = norm_backward(upstream, scaled_two, inverse_two, second_gain)
    delta_update = grad_two.astype(bf16)
    down_weight_term = transposed(hidden, delta_update)
    down_bias_term = jnp.sum(delta_update.astype(f32), axis=0)
    _, gelu_pull = jax.vjp(functools.partial(jax.nn.gelu, approximate=False), inner)
    delta_inner = gelu_pull(against(delta_update, down_weight))[0].astype(bf16)
    up_weight_term = transposed(normed_low, delta_inner)
    up_bias_term = jnp.sum(delta_inner.astype(f32), axis=0)
    grad_normed = against(delta_inner, up_weight) + grad_two
    grad_one, first_gain_term, first_shift_term = norm_backward(grad_normed, scaled_one, inverse_one, first_gain)
    delta_branch = grad_one.astype(bf16)
    out_weight_term = transposed(mixed, delta_branch)
    out_bias_term = jnp.sum(delta_branch.astype(f32), axis=0)
    delta_mixed = against(delta_branch, out_weight).astype(bf16).reshape(heads_shape)
    delta_values = jnp.einsum("bhqk,bqhd->bkhd", attention_low, delta_mixed, preferred_element_type=f32)
    delta_values = delta_values.astype(bf16).reshape(count * length, width)
    grad_attention = jnp.einsum("bqhd,bkhd->bhqk", delta_mixed, value_rows, preferred_element_type=f32)
    row_total = jnp.sum(attention * grad_attention, axis=-1, keepdims=True)
    delta_scores = (attention * (grad_attention - row_total)).astype(bf16)
    delta_queries = jnp.einsum("bhqk,bkhd->bqhd", delta_scores, key_rows, preferred_element_type=f32) * score_scale
    delta_queries = delta_queries.astype(bf16).reshape(count * length, width)
    delta_keys = jnp.einsum("bhqk,bqhd->bkhd", delta_scores, queries, preferred_element_type=f32) * score_scale
    delta_keys = delta_keys.astype(bf16).reshape(count * length, width)
    query_weight_term = transposed(rows, delta_queries)
    query_bias_term = jnp.sum(delta_queries.astype(f32), axis=0)
    key_weight_term = transposed(rows, delta_keys)
    value_weight_term = transposed(rows, delta_values)
    value_bias_term = jnp.sum(delta_values.astype(f32), axis=0)
    input_grad = (
        grad_one
        + against(delta_queries, query_weight)
        + against(delta_keys, key_weight)
        + against(delta_values, value_weight)
    )
    terms = (
        query_weight_term,
        query_bias_term,
        key_weight_term,
        value_weight_term,
        value_bias_term,
        out_weight_term,
        out_bias_term,
        first_gain_term,
        first_shift_term,
        up_weight_term,
        up_bias_term,
        down_weight_term,
        down_bias_term,
        second_gain_term,
        second_shift_term,
    )
    return (input_grad.reshape(count, length, width), terms)


class Place:
    def __init__(self):
        chip = lax.axis_index("fsdp")
        core = lax.axis_index("dp")
        z, y, x = chip // 4, (chip // 2) % 2, chip % 2
        self.z, self.y, self.x, self.core = z, y, x, core
        first = 1 - core
        self.own = (y, x)
        self.near = (jnp.where(core == 0, y, 1 - y), jnp.where(core == 0, 1 - x, x))
        self.far = (jnp.where(core == 0, 1 - y, y), jnp.where(core == 0, x, 1 - x))
        self.across = (1 - y, 1 - x)
        self.up = [(z + d) % 4 for d in (1, 2, 3)]
        self.down = [(z + 4 - d) % 4 for d in (1, 2, 3)]
        self.column = [self.device(q, y, x, core) for q in self.up]
        self.near_device = self.device(z, *self.near, core)
        self.far_device = self.device(z, *self.far, core)
        self.partner = self.device(z, y, x, 1 - core)

    def device(self, z, y, x, core):
        return (z * 4 + y * 2 + x, core)

    def greet(self):
        barrier = pltpu.get_barrier_semaphore()
        for peer in self.column + [self.near_device, self.far_device, self.partner]:
            pl.semaphore_signal(barrier, 1, device_id=peer, device_id_type=MESH)
        return barrier


def half(kind, core):
    if kind == "w":
        return (slice(None), pl.ds(pl.multiple_of(core * 384, 128), 384))
    if kind == "d":
        return (slice(None), pl.ds(pl.multiple_of(core * 128, 128), 128))
    return (pl.ds(pl.multiple_of(core * 8, 8), 8), slice(None))


UNIT = {"w": (48, 768), "d": (192, 256), "v": (16, 128)}
HALF = {"w": (48, 384), "d": (192, 128), "v": (8, 128)}
TYPE = {"w": bf16, "d": bf16, "v": f32}
COUNT = {"w": 8, "d": 3, "v": 1}
GATHER = [("v", 0)] + [("w", i) for i in range(8)] + [("d", i) for i in range(3)]
REDUCE = [("d", i) for i in range(3)] + [("w", i) for i in (4, 5, 6, 7, 3, 2, 1, 0)] + [("v", 0)]
JOBS = len(GATHER)
SMALL = (1, 4, 6, 7, 8, 12, 13, 14)
QUERY_BIAS, VALUE_BIAS, OUT_BIAS, FIRST_GAIN, FIRST_SHIFT, DOWN_BIAS, SECOND_GAIN, SECOND_SHIFT = range(8)
ORDER = (
    "g1.0", "g1.1", "g2.0", "g1.2", "g2.1", "g1.3", "g2.2", "g3.0", "g4.0", "g1.4",
    "g2.3", "g3.1", "g4.1", "g1.5", "g2.4", "g3.2", "g4.2", "g5.0", "g1.6", "g2.5",
    "g3.3", "g4.3", "g5.1", "g6.0", "spread.0", "g1.7", "g2.6", "g3.4", "g4.4", "g5.2",
    "g6.1", "project.0", "g1.8", "g2.7", "g3.5", "g4.5", "g5.3", "g6.2", "project.1", "g1.9",
    "g2.8", "g3.6", "g4.6", "g5.4", "g6.3", "project.2", "attend.0", "g1.10", "g2.9", "g3.7",
    "g4.7", "attend.1", "g5.5", "g6.4", "g1.11", "g2.10", "attend.2", "g3.8", "g4.8", "g5.6",
    "g6.5", "first_norm.0", "expand.0", "g2.11", "g3.9", "g4.9", "g5.7", "g6.6", "expand.1", "g3.10",
    "g4.10", "g5.8", "g6.7", "expand.2", "g3.11", "g4.11", "g5.9", "g6.8", "expand.3", "g5.10",
    "g6.9", "contract.0", "g5.11", "g6.10", "contract.1", "g6.11", "contract.2", "second_norm.0", "down_grad.0", "r0.0",
    "down_grad.1", "r0.1", "down_grad.2", "r0.2", "inner_grad.0", "up_grad.0", "r1.0", "r0.3", "inner_grad.1", "up_grad.1",
    "r1.1", "r0.4", "inner_grad.2", "up_grad.2", "r1.2", "r2.0", "r0.5", "inner_grad.3", "up_grad.3", "r1.3",
    "r2.1", "r0.6", "up_pull.0", "r1.4", "r2.2", "r3.0", "first_pull.0", "out_grad.0", "r0.7", "mixed_pull.0",
    "attend_pull.0", "r1.5", "r2.3", "r3.1", "r4.0", "attend_pull.1", "attend_pull.2", "attend_pull.3", "attend_pull.4", "attend_pull.5",
    "head_grad.0", "r0.8", "head_grad.1", "r1.6", "r2.4", "r3.2", "r4.1", "r0.9", "head_grad.2", "r1.7",
    "r2.5", "r3.3", "r4.2", "r0.10", "vectors.0", "r1.8", "r2.6", "r3.4", "r4.3", "r0.11",
    "input_pull.0", "r1.9", "r2.7", "r3.5", "r4.4", "input_pull.1", "r1.10", "r2.8", "r3.6", "r4.5",
    "r1.11", "r2.9", "r3.7", "r4.6", "r2.10", "r3.8", "r4.7", "r2.11", "r3.9", "r4.8",
    "r3.10", "r4.9", "r3.11", "r4.10", "r4.11",
)
D = 768
TILE = 192
PAIRS = HEADS // 2
BLOCK = 128


class Sender:
    def __init__(self, place):
        self.place = place
        self.started = []

    def copy(self, source, target, send, receive, device):
        return pltpu.make_async_remote_copy(
            source, target, send, receive, device_id=device, device_id_type=MESH
        )

    def send(self, source, target, send, receive, device):
        copy = self.copy(source, target, send, receive, device)
        copy.start()
        self.started.append(copy)

    def arrived(self, target, send, receive):
        self.copy(target, target, send, receive, self.place.partner).wait_recv()

    def finish(self):
        for copy in self.started:
            copy.wait_send()


def gather_steps(place, sender, given, whole, own_s, z_s, z_r, h_s, h_r, p_s, p_r):
    z, core = place.z, place.core
    local = [
        pltpu.make_async_copy(
            given(kind, i, half(kind, core)),
            whole[kind].at[(i, z, *place.own, *half(kind, core))],
            own_s.at[n],
        )
        for n, (kind, i) in enumerate(GATHER)
    ]
    for copy in local:
        copy.start()

    def unit(n, q):
        kind, i = GATHER[n]
        return whole[kind].at[(i, q, *place.own, *half(kind, core))]

    def column(n, spot, core=core):
        kind, i = GATHER[n]
        return whole[kind].at[(i, slice(None), *spot, *half(kind, core))]

    def pass_on(n, spot, j, to):
        part = column(n, spot)
        sender.send(part, part, h_s.at[n, j], h_r.at[n, j], to)

    def share(n, spot, j):
        part = column(n, spot)
        sender.send(part, part, p_s.at[n, j], p_r.at[n, j], place.partner)

    def first(n):
        local[n].wait()
        for j in range(3):
            sender.send(unit(n, z), unit(n, z), z_s.at[n, j], z_r.at[n, j], place.column[j])

    def second(n):
        for j in range(3):
            sender.arrived(unit(n, place.down[j]), z_s.at[n, j], z_r.at[n, j])
        pass_on(n, place.own, 0, place.near_device)
        pass_on(n, place.own, 1, place.far_device)
        share(n, place.own, 0)

    def third(n):
        sender.arrived(column(n, place.near), h_s.at[n, 0], h_r.at[n, 0])
        pass_on(n, place.near, 2, place.far_device)
        share(n, place.near, 1)

    def fourth(n):
        sender.arrived(column(n, place.far), h_s.at[n, 1], h_r.at[n, 1])
        share(n, place.far, 2)

    def fifth(n):
        sender.arrived(column(n, place.across), h_s.at[n, 2], h_r.at[n, 2])
        share(n, place.across, 3)

    def complete(n):
        for j, spot in enumerate((place.own, place.far, place.near, place.across)):
            sender.arrived(column(n, spot, 1 - core), p_s.at[n, j], p_r.at[n, j])

    return {"g1": first, "g2": second, "g3": third, "g4": fourth, "g5": fifth, "g6": complete}


def reduce_steps(place, sender, total, shared, far, near, high, final, out, p_s, p_r, h_s, h_r, z_s, z_r, f_s, f_r, o_s):
    z, core = place.z, place.core

    def add(n, spot, more):
        kind, i = REDUCE[n]
        ref = total(kind, i)

        def one(q, _):
            at = (core, q, *spot)
            ref[at] = (ref[at].astype(f32) + more[q].astype(f32)).astype(TYPE[kind])
            return 0

        lax.fori_loop(0, 4, one, 0)

    def column(n, spot):
        return total(*REDUCE[n]).at[(core, slice(None), *spot)]

    def give(n):
        kind, i = REDUCE[n]
        sender.send(total(kind, i).at[1 - core], shared[kind].at[i], p_s.at[n], p_r.at[n], place.partner)

    def first(n):
        kind, i = REDUCE[n]
        sender.arrived(shared[kind].at[i], p_s.at[n], p_r.at[n])
        for j, spot in enumerate((place.across, place.far)):
            add(n, spot, shared[kind].at[(i, slice(None), *spot)])
            sender.send(column(n, spot), far[kind].at[i, j], h_s.at[n, j], h_r.at[n, j], place.far_device)
        for spot in (place.near, place.own):
            add(n, spot, shared[kind].at[(i, slice(None), *spot)])

    def second(n):
        kind, i = REDUCE[n]
        sender.arrived(far[kind].at[i, 0], h_s.at[n, 0], h_r.at[n, 0])
        add(n, place.near, far[kind].at[i, 0])
        sender.send(column(n, place.near), near[kind].at[i], h_s.at[n, 2], h_r.at[n, 2], place.near_device)

    def third(n):
        kind, i = REDUCE[n]
        sender.arrived(far[kind].at[i, 1], h_s.at[n, 1], h_r.at[n, 1])
        add(n, place.own, far[kind].at[i, 1])
        sender.arrived(near[kind].at[i], h_s.at[n, 2], h_r.at[n, 2])
        add(n, place.own, near[kind].at[i])
        for j in range(3):
            part = total(kind, i).at[(core, place.up[j], *place.own)]
            sender.send(part, high[kind].at[i, j], z_s.at[n, j], z_r.at[n, j], place.column[j])

    def fourth(n):
        kind, i = REDUCE[n]
        mine = total(kind, i)[(core, z, *place.own)].astype(f32)
        for j in range(3):
            sender.arrived(high[kind].at[i, j], z_s.at[n, j], z_r.at[n, j])
            mine = mine + high[kind][i, j].astype(f32)
        final[kind][i] = mine
        mine_out = out(kind, i, core)
        sender.send(final[kind].at[i], mine_out, f_s.at[n], f_r.at[n], place.partner)
        pltpu.make_async_copy(final[kind].at[i], mine_out, o_s.at[n]).start()

    def stored(n):
        kind, i = REDUCE[n]
        pltpu.make_async_copy(final[kind].at[i], out(kind, i, core), o_s.at[n]).wait()
        sender.arrived(out(kind, i, 1 - core), f_s.at[n], f_r.at[n])

    return {"r0": give, "r1": first, "r2": second, "r3": third, "r4": fourth, "r5": stored}


def iota(shape, axis):
    return lax.broadcasted_iota(jnp.int32, shape, axis)


def loop(count, body):
    def step(i, _):
        body(i)
        return 0

    lax.fori_loop(0, count, step, 0)


def tile_rows(i):
    return pl.ds(pl.multiple_of(i * TILE, TILE), TILE)


def flat(value):
    return value.reshape(math.prod(value.shape[:-1]), value.shape[-1])


def spread_table():
    return jnp.where(iota((128, D), 1) % 48 == iota((128, D), 0), 1.0, 0.0)


def spread_tables_wide():
    l = iota((128, D), 1) % 192
    j = iota((128, D), 0)
    return jnp.where(l == j, 1.0, 0.0), jnp.where(l == j + 128, 1.0, 0.0)


def wide_rows():
    row = iota((64, D), 0)
    mine = iota((64, D), 1) // 192 == row // 16
    return mine & (row % 16 == 8), mine & (row % 16 == 9)


def total_over(mask, value):
    return jnp.sum(jnp.where(mask, value, 0.0), axis=0, keepdims=True)


def fused_kernel(
    long_lengths,
    short_lengths,
    long_inputs,
    short_inputs,
    long_cotangent,
    short_cotangent,
    wq_in,
    wk_in,
    wv_in,
    wo_in,
    up_in,
    down_in,
    v_in,
    long_output,
    short_output,
    long_grad,
    short_grad,
    wq_out,
    wk_out,
    wv_out,
    wo_out,
    up_out,
    down_out,
    v_out,
    w,
    d,
    v,
    shared_w,
    shared_d,
    shared_v,
    far_w,
    far_d,
    far_v,
    near_w,
    near_d,
    near_v,
    high_w,
    high_d,
    high_v,
    final_w,
    final_d,
    final_v,
    total_d,
    total_v,
    x,
    c,
    q,
    k,
    vl,
    mixed,
    xhat,
    inverse,
    low,
    hidden,
    slope,
    acc,
    delta,
    vec,
    stats,
    up_bias,
    small,
    up_bias_sum,
    own_s,
    gz_s,
    gz_r,
    gh_s,
    gh_r,
    gp_s,
    gp_r,
    p_s,
    p_r,
    h_s,
    h_r,
    z_s,
    z_r,
    f_s,
    f_r,
    o_s,
    in_s,
    out_s,
):
    place = Place()
    barrier = place.greet()
    sender = Sender(place)
    matrices_in = (wq_in, wk_in, wv_in, wo_in)
    matrices_out = (wq_out, wk_out, wv_out, wo_out)

    def given(kind, i, at):
        rows, cols = at
        if kind == "v":
            return v_in.at[rows, cols]
        core = place.core
        if kind == "d":
            return down_in.at[:, pl.ds(pl.multiple_of(256 * i + core * 128, 128), 128)]
        if i < 4:
            return matrices_in[i].at[rows, cols]
        return up_in.at[:, pl.ds(pl.multiple_of(D * (i - 4) + core * 384, 128), 384)]

    def out(kind, i, core):
        rows, cols = half(kind, core)
        if kind == "v":
            return v_out.at[rows, cols]
        if kind == "d":
            return down_out.at[:, pl.ds(pl.multiple_of(256 * i + core * 128, 128), 128)]
        if i < 4:
            return matrices_out[i].at[rows, cols]
        return up_out.at[:, pl.ds(pl.multiple_of(D * (i - 4) + core * 384, 128), 384)]

    def total(kind, i):
        if kind == "d":
            return total_d.at[i]
        if kind == "v":
            return total_v
        return hidden.at[i - 4] if i >= 4 else slope.at[i]

    steps = gather_steps(
        place, sender, given, {"w": w, "d": d, "v": v}, own_s, gz_s, gz_r, gh_s, gh_r, gp_s, gp_r
    )
    steps |= reduce_steps(
        place,
        sender,
        total,
        {"w": shared_w, "d": shared_d, "v": shared_v},
        {"w": far_w, "d": far_d, "v": far_v},
        {"w": near_w, "d": near_d, "v": near_v},
        {"w": high_w, "d": high_d, "v": high_v},
        {"w": final_w, "d": final_d, "v": final_v},
        out,
        p_s,
        p_r,
        h_s,
        h_r,
        z_s,
        z_r,
        f_s,
        f_r,
        o_s,
    )

    count, length, _ = long_inputs.shape
    short = short_inputs.shape[1]

    def groups(buffer, long_ref, short_ref, outward, s):
        copies = []
        for i in range(count):
            copies.append((buffer.at[i * length : (i + 1) * length], long_ref.at[i]))
        for i in range(count):
            start = count * length + i * short
            copies.append((buffer.at[start : start + short], short_ref.at[i]))
        return [
            pltpu.make_async_copy(*((a, b) if outward else (b, a)), s.at[i]) for i, (a, b) in enumerate(copies)
        ]

    x_copies = groups(x, long_inputs, short_inputs, False, in_s.at[0])
    c_copies = groups(c, long_cotangent, short_cotangent, False, in_s.at[1])
    for copy in x_copies + c_copies:
        copy.start()
    small[...] = jnp.zeros_like(small)
    up_bias_sum[...] = jnp.zeros_like(up_bias_sum)
    total_v[...] = jnp.zeros_like(total_v)
    pl.semaphore_wait(barrier, 6)

    def weight(i):
        return flat(w[i])

    def row(at):
        return vec[at : at + 1, :]


    def spread():
        wide = matmul(flat(v[0]).astype(bf16), spread_table().astype(bf16))
        mine = iota((256, D), 1) // 48 == iota((256, D), 0) // 16
        vec[...] = jnp.sum(jnp.where(mine, wide, 0.0).reshape(16, 16, D), axis=0)
        table_a, table_b = spread_tables_wide()
        mask_a, mask_b = wide_rows()
        for j in range(4):
            unit = flat(v[0, j]).astype(bf16)
            up_bias[j : j + 1, :] = total_over(mask_a, matmul(unit, table_a.astype(bf16))) + total_over(
                mask_b, matmul(unit, table_b.astype(bf16))
            )

    def project(i, target, bias, scale=1.0):
        result = matmul(x[...], weight(i))
        if bias is not None:
            result = result + row(bias)
        result = (result.astype(bf16) * scale).astype(bf16)
        for p in range(PAIRS):
            target[p] = result[:, 128 * p : 128 * p + 128]

    left_lanes = iota((BLOCK, BLOCK), 1) < HEAD_DIM

    def stacked(value):
        none = jnp.zeros_like(value)
        return jnp.concatenate([jnp.where(left_lanes, value, none), jnp.where(left_lanes, none, value)], axis=0)

    def picked(value):
        return jnp.where(left_lanes, value[:BLOCK], value[BLOCK:])

    def live_keys(b, is_long):
        key = iota((BLOCK, BLOCK), 0)
        if is_long:
            return key < long_lengths[b]
        left = key < short
        limit = jnp.where(left, short_lengths[2 * b], short + short_lengths[2 * b + 1])
        return (key < limit) & (left == (iota((BLOCK, BLOCK), 1) < short))

    def block_rows(b, is_long):
        start = b * BLOCK if is_long else count * length + b * BLOCK
        return pl.ds(pl.multiple_of(start, BLOCK), BLOCK)

    def block_scores(p, rows, live):
        scores = against(stacked(k[p, rows, :]), q[p, rows, :])
        return [jnp.where(live, scores[BLOCK * head : BLOCK * head + BLOCK], masked_score) for head in range(2)]

    def attend(b, is_long):
        rows = block_rows(b, is_long)
        live = live_keys(b, is_long)
        at = b if is_long else b + count
        results = []
        for p in range(PAIRS):
            parts = []
            for head, part in enumerate(block_scores(p, rows, live)):
                highest = jnp.max(part, axis=0, keepdims=True)
                raised = jnp.exp(part - highest)
                scale = 1.0 / jnp.sum(raised, axis=0, keepdims=True)
                stats[at, 2 * p + head : 2 * p + head + 1, :] = highest
                stats[at, HEADS + 2 * p + head : HEADS + 2 * p + head + 1, :] = scale
                parts.append((raised * scale).astype(bf16))
            both = jnp.concatenate(parts, axis=0)
            results.append(transposed(both, stacked(vl[p, rows, :])).astype(bf16))
        mixed[rows, :] = jnp.concatenate(results, axis=1)

    def branch():
        acc[...] = matmul(mixed[...], weight(3)) + row(OUT_BIAS)

    def first_norm(t):
        rows = tile_rows(t)
        normed, scaled, inv = norm_forward(x[rows, :].astype(f32) + acc[rows, :], row(FIRST_GAIN), row(FIRST_SHIFT))
        xhat[rows, :] = scaled
        inverse[rows, :] = inv
        low[rows, :] = normed.astype(bf16)

    def put(buffer, j, value):
        for side in range(2):
            buffer[j, side] = value[:, 384 * side : 384 * side + 384].reshape(4, 2, 2, 48, 384)

    def take(buffer, j):
        return jnp.concatenate([flat(buffer[j, side]) for side in range(2)], axis=1)

    def expand(j):
        inner = matmul(low[...], weight(4 + j)) + up_bias[j : j + 1, :]
        phi = 0.5 + 0.5 * lax.erf(inner * 0.5**0.5)
        put(hidden, j, (inner * phi).astype(bf16))
        density = jnp.exp(-0.5 * inner * inner) * (2 * math.pi) ** -0.5
        put(slope, j, (phi + inner * density).astype(bf16))

    def contract(n):
        update = row(DOWN_BIAS)[:, 256 * n : 256 * n + 256]
        for j in range(4):
            update = update + matmul(take(hidden, j), flat(d[n, j]))
        acc[:, 256 * n : 256 * n + 256] = update

    def tally(at, value):
        small[at : at + 1, :] += jnp.sum(value, axis=0, keepdims=True)

    def norm_pull(upstream, scaled, inv, gain):
        g = upstream * gain
        plain = jnp.mean(g, axis=-1, keepdims=True)
        cross = jnp.mean(g * scaled, axis=-1, keepdims=True)
        return inv * (g - plain - scaled * cross)

    def second_norm(t):
        rows = tile_rows(t)
        normed = xhat[rows, :] * row(FIRST_GAIN) + row(FIRST_SHIFT)
        final, scaled, inv = norm_forward(normed + acc[rows, :], row(SECOND_GAIN), row(SECOND_SHIFT))
        upstream = c[rows, :].astype(f32)
        c[rows, :] = final.astype(bf16)
        tally(SECOND_GAIN, upstream * scaled)
        tally(SECOND_SHIFT, upstream)
        grad = norm_pull(upstream, scaled, inv, row(SECOND_GAIN))
        acc[rows, :] = grad
        lowered = grad.astype(bf16)
        delta[rows, :] = lowered
        tally(DOWN_BIAS, lowered.astype(f32))


    def down_grad(n):
        for j in range(4):
            grad = transposed(take(hidden, j), delta[:, 256 * n : 256 * n + 256]).astype(bf16)
            for side in range(2):
                total_d[n, side, j] = grad[:, 128 * side : 128 * side + 128].reshape(2, 2, 192, 128)

    def inner_grad(j):
        pulled = against(delta[...], jnp.concatenate([flat(d[n, j]) for n in range(3)], axis=1))
        inner = (pulled * take(slope, j).astype(f32)).astype(bf16)
        put(slope, j, inner)
        up_bias_sum[j : j + 1, :] = jnp.sum(inner.astype(f32), axis=0, keepdims=True)

    def weight_grad(left, right, buffer, slot):
        put(buffer, slot, transposed(left[...], right()).astype(bf16))

    def up_pull():
        grad = acc[...]
        for j in range(4):
            grad = grad + against(take(slope, j), weight(4 + j))
        acc[...] = grad

    def first_pull(t):
        rows = tile_rows(t)
        upstream = acc[rows, :]
        scaled = xhat[rows, :]
        tally(FIRST_GAIN, upstream * scaled)
        tally(FIRST_SHIFT, upstream)
        grad = norm_pull(upstream, scaled, inverse[rows, :], row(FIRST_GAIN))
        acc[rows, :] = grad
        lowered = grad.astype(bf16)
        delta[rows, :] = lowered
        tally(OUT_BIAS, lowered.astype(f32))

    def mixed_pull():
        mixed[...] = against(delta[...], weight(3)).astype(bf16)

    def attend_pull(b, is_long):
        rows = block_rows(b, is_long)
        live = live_keys(b, is_long)
        at = b if is_long else b + count
        results = []
        for p in range(PAIRS):
            down = mixed[rows, 128 * p : 128 * p + 128]
            probs = []
            for head, part in enumerate(block_scores(p, rows, live)):
                highest = stats[at, 2 * p + head : 2 * p + head + 1, :]
                scale = stats[at, HEADS + 2 * p + head : HEADS + 2 * p + head + 1, :]
                probs.append(jnp.exp(part - highest) * scale)
            both = jnp.concatenate(probs, axis=0).astype(bf16)
            grad_values = picked(matmul(both, down))
            grad_probs = against(stacked(vl[p, rows, :]), down)
            parts = []
            for head in range(2):
                part = grad_probs[BLOCK * head : BLOCK * head + BLOCK]
                mean = jnp.sum(probs[head] * part, axis=0, keepdims=True)
                parts.append((probs[head] * (part - mean)).astype(bf16))
            grad_scores = jnp.concatenate(parts, axis=0)
            grad_queries = transposed(grad_scores, stacked(k[p, rows, :])) * HEAD_DIM**-0.5
            grad_keys = picked(matmul(grad_scores, q[p, rows, :]))
            results.append((grad_queries.astype(bf16), grad_keys.astype(bf16), grad_values.astype(bf16)))
        for p, (grad_queries, grad_keys, grad_values) in enumerate(results):
            q[p, rows, :] = grad_queries
            k[p, rows, :] = grad_keys
            vl[p, rows, :] = grad_values

    def joined(heads):
        return lambda: jnp.concatenate([heads[p] for p in range(PAIRS)], axis=1)

    def head_sum(at, heads):
        for p in range(PAIRS):
            small[at : at + 1, 128 * p : 128 * p + 128] = jnp.sum(heads[p].astype(f32), axis=0, keepdims=True)

    def input_pull(t):
        rows = slice(384 * t, 384 * t + 384)
        grad = acc[rows, :]
        for i, heads in enumerate((q, k, vl)):
            grad = grad + against(jnp.concatenate([heads[p, rows, :] for p in range(PAIRS)], axis=1), weight(i))
        acc[rows, :] = grad

    def exact(left, right):
        return lax.dot_general(
            left, right, (((1,), (1,)), ((), ())), precision=lax.Precision.HIGHEST, preferred_element_type=f32
        )

    def vectors_out():
        mine = iota((16, 8, D), 2) // 48 == iota((16, 8, D), 0)
        pieces = jnp.where(mine, jnp.broadcast_to(small[...][None], (16, 8, D)), 0.0).reshape(128, D)
        total_v[0] = exact(pieces, spread_table()).reshape(4, 2, 2, 8, 128)
        table_a, table_b = spread_tables_wide()
        mask_a, mask_b = wide_rows()
        for j in range(4):
            sums = jnp.broadcast_to(up_bias_sum[j : j + 1, :], (64, D))
            wide = exact(jnp.where(mask_a, sums, 0.0), table_a) + exact(jnp.where(mask_b, sums, 0.0), table_b)
            total_v[1, j] = wide.reshape(2, 2, 16, 128)[:, :, 8:, :]


    def wait_all(copies):
        for copy in copies:
            copy.wait()

    def start_all(copies):
        for copy in copies:
            copy.start()

    final_copies = groups(c, long_output, short_output, True, out_s.at[0])
    grad_copies = groups(acc, long_grad, short_grad, True, out_s.at[1])

    def project_all(i):
        if i == 0:
            wait_all(x_copies)
        project(i, (q, k, vl)[i], (QUERY_BIAS, None, VALUE_BIAS)[i], HEAD_DIM**-0.5 if i == 0 else 1.0)

    def attend_all(i):
        if 2 * i < count:
            loop(2, lambda b: attend(2 * i + b, True))
        else:
            loop(count // 2, lambda b: attend(b, False))

    def normalise():
        branch()
        loop(4, first_norm)

    def finish():
        wait_all(c_copies)
        loop(4, second_norm)
        start_all(final_copies)

    def attend_pull_all(b):
        attend_pull(b % count, b < count)

    def head_grad(i):
        weight_grad(x, joined((vl, k, q)[i]), slope, 2 - i)

    def vector_grads():
        head_sum(QUERY_BIAS, q)
        head_sum(VALUE_BIAS, vl)
        vectors_out()

    def input_pull_all(t):
        input_pull(t)
        if t == 1:
            start_all(grad_copies)

    steps |= {
        "spread": lambda _: spread(),
        "project": project_all,
        "attend": attend_all,
        "first_norm": lambda _: normalise(),
        "expand": expand,
        "contract": contract,
        "second_norm": lambda _: finish(),
        "down_grad": down_grad,
        "inner_grad": inner_grad,
        "up_grad": lambda j: weight_grad(low, lambda: take(slope, j), hidden, j),
        "up_pull": lambda _: up_pull(),
        "first_pull": lambda _: loop(4, first_pull),
        "out_grad": lambda _: weight_grad(mixed, lambda: delta[...], slope, 3),
        "mixed_pull": lambda _: mixed_pull(),
        "attend_pull": attend_pull_all,
        "head_grad": head_grad,
        "vectors": lambda _: vector_grads(),
        "input_pull": input_pull_all,
    }
    for entry in ORDER:
        name, at = entry.split(".")
        steps[name](int(at))
    sender.finish()
    wait_all(final_copies + grad_copies)
    for n in range(JOBS):
        steps["r5"](n)


def fused(lengths, rows, matrices, vectors):
    long_inputs, short_inputs = rows[:2]
    count = long_inputs.shape[0]
    tokens = count * (long_inputs.shape[1] + short_inputs.shape[1])
    n = JOBS
    anywhere = pl.BlockSpec(memory_space=pl.ANY)
    scalar = pl.BlockSpec(memory_space=pltpu.SMEM)
    spots = (4, 2, 2)
    scratch = [pltpu.VMEM((COUNT[kind], *spots, *UNIT[kind]), TYPE[kind]) for kind in "wdv"]
    for lead in (spots, (2, 4), (4,), (3,)):
        scratch += [pltpu.VMEM((COUNT[kind], *lead, *HALF[kind]), TYPE[kind]) for kind in "wdv"]
    scratch += [pltpu.VMEM((COUNT[kind], *HALF[kind]), f32) for kind in "wdv"]
    scratch += [pltpu.VMEM((3, 2, *spots, *HALF["d"]), bf16), pltpu.VMEM((2, *spots, *HALF["v"]), f32)]
    heads = pltpu.VMEM((PAIRS, tokens, 128), bf16)
    low = pltpu.VMEM((tokens, D), bf16)
    high = pltpu.VMEM((tokens, D), f32)
    wide = pltpu.VMEM((4, 2, *spots, *HALF["w"]), bf16)
    scratch += [low, low, heads, heads, heads, low, high, pltpu.VMEM((tokens, 1), f32), low, wide, wide, high, low]
    scratch += [pltpu.VMEM((16, D), f32), pltpu.VMEM((count + count // 2, 2 * HEADS, BLOCK), f32), pltpu.VMEM((4, D), f32), pltpu.VMEM((8, D), f32), pltpu.VMEM((4, D), f32)]
    scratch += [DMA((n,))] + [DMA((n, 3))] * 4 + [DMA((n, 4))] * 2
    scratch += [DMA((n,))] * 2 + [DMA((n, 3))] * 4 + [DMA((n,))] * 2 + [DMA((n,)), DMA((2, 2 * count)), DMA((2, 2 * count))]
    results = [jax.ShapeDtypeStruct(a.shape, bf16) for a in rows[:2]]
    results += [jax.ShapeDtypeStruct(a.shape, f32) for a in rows[:2]]
    results += [jax.ShapeDtypeStruct(a.shape, f32) for a in matrices]
    results += [jax.ShapeDtypeStruct((16, 128), f32)]
    return pl.pallas_call(
        fused_kernel,
        out_shape=results,
        in_specs=[scalar] * 2 + [anywhere] * 11,
        out_specs=[anywhere] * 11,
        scratch_shapes=scratch,
        compiler_params=pltpu.CompilerParams(
            collective_id=0, has_side_effects=True, vmem_limit_bytes=61 << 20
        ),
        name="layer",
    )(*lengths, *rows, *matrices, vectors)


def layer_by_kernel(long_inputs, short_inputs, long_lengths, short_lengths, long_cotangent, short_cotangent, *shards):
    small = jnp.pad(jnp.stack([shards[i] for i in SMALL]), ((0, 0), (0, 80)))
    tail = jnp.pad(shards[10], (0, 64)).reshape(2, 128)
    vectors = jnp.pad(jnp.concatenate([small, tail]), ((0, 6), (0, 0))).astype(f32)
    *results, wq, wk, wv, wo, up, down, v = fused(
        (long_lengths, short_lengths),
        (long_inputs, short_inputs, long_cotangent, short_cotangent),
        tuple(shards[i] for i in (0, 2, 3, 5, 9, 11)),
        vectors,
    )
    done = {0: wq, 2: wk, 3: wv, 5: wo, 9: up, 11: down}
    for at, i in enumerate(SMALL):
        done[i] = v[at, :48]
    done[10] = v[8:10].reshape(256)[:192]
    return (*results, *(done[i] for i in range(15)))


def gathered_by_collectives(shards):
    full = tuple(lax.all_gather(shard, "fsdp", axis=0, tiled=True) for shard in shards)
    return tuple(a.astype(f32) if a.ndim == 1 else a for a in full)


def reduced_by_collectives(totals):
    reduced = lax.psum_scatter(totals, "fsdp", scatter_dimension=0, tiled=True)
    low = jax.tree.map(lambda a: a.astype(bf16), reduced)
    return jax.tree.map(lambda a: a.astype(f32), lax.psum(low, "dp"))


def layer_by_collectives(
    long_inputs, short_inputs, long_lengths, short_lengths, long_cotangent, short_cotangent, *shards
):
    weights = gathered_by_collectives(shards)
    long_output, long_saved = layer_pass(weights, long_inputs, long_lengths)
    short_output, short_saved = layer_pass(weights, short_inputs, short_lengths)
    long_grad, long_terms = layer_back(weights, long_saved, long_cotangent)
    short_grad, short_terms = layer_back(weights, short_saved, short_cotangent)
    totals = tuple((first + second for first, second in zip(long_terms, short_terms)))
    reduced = reduced_by_collectives(totals)
    return (long_output.astype(bf16), short_output.astype(bf16), long_grad, short_grad, *reduced)


def solution(mesh):
    rows = P(("fsdp", "dp"), None, None)
    count = P(("fsdp", "dp"))
    matrix, vector = P("fsdp", None), P("fsdp")
    params = tuple(matrix if i in (0, 2, 3, 5, 9, 11) else vector for i in range(15))
    by_kernel = mesh.shape["fsdp"] == 16 and mesh.shape["dp"] == 2
    return jax.shard_map(
        layer_by_kernel if by_kernel else layer_by_collectives,
        mesh=mesh,
        in_specs=(rows, rows, count, count, rows, rows, *params),
        out_specs=(rows, rows, rows, rows, *params),
        check_vma=False,
    )
```

```python
import functools
import math

import jax
import jax.numpy as jnp
from jax import lax
from jax.experimental import pallas as pl
from jax.experimental.pallas import tpu as pltpu
from jax.sharding import PartitionSpec as P

HEADS = 12
HEAD_DIM = 64
MESH = pl.DeviceIdType.MESH
DMA = pltpu.SemaphoreType.DMA
f32 = jnp.float32
bf16 = jnp.bfloat16

epsilon = 1e-05
masked_score = -1000000000.0


def matmul(left, right):
    return jnp.dot(left, right, preferred_element_type=f32)


def transposed(left, right):
    return lax.dot_general(left, right, (((0,), (0,)), ((), ())), preferred_element_type=f32)


def against(left, right):
    return lax.dot_general(left, right, (((1,), (1,)), ((), ())), preferred_element_type=f32)


def norm_forward(tensor, scales, offsets):
    centre = jnp.mean(tensor, axis=-1, keepdims=True)
    centred = tensor - centre
    inverse = lax.rsqrt(jnp.mean(centred * centred, axis=-1, keepdims=True) + epsilon)
    scaled = centred * inverse
    return (scaled * scales + offsets, scaled, inverse)


def norm_backward(upstream, scaled, inverse, scales):
    delta_scaled = upstream * scales
    plain_mean = jnp.mean(delta_scaled, axis=-1, keepdims=True)
    cross_mean = jnp.mean(delta_scaled * scaled, axis=-1, keepdims=True)
    delta_input = inverse * (delta_scaled - plain_mean - scaled * cross_mean)
    return (delta_input, jnp.sum(upstream * scaled, axis=0), jnp.sum(upstream, axis=0))


def layer_pass(weights, inputs, lengths):
    (
        query_weight,
        query_bias,
        key_weight,
        value_weight,
        value_bias,
        out_weight,
        out_bias,
        first_gain,
        first_shift,
        up_weight,
        up_bias,
        down_weight,
        down_bias,
        second_gain,
        second_shift,
    ) = weights
    count, length, width = inputs.shape
    heads_shape = (count, length, HEADS, HEAD_DIM)
    rows = inputs.reshape(count * length, width)
    queries = (matmul(rows, query_weight) + query_bias).astype(bf16).reshape(heads_shape)
    key_rows = matmul(rows, key_weight).astype(bf16).reshape(heads_shape)
    value_rows = (matmul(rows, value_weight) + value_bias).astype(bf16).reshape(heads_shape)
    score_scale = HEAD_DIM ** (-0.5)
    scores = jnp.einsum("bqhd,bkhd->bhqk", queries, key_rows, preferred_element_type=f32) * score_scale
    live = lax.broadcasted_iota(jnp.int32, (count, length), 1) < lengths[:, None]
    scores = jnp.where(live[:, None, None, :], scores, masked_score)
    highest = jnp.max(scores, axis=-1, keepdims=True)
    raised = jnp.exp(scores - highest)
    attention = raised / jnp.sum(raised, axis=-1, keepdims=True)
    attention_low = attention.astype(bf16)
    mixed = jnp.einsum("bhqk,bkhd->bqhd", attention_low, value_rows, preferred_element_type=f32)
    mixed = mixed.reshape(count * length, width).astype(bf16)
    branch = matmul(mixed, out_weight) + out_bias
    normed, scaled_one, inverse_one = norm_forward(rows.astype(f32) + branch, first_gain, first_shift)
    normed_low = normed.astype(bf16)
    inner = matmul(normed_low, up_weight) + up_bias
    hidden = jax.nn.gelu(inner, approximate=False).astype(bf16)
    update = matmul(hidden, down_weight) + down_bias
    final, scaled_two, inverse_two = norm_forward(normed + update, second_gain, second_shift)
    saved = (
        rows,
        queries,
        key_rows,
        value_rows,
        attention,
        attention_low,
        mixed,
        scaled_one,
        inverse_one,
        normed_low,
        inner,
        hidden,
        scaled_two,
        inverse_two,
    )
    return (final.reshape(count, length, width), saved)


def layer_back(weights, saved, cotangent):
    (
        query_weight,
        query_bias,
        key_weight,
        value_weight,
        value_bias,
        out_weight,
        out_bias,
        first_gain,
        first_shift,
        up_weight,
        up_bias,
        down_weight,
        down_bias,
        second_gain,
        second_shift,
    ) = weights
    (
        rows,
        queries,
        key_rows,
        value_rows,
        attention,
        attention_low,
        mixed,
        scaled_one,
        inverse_one,
        normed_low,
        inner,
        hidden,
        scaled_two,
        inverse_two,
    ) = saved
    count, length, width = cotangent.shape
    heads_shape = (count, length, HEADS, HEAD_DIM)
    score_scale = HEAD_DIM ** (-0.5)
    upstream = cotangent.reshape(count * length, width).astype(f32)
    grad_two, second_gain_term, second_shift_term = norm_backward(upstream, scaled_two, inverse_two, second_gain)
    delta_update = grad_two.astype(bf16)
    down_weight_term = transposed(hidden, delta_update)
    down_bias_term = jnp.sum(delta_update.astype(f32), axis=0)
    _, gelu_pull = jax.vjp(functools.partial(jax.nn.gelu, approximate=False), inner)
    delta_inner = gelu_pull(against(delta_update, down_weight))[0].astype(bf16)
    up_weight_term = transposed(normed_low, delta_inner)
    up_bias_term = jnp.sum(delta_inner.astype(f32), axis=0)
    grad_normed = against(delta_inner, up_weight) + grad_two
    grad_one, first_gain_term, first_shift_term = norm_backward(grad_normed, scaled_one, inverse_one, first_gain)
    delta_branch = grad_one.astype(bf16)
    out_weight_term = transposed(mixed, delta_branch)
    out_bias_term = jnp.sum(delta_branch.astype(f32), axis=0)
    delta_mixed = against(delta_branch, out_weight).astype(bf16).reshape(heads_shape)
    delta_values = jnp.einsum("bhqk,bqhd->bkhd", attention_low, delta_mixed, preferred_element_type=f32)
    delta_values = delta_values.astype(bf16).reshape(count * length, width)
    grad_attention = jnp.einsum("bqhd,bkhd->bhqk", delta_mixed, value_rows, preferred_element_type=f32)
    row_total = jnp.sum(attention * grad_attention, axis=-1, keepdims=True)
    delta_scores = (attention * (grad_attention - row_total)).astype(bf16)
    delta_queries = jnp.einsum("bhqk,bkhd->bqhd", delta_scores, key_rows, preferred_element_type=f32) * score_scale
    delta_queries = delta_queries.astype(bf16).reshape(count * length, width)
    delta_keys = jnp.einsum("bhqk,bqhd->bkhd", delta_scores, queries, preferred_element_type=f32) * score_scale
    delta_keys = delta_keys.astype(bf16).reshape(count * length, width)
    query_weight_term = transposed(rows, delta_queries)
    query_bias_term = jnp.sum(delta_queries.astype(f32), axis=0)
    key_weight_term = transposed(rows, delta_keys)
    value_weight_term = transposed(rows, delta_values)
    value_bias_term = jnp.sum(delta_values.astype(f32), axis=0)
    input_grad = (
        grad_one
        + against(delta_queries, query_weight)
        + against(delta_keys, key_weight)
        + against(delta_values, value_weight)
    )
    terms = (
        query_weight_term,
        query_bias_term,
        key_weight_term,
        value_weight_term,
        value_bias_term,
        out_weight_term,
        out_bias_term,
        first_gain_term,
        first_shift_term,
        up_weight_term,
        up_bias_term,
        down_weight_term,
        down_bias_term,
        second_gain_term,
        second_shift_term,
    )
    return (input_grad.reshape(count, length, width), terms)


class Place:
    def __init__(self):
        chip = lax.axis_index("fsdp")
        core = lax.axis_index("dp")
        z, y, x = chip // 4, (chip // 2) % 2, chip % 2
        self.z, self.y, self.x, self.core = z, y, x, core
        first = 1 - core
        self.own = (y, x)
        self.near = (jnp.where(core == 0, y, 1 - y), jnp.where(core == 0, 1 - x, x))
        self.far = (jnp.where(core == 0, 1 - y, y), jnp.where(core == 0, x, 1 - x))
        self.across = (1 - y, 1 - x)
        self.up = [(z + d) % 4 for d in (1, 2, 3)]
        self.down = [(z + 4 - d) % 4 for d in (1, 2, 3)]
        self.column = [self.device(q, y, x, core) for q in self.up]
        self.near_device = self.device(z, *self.near, core)
        self.far_device = self.device(z, *self.far, core)
        self.partner = self.device(z, y, x, 1 - core)

    def device(self, z, y, x, core):
        return (z * 4 + y * 2 + x, core)

    def greet(self):
        barrier = pltpu.get_barrier_semaphore()
        for peer in self.column + [self.near_device, self.far_device, self.partner]:
            pl.semaphore_signal(barrier, 1, device_id=peer, device_id_type=MESH)
        return barrier


def half(kind, core):
    if kind == "w":
        return (slice(None), pl.ds(pl.multiple_of(core * 384, 128), 384))
    if kind == "d":
        return (slice(None), pl.ds(pl.multiple_of(core * 128, 128), 128))
    return (pl.ds(pl.multiple_of(core * 8, 8), 8), slice(None))


UNIT = {"w": (48, 768), "d": (192, 256), "v": (16, 128)}
HALF = {"w": (48, 384), "d": (192, 128), "v": (8, 128)}
TYPE = {"w": bf16, "d": bf16, "v": f32}
COUNT = {"w": 8, "d": 3, "v": 1}
GATHER = [("v", 0)] + [("w", i) for i in range(8)] + [("d", i) for i in range(3)]
REDUCE = [("d", i) for i in range(3)] + [("w", i) for i in (4, 5, 6, 7, 3, 2, 1, 0)] + [("v", 0)]
JOBS = len(GATHER)
SMALL = (1, 4, 6, 7, 8, 12, 13, 14)
QUERY_BIAS, VALUE_BIAS, OUT_BIAS, FIRST_GAIN, FIRST_SHIFT, DOWN_BIAS, SECOND_GAIN, SECOND_SHIFT = range(8)
ORDER = (
    "g1.0", "g1.1", "g2.0", "g1.2", "g2.1", "g1.3", "g2.2", "g3.0", "g4.0", "g1.4",
    "g2.3", "g3.1", "g4.1", "g1.5", "g2.4", "g3.2", "g4.2", "g5.0", "g1.6", "g2.5",
    "g3.3", "g4.3", "g5.1", "g6.0", "spread.0", "g1.7", "g2.6", "g3.4", "g4.4", "g5.2",
    "g6.1", "project.0", "g1.8", "g2.7", "g3.5", "g4.5", "g5.3", "g6.2", "project.1", "g1.9",
    "g2.8", "g3.6", "g4.6", "g5.4", "g6.3", "project.2", "attend.0", "g1.10", "g2.9", "g3.7",
    "g4.7", "attend.1", "g5.5", "g6.4", "g1.11", "g2.10", "attend.2", "g3.8", "g4.8", "g5.6",
    "g6.5", "first_norm.0", "expand.0", "g2.11", "g3.9", "g4.9", "g5.7", "g6.6", "expand.1", "g3.10",
    "g4.10", "g5.8", "g6.7", "expand.2", "g3.11", "g4.11", "g5.9", "g6.8", "expand.3", "g5.10",
    "g6.9", "contract.0", "g5.11", "g6.10", "contract.1", "g6.11", "contract.2", "second_norm.0", "down_grad.0", "r0.0",
    "down_grad.1", "r0.1", "down_grad.2", "r0.2", "inner_grad.0", "up_grad.0", "r1.0", "r0.3", "inner_grad.1", "up_grad.1",
    "r1.1", "r0.4", "inner_grad.2", "up_grad.2", "r1.2", "r2.0", "r0.5", "inner_grad.3", "up_grad.3", "r1.3",
    "r2.1", "r0.6", "up_pull.0", "r1.4", "r2.2", "r3.0", "first_pull.0", "out_grad.0", "r0.7", "mixed_pull.0",
    "attend_pull.0", "r1.5", "r2.3", "r3.1", "r4.0", "attend_pull.1", "attend_pull.2", "attend_pull.3", "attend_pull.4", "attend_pull.5",
    "head_grad.0", "r0.8", "head_grad.1", "r1.6", "r2.4", "r3.2", "r4.1", "r0.9", "head_grad.2", "r1.7",
    "r2.5", "r3.3", "r4.2", "r0.10", "vectors.0", "r1.8", "r2.6", "r3.4", "r4.3", "r0.11",
    "input_pull.0", "r1.9", "r2.7", "r3.5", "r4.4", "input_pull.1", "r1.10", "r2.8", "r3.6", "r4.5",
    "r1.11", "r2.9", "r3.7", "r4.6", "r2.10", "r3.8", "r4.7", "r2.11", "r3.9", "r4.8",
    "r3.10", "r4.9", "r3.11", "r4.10", "r4.11",
)
D = 768
TILE = 192
PAIRS = HEADS // 2
BLOCK = 128


class Sender:
    def __init__(self, place):
        self.place = place
        self.started = []

    def copy(self, source, target, send, receive, device):
        return pltpu.make_async_remote_copy(
            source, target, send, receive, device_id=device, device_id_type=MESH
        )

    def send(self, source, target, send, receive, device):
        copy = self.copy(source, target, send, receive, device)
        copy.start()
        self.started.append(copy)

    def arrived(self, target, send, receive):
        self.copy(target, target, send, receive, self.place.partner).wait_recv()

    def finish(self):
        for copy in self.started:
            copy.wait_send()


def gather_steps(place, sender, given, whole, own_s, z_s, z_r, h_s, h_r, p_s, p_r):
    z, core = place.z, place.core
    local = [
        pltpu.make_async_copy(
            given(kind, i, half(kind, core)),
            whole[kind].at[(i, z, *place.own, *half(kind, core))],
            own_s.at[n],
        )
        for n, (kind, i) in enumerate(GATHER)
    ]
    for copy in local:
        copy.start()

    def unit(n, q):
        kind, i = GATHER[n]
        return whole[kind].at[(i, q, *place.own, *half(kind, core))]

    def column(n, spot, core=core):
        kind, i = GATHER[n]
        return whole[kind].at[(i, slice(None), *spot, *half(kind, core))]

    def pass_on(n, spot, j, to):
        part = column(n, spot)
        sender.send(part, part, h_s.at[n, j], h_r.at[n, j], to)

    def share(n, spot, j):
        part = column(n, spot)
        sender.send(part, part, p_s.at[n, j], p_r.at[n, j], place.partner)

    def first(n):
        local[n].wait()
        for j in range(3):
            sender.send(unit(n, z), unit(n, z), z_s.at[n, j], z_r.at[n, j], place.column[j])

    def second(n):
        for j in range(3):
            sender.arrived(unit(n, place.down[j]), z_s.at[n, j], z_r.at[n, j])
        pass_on(n, place.own, 0, place.near_device)
        pass_on(n, place.own, 1, place.far_device)
        share(n, place.own, 0)

    def third(n):
        sender.arrived(column(n, place.near), h_s.at[n, 0], h_r.at[n, 0])
        pass_on(n, place.near, 2, place.far_device)
        share(n, place.near, 1)

    def fourth(n):
        sender.arrived(column(n, place.far), h_s.at[n, 1], h_r.at[n, 1])
        share(n, place.far, 2)

    def fifth(n):
        sender.arrived(column(n, place.across), h_s.at[n, 2], h_r.at[n, 2])
        share(n, place.across, 3)

    def complete(n):
        for j, spot in enumerate((place.own, place.far, place.near, place.across)):
            sender.arrived(column(n, spot, 1 - core), p_s.at[n, j], p_r.at[n, j])

    return {"g1": first, "g2": second, "g3": third, "g4": fourth, "g5": fifth, "g6": complete}


def reduce_steps(place, sender, total, shared, far, near, high, final, out, p_s, p_r, h_s, h_r, z_s, z_r, f_s, f_r, o_s):
    z, core = place.z, place.core

    def add(n, spot, more):
        kind, i = REDUCE[n]
        ref = total(kind, i)

        def one(q, _):
            at = (core, q, *spot)
            ref[at] = (ref[at].astype(f32) + more[q].astype(f32)).astype(TYPE[kind])
            return 0

        lax.fori_loop(0, 4, one, 0)

    def column(n, spot):
        return total(*REDUCE[n]).at[(core, slice(None), *spot)]

    def give(n):
        kind, i = REDUCE[n]
        sender.send(total(kind, i).at[1 - core], shared[kind].at[i], p_s.at[n], p_r.at[n], place.partner)

    def first(n):
        kind, i = REDUCE[n]
        sender.arrived(shared[kind].at[i], p_s.at[n], p_r.at[n])
        for j, spot in enumerate((place.across, place.far)):
            add(n, spot, shared[kind].at[(i, slice(None), *spot)])
            sender.send(column(n, spot), far[kind].at[i, j], h_s.at[n, j], h_r.at[n, j], place.far_device)
        for spot in (place.near, place.own):
            add(n, spot, shared[kind].at[(i, slice(None), *spot)])

    def second(n):
        kind, i = REDUCE[n]
        sender.arrived(far[kind].at[i, 0], h_s.at[n, 0], h_r.at[n, 0])
        add(n, place.near, far[kind].at[i, 0])
        sender.send(column(n, place.near), near[kind].at[i], h_s.at[n, 2], h_r.at[n, 2], place.near_device)

    def third(n):
        kind, i = REDUCE[n]
        sender.arrived(far[kind].at[i, 1], h_s.at[n, 1], h_r.at[n, 1])
        add(n, place.own, far[kind].at[i, 1])
        sender.arrived(near[kind].at[i], h_s.at[n, 2], h_r.at[n, 2])
        add(n, place.own, near[kind].at[i])
        for j in range(3):
            part = total(kind, i).at[(core, place.up[j], *place.own)]
            sender.send(part, high[kind].at[i, j], z_s.at[n, j], z_r.at[n, j], place.column[j])

    def fourth(n):
        kind, i = REDUCE[n]
        mine = total(kind, i)[(core, z, *place.own)].astype(f32)
        for j in range(3):
            sender.arrived(high[kind].at[i, j], z_s.at[n, j], z_r.at[n, j])
            mine = mine + high[kind][i, j].astype(f32)
        final[kind][i] = mine
        mine_out = out(kind, i, core)
        sender.send(final[kind].at[i], mine_out, f_s.at[n], f_r.at[n], place.partner)
        pltpu.make_async_copy(final[kind].at[i], mine_out, o_s.at[n]).start()

    def stored(n):
        kind, i = REDUCE[n]
        pltpu.make_async_copy(final[kind].at[i], out(kind, i, core), o_s.at[n]).wait()
        sender.arrived(out(kind, i, 1 - core), f_s.at[n], f_r.at[n])

    return {"r0": give, "r1": first, "r2": second, "r3": third, "r4": fourth, "r5": stored}


def iota(shape, axis):
    return lax.broadcasted_iota(jnp.int32, shape, axis)


def loop(count, body):
    def step(i, _):
        body(i)
        return 0

    lax.fori_loop(0, count, step, 0)


def tile_rows(i):
    return pl.ds(pl.multiple_of(i * TILE, TILE), TILE)


def flat(value):
    return value.reshape(math.prod(value.shape[:-1]), value.shape[-1])


def spread_table():
    return jnp.where(iota((128, D), 1) % 48 == iota((128, D), 0), 1.0, 0.0)


def spread_tables_wide():
    l = iota((128, D), 1) % 192
    j = iota((128, D), 0)
    return jnp.where(l == j, 1.0, 0.0), jnp.where(l == j + 128, 1.0, 0.0)


def wide_rows():
    row = iota((64, D), 0)
    mine = iota((64, D), 1) // 192 == row // 16
    return mine & (row % 16 == 8), mine & (row % 16 == 9)


def total_over(mask, value):
    return jnp.sum(jnp.where(mask, value, 0.0), axis=0, keepdims=True)


def fused_kernel(
    long_lengths,
    short_lengths,
    long_inputs,
    short_inputs,
    long_cotangent,
    short_cotangent,
    wq_in,
    wk_in,
    wv_in,
    wo_in,
    up_in,
    down_in,
    v_in,
    long_output,
    short_output,
    long_grad,
    short_grad,
    wq_out,
    wk_out,
    wv_out,
    wo_out,
    up_out,
    down_out,
    v_out,
    w,
    d,
    v,
    shared_w,
    shared_d,
    shared_v,
    far_w,
    far_d,
    far_v,
    near_w,
    near_d,
    near_v,
    high_w,
    high_d,
    high_v,
    final_w,
    final_d,
    final_v,
    total_d,
    total_v,
    x,
    c,
    q,
    k,
    vl,
    mixed,
    xhat,
    inverse,
    low,
    hidden,
    slope,
    acc,
    delta,
    vec,
    stats,
    up_bias,
    small,
    up_bias_sum,
    own_s,
    gz_s,
    gz_r,
    gh_s,
    gh_r,
    gp_s,
    gp_r,
    p_s,
    p_r,
    h_s,
    h_r,
    z_s,
    z_r,
    f_s,
    f_r,
    o_s,
    in_s,
    out_s,
):
    place = Place()
    barrier = place.greet()
    sender = Sender(place)
    matrices_in = (wq_in, wk_in, wv_in, wo_in)
    matrices_out = (wq_out, wk_out, wv_out, wo_out)

    def given(kind, i, at):
        rows, cols = at
        if kind == "v":
            return v_in.at[rows, cols]
        core = place.core
        if kind == "d":
            return down_in.at[:, pl.ds(pl.multiple_of(256 * i + core * 128, 128), 128)]
        if i < 4:
            return matrices_in[i].at[rows, cols]
        return up_in.at[:, pl.ds(pl.multiple_of(D * (i - 4) + core * 384, 128), 384)]

    def out(kind, i, core):
        rows, cols = half(kind, core)
        if kind == "v":
            return v_out.at[rows, cols]
        if kind == "d":
            return down_out.at[:, pl.ds(pl.multiple_of(256 * i + core * 128, 128), 128)]
        if i < 4:
            return matrices_out[i].at[rows, cols]
        return up_out.at[:, pl.ds(pl.multiple_of(D * (i - 4) + core * 384, 128), 384)]

    def total(kind, i):
        if kind == "d":
            return total_d.at[i]
        if kind == "v":
            return total_v
        return hidden.at[i - 4] if i >= 4 else slope.at[i]

    steps = gather_steps(
        place, sender, given, {"w": w, "d": d, "v": v}, own_s, gz_s, gz_r, gh_s, gh_r, gp_s, gp_r
    )
    steps |= reduce_steps(
        place,
        sender,
        total,
        {"w": shared_w, "d": shared_d, "v": shared_v},
        {"w": far_w, "d": far_d, "v": far_v},
        {"w": near_w, "d": near_d, "v": near_v},
        {"w": high_w, "d": high_d, "v": high_v},
        {"w": final_w, "d": final_d, "v": final_v},
        out,
        p_s,
        p_r,
        h_s,
        h_r,
        z_s,
        z_r,
        f_s,
        f_r,
        o_s,
    )

    count, length, _ = long_inputs.shape
    short = short_inputs.shape[1]

    def groups(buffer, long_ref, short_ref, outward, s):
        copies = []
        for i in range(count):
            copies.append((buffer.at[i * length : (i + 1) * length], long_ref.at[i]))
        for i in range(count):
            start = count * length + i * short
            copies.append((buffer.at[start : start + short], short_ref.at[i]))
        return [
            pltpu.make_async_copy(*((a, b) if outward else (b, a)), s.at[i]) for i, (a, b) in enumerate(copies)
        ]

    x_copies = groups(x, long_inputs, short_inputs, False, in_s.at[0])
    c_copies = groups(c, long_cotangent, short_cotangent, False, in_s.at[1])
    for copy in x_copies + c_copies:
        copy.start()
    small[...] = jnp.zeros_like(small)
    up_bias_sum[...] = jnp.zeros_like(up_bias_sum)
    total_v[...] = jnp.zeros_like(total_v)
    pl.semaphore_wait(barrier, 6)

    def weight(i):
        return flat(w[i])

    def row(at):
        return vec[at : at + 1, :]


    def spread():
        wide = matmul(flat(v[0]).astype(bf16), spread_table().astype(bf16))
        mine = iota((256, D), 1) // 48 == iota((256, D), 0) // 16
        vec[...] = jnp.sum(jnp.where(mine, wide, 0.0).reshape(16, 16, D), axis=0)
        table_a, table_b = spread_tables_wide()
        mask_a, mask_b = wide_rows()
        for j in range(4):
            unit = flat(v[0, j]).astype(bf16)
            up_bias[j : j + 1, :] = total_over(mask_a, matmul(unit, table_a.astype(bf16))) + total_over(
                mask_b, matmul(unit, table_b.astype(bf16))
            )

    def project(i, target, bias, scale=1.0):
        result = matmul(x[...], weight(i))
        if bias is not None:
            result = result + row(bias)
        result = (result.astype(bf16) * scale).astype(bf16)
        for p in range(PAIRS):
            target[p] = result[:, 128 * p : 128 * p + 128]

    left_lanes = iota((BLOCK, BLOCK), 1) < HEAD_DIM

    def stacked(value):
        none = jnp.zeros_like(value)
        return jnp.concatenate([jnp.where(left_lanes, value, none), jnp.where(left_lanes, none, value)], axis=0)

    def picked(value):
        return jnp.where(left_lanes, value[:BLOCK], value[BLOCK:])

    def live_keys(b, is_long):
        key = iota((BLOCK, BLOCK), 0)
        if is_long:
            return key < long_lengths[b]
        left = key < short
        limit = jnp.where(left, short_lengths[2 * b], short + short_lengths[2 * b + 1])
        return (key < limit) & (left == (iota((BLOCK, BLOCK), 1) < short))

    def block_rows(b, is_long):
        start = b * BLOCK if is_long else count * length + b * BLOCK
        return pl.ds(pl.multiple_of(start, BLOCK), BLOCK)

    def block_scores(p, rows, live):
        scores = against(stacked(k[p, rows, :]), q[p, rows, :])
        return [jnp.where(live, scores[BLOCK * head : BLOCK * head + BLOCK], masked_score) for head in range(2)]

    def attend(b, is_long):
        rows = block_rows(b, is_long)
        live = live_keys(b, is_long)
        at = b if is_long else b + count
        results = []
        for p in range(PAIRS):
            parts = []
            for head, part in enumerate(block_scores(p, rows, live)):
                highest = jnp.max(part, axis=0, keepdims=True)
                raised = jnp.exp(part - highest)
                scale = 1.0 / jnp.sum(raised, axis=0, keepdims=True)
                stats[at, 2 * p + head : 2 * p + head + 1, :] = highest
                stats[at, HEADS + 2 * p + head : HEADS + 2 * p + head + 1, :] = scale
                parts.append((raised * scale).astype(bf16))
            both = jnp.concatenate(parts, axis=0)
            results.append(transposed(both, stacked(vl[p, rows, :])).astype(bf16))
        mixed[rows, :] = jnp.concatenate(results, axis=1)

    def branch():
        acc[...] = matmul(mixed[...], weight(3)) + row(OUT_BIAS)

    def first_norm(t):
        rows = tile_rows(t)
        normed, scaled, inv = norm_forward(x[rows, :].astype(f32) + acc[rows, :], row(FIRST_GAIN), row(FIRST_SHIFT))
        xhat[rows, :] = scaled
        inverse[rows, :] = inv
        low[rows, :] = normed.astype(bf16)

    def put(buffer, j, value):
        for side in range(2):
            buffer[j, side] = value[:, 384 * side : 384 * side + 384].reshape(4, 2, 2, 48, 384)

    def take(buffer, j):
        return jnp.concatenate([flat(buffer[j, side]) for side in range(2)], axis=1)

    def expand(j):
        inner = matmul(low[...], weight(4 + j)) + up_bias[j : j + 1, :]
        phi = 0.5 + 0.5 * lax.erf(inner * 0.5**0.5)
        put(hidden, j, (inner * phi).astype(bf16))
        density = jnp.exp(-0.5 * inner * inner) * (2 * math.pi) ** -0.5
        put(slope, j, (phi + inner * density).astype(bf16))

    def contract(n):
        update = row(DOWN_BIAS)[:, 256 * n : 256 * n + 256]
        for j in range(4):
            update = update + matmul(take(hidden, j), flat(d[n, j]))
        acc[:, 256 * n : 256 * n + 256] = update

    def tally(at, value):
        small[at : at + 1, :] += jnp.sum(value, axis=0, keepdims=True)

    def norm_pull(upstream, scaled, inv, gain):
        g = upstream * gain
        plain = jnp.mean(g, axis=-1, keepdims=True)
        cross = jnp.mean(g * scaled, axis=-1, keepdims=True)
        return inv * (g - plain - scaled * cross)

    def second_norm(t):
        rows = tile_rows(t)
        normed = xhat[rows, :] * row(FIRST_GAIN) + row(FIRST_SHIFT)
        final, scaled, inv = norm_forward(normed + acc[rows, :], row(SECOND_GAIN), row(SECOND_SHIFT))
        upstream = c[rows, :].astype(f32)
        c[rows, :] = final.astype(bf16)
        tally(SECOND_GAIN, upstream * scaled)
        tally(SECOND_SHIFT, upstream)
        grad = norm_pull(upstream, scaled, inv, row(SECOND_GAIN))
        acc[rows, :] = grad
        lowered = grad.astype(bf16)
        delta[rows, :] = lowered
        tally(DOWN_BIAS, lowered.astype(f32))


    def down_grad(n):
        for j in range(4):
            grad = transposed(take(hidden, j), delta[:, 256 * n : 256 * n + 256]).astype(bf16)
            for side in range(2):
                total_d[n, side, j] = grad[:, 128 * side : 128 * side + 128].reshape(2, 2, 192, 128)

    def inner_grad(j):
        pulled = against(delta[...], jnp.concatenate([flat(d[n, j]) for n in range(3)], axis=1))
        inner = (pulled * take(slope, j).astype(f32)).astype(bf16)
        put(slope, j, inner)
        up_bias_sum[j : j + 1, :] = jnp.sum(inner.astype(f32), axis=0, keepdims=True)

    def weight_grad(left, right, buffer, slot):
        put(buffer, slot, transposed(left[...], right()).astype(bf16))

    def up_pull():
        grad = acc[...]
        for j in range(4):
            grad = grad + against(take(slope, j), weight(4 + j))
        acc[...] = grad

    def first_pull(t):
        rows = tile_rows(t)
        upstream = acc[rows, :]
        scaled = xhat[rows, :]
        tally(FIRST_GAIN, upstream * scaled)
        tally(FIRST_SHIFT, upstream)
        grad = norm_pull(upstream, scaled, inverse[rows, :], row(FIRST_GAIN))
        acc[rows, :] = grad
        lowered = grad.astype(bf16)
        delta[rows, :] = lowered
        tally(OUT_BIAS, lowered.astype(f32))

    def mixed_pull():
        mixed[...] = against(delta[...], weight(3)).astype(bf16)

    def attend_pull(b, is_long):
        rows = block_rows(b, is_long)
        live = live_keys(b, is_long)
        at = b if is_long else b + count
        results = []
        for p in range(PAIRS):
            down = mixed[rows, 128 * p : 128 * p + 128]
            probs = []
            for head, part in enumerate(block_scores(p, rows, live)):
                highest = stats[at, 2 * p + head : 2 * p + head + 1, :]
                scale = stats[at, HEADS + 2 * p + head : HEADS + 2 * p + head + 1, :]
                probs.append(jnp.exp(part - highest) * scale)
            both = jnp.concatenate(probs, axis=0).astype(bf16)
            grad_values = picked(matmul(both, down))
            grad_probs = against(stacked(vl[p, rows, :]), down)
            parts = []
            for head in range(2):
                part = grad_probs[BLOCK * head : BLOCK * head + BLOCK]
                mean = jnp.sum(probs[head] * part, axis=0, keepdims=True)
                parts.append((probs[head] * (part - mean)).astype(bf16))
            grad_scores = jnp.concatenate(parts, axis=0)
            grad_queries = transposed(grad_scores, stacked(k[p, rows, :])) * HEAD_DIM**-0.5
            grad_keys = picked(matmul(grad_scores, q[p, rows, :]))
            results.append((grad_queries.astype(bf16), grad_keys.astype(bf16), grad_values.astype(bf16)))
        for p, (grad_queries, grad_keys, grad_values) in enumerate(results):
            q[p, rows, :] = grad_queries
            k[p, rows, :] = grad_keys
            vl[p, rows, :] = grad_values

    def joined(heads):
        return lambda: jnp.concatenate([heads[p] for p in range(PAIRS)], axis=1)

    def head_sum(at, heads):
        for p in range(PAIRS):
            small[at : at + 1, 128 * p : 128 * p + 128] = jnp.sum(heads[p].astype(f32), axis=0, keepdims=True)

    def input_pull(t):
        rows = slice(384 * t, 384 * t + 384)
        grad = acc[rows, :]
        for i, heads in enumerate((q, k, vl)):
            grad = grad + against(jnp.concatenate([heads[p, rows, :] for p in range(PAIRS)], axis=1), weight(i))
        acc[rows, :] = grad

    def exact(left, right):
        return lax.dot_general(
            left, right, (((1,), (1,)), ((), ())), precision=lax.Precision.HIGHEST, preferred_element_type=f32
        )

    def vectors_out():
        mine = iota((16, 8, D), 2) // 48 == iota((16, 8, D), 0)
        pieces = jnp.where(mine, jnp.broadcast_to(small[...][None], (16, 8, D)), 0.0).reshape(128, D)
        total_v[0] = exact(pieces, spread_table()).reshape(4, 2, 2, 8, 128)
        table_a, table_b = spread_tables_wide()
        mask_a, mask_b = wide_rows()
        for j in range(4):
            sums = jnp.broadcast_to(up_bias_sum[j : j + 1, :], (64, D))
            wide = exact(jnp.where(mask_a, sums, 0.0), table_a) + exact(jnp.where(mask_b, sums, 0.0), table_b)
            total_v[1, j] = wide.reshape(2, 2, 16, 128)[:, :, 8:, :]


    def wait_all(copies):
        for copy in copies:
            copy.wait()

    def start_all(copies):
        for copy in copies:
            copy.start()

    final_copies = groups(c, long_output, short_output, True, out_s.at[0])
    grad_copies = groups(acc, long_grad, short_grad, True, out_s.at[1])

    def project_all(i):
        if i == 0:
            wait_all(x_copies)
        project(i, (q, k, vl)[i], (QUERY_BIAS, None, VALUE_BIAS)[i], HEAD_DIM**-0.5 if i == 0 else 1.0)

    def attend_all(i):
        if 2 * i < count:
            loop(2, lambda b: attend(2 * i + b, True))
        else:
            loop(count // 2, lambda b: attend(b, False))

    def normalise():
        branch()
        loop(4, first_norm)

    def finish():
        wait_all(c_copies)
        loop(4, second_norm)
        start_all(final_copies)

    def attend_pull_all(b):
        attend_pull(b % count, b < count)

    def head_grad(i):
        weight_grad(x, joined((vl, k, q)[i]), slope, 2 - i)

    def vector_grads():
        head_sum(QUERY_BIAS, q)
        head_sum(VALUE_BIAS, vl)
        vectors_out()

    def input_pull_all(t):
        input_pull(t)
        if t == 1:
            start_all(grad_copies)

    steps |= {
        "spread": lambda _: spread(),
        "project": project_all,
        "attend": attend_all,
        "first_norm": lambda _: normalise(),
        "expand": expand,
        "contract": contract,
        "second_norm": lambda _: finish(),
        "down_grad": down_grad,
        "inner_grad": inner_grad,
        "up_grad": lambda j: weight_grad(low, lambda: take(slope, j), hidden, j),
        "up_pull": lambda _: up_pull(),
        "first_pull": lambda _: loop(4, first_pull),
        "out_grad": lambda _: weight_grad(mixed, lambda: delta[...], slope, 3),
        "mixed_pull": lambda _: mixed_pull(),
        "attend_pull": attend_pull_all,
        "head_grad": head_grad,
        "vectors": lambda _: vector_grads(),
        "input_pull": input_pull_all,
    }
    for entry in ORDER:
        name, at = entry.split(".")
        steps[name](int(at))
    sender.finish()
    wait_all(final_copies + grad_copies)
    for n in range(JOBS):
        steps["r5"](n)


def fused(lengths, rows, matrices, vectors):
    long_inputs, short_inputs = rows[:2]
    count = long_inputs.shape[0]
    tokens = count * (long_inputs.shape[1] + short_inputs.shape[1])
    n = JOBS
    anywhere = pl.BlockSpec(memory_space=pl.ANY)
    scalar = pl.BlockSpec(memory_space=pltpu.SMEM)
    spots = (4, 2, 2)
    scratch = [pltpu.VMEM((COUNT[kind], *spots, *UNIT[kind]), TYPE[kind]) for kind in "wdv"]
    for lead in (spots, (2, 4), (4,), (3,)):
        scratch += [pltpu.VMEM((COUNT[kind], *lead, *HALF[kind]), TYPE[kind]) for kind in "wdv"]
    scratch += [pltpu.VMEM((COUNT[kind], *HALF[kind]), f32) for kind in "wdv"]
    scratch += [pltpu.VMEM((3, 2, *spots, *HALF["d"]), bf16), pltpu.VMEM((2, *spots, *HALF["v"]), f32)]
    heads = pltpu.VMEM((PAIRS, tokens, 128), bf16)
    low = pltpu.VMEM((tokens, D), bf16)
    high = pltpu.VMEM((tokens, D), f32)
    wide = pltpu.VMEM((4, 2, *spots, *HALF["w"]), bf16)
    scratch += [low, low, heads, heads, heads, low, high, pltpu.VMEM((tokens, 1), f32), low, wide, wide, high, low]
    scratch += [pltpu.VMEM((16, D), f32), pltpu.VMEM((count + count // 2, 2 * HEADS, BLOCK), f32), pltpu.VMEM((4, D), f32), pltpu.VMEM((8, D), f32), pltpu.VMEM((4, D), f32)]
    scratch += [DMA((n,))] + [DMA((n, 3))] * 4 + [DMA((n, 4))] * 2
    scratch += [DMA((n,))] * 2 + [DMA((n, 3))] * 4 + [DMA((n,))] * 2 + [DMA((n,)), DMA((2, 2 * count)), DMA((2, 2 * count))]
    results = [jax.ShapeDtypeStruct(a.shape, bf16) for a in rows[:2]]
    results += [jax.ShapeDtypeStruct(a.shape, f32) for a in rows[:2]]
    results += [jax.ShapeDtypeStruct(a.shape, f32) for a in matrices]
    results += [jax.ShapeDtypeStruct((16, 128), f32)]
    return pl.pallas_call(
        fused_kernel,
        out_shape=results,
        in_specs=[scalar] * 2 + [anywhere] * 11,
        out_specs=[anywhere] * 11,
        scratch_shapes=scratch,
        compiler_params=pltpu.CompilerParams(
            collective_id=0, has_side_effects=True, vmem_limit_bytes=61 << 20
        ),
        name="layer",
    )(*lengths, *rows, *matrices, vectors)


def deliver_kernel(*refs):
    v, v_s, s = refs[-3:]
    sources, targets = refs[:11], refs[11:-3]
    copies = [
        pltpu.make_async_copy(source, target, s.at[at])
        for at, (source, target) in enumerate(zip(sources[:10], targets[:10]))
    ]
    for copy in copies:
        copy.start()
    load = pltpu.make_async_copy(sources[10], v, v_s)
    load.start()
    load.wait()
    for at in range(8):
        targets[10 + at][...] = v[at, :48]
    targets[18][0:128] = v[8]
    targets[18][128:192] = v[9, :64]
    for copy in copies:
        copy.wait()


def deliver(results):
    anywhere = pl.BlockSpec(memory_space=pl.ANY)
    vmem = pl.BlockSpec(memory_space=pltpu.VMEM)
    vectors = [jax.ShapeDtypeStruct((48,), f32)] * 8 + [jax.ShapeDtypeStruct((192,), f32)]
    return pl.pallas_call(
        deliver_kernel,
        out_shape=[jax.ShapeDtypeStruct(a.shape, a.dtype) for a in results[:10]] + vectors,
        in_specs=[anywhere] * 11,
        out_specs=[anywhere] * 10 + [vmem] * 9,
        scratch_shapes=[pltpu.VMEM((16, 128), f32), DMA, DMA((10,))],
        compiler_params=pltpu.CompilerParams(vmem_limit_bytes=60 << 20),
        name="deliver",
    )(*results)


def layer_by_kernel(long_inputs, short_inputs, long_lengths, short_lengths, long_cotangent, short_cotangent, *shards):
    small = jnp.pad(jnp.stack([shards[i] for i in SMALL]), ((0, 0), (0, 80)))
    tail = jnp.pad(shards[10], (0, 64)).reshape(2, 128)
    vectors = jnp.pad(jnp.concatenate([small, tail]), ((0, 6), (0, 0))).astype(f32)
    results = fused(
        (long_lengths, short_lengths),
        (long_inputs, short_inputs, long_cotangent, short_cotangent),
        tuple(shards[i] for i in (0, 2, 3, 5, 9, 11)),
        vectors,
    )
    results = deliver(results)
    *rows, wq, wk, wv, wo, up, down = results[:10]
    *small, up_bias = results[10:]
    done = {0: wq, 2: wk, 3: wv, 5: wo, 9: up, 11: down, 10: up_bias, **dict(zip(SMALL, small))}
    return (*rows, *(done[i] for i in range(15)))


def gathered_by_collectives(shards):
    full = tuple(lax.all_gather(shard, "fsdp", axis=0, tiled=True) for shard in shards)
    return tuple(a.astype(f32) if a.ndim == 1 else a for a in full)


def reduced_by_collectives(totals):
    reduced = lax.psum_scatter(totals, "fsdp", scatter_dimension=0, tiled=True)
    low = jax.tree.map(lambda a: a.astype(bf16), reduced)
    return jax.tree.map(lambda a: a.astype(f32), lax.psum(low, "dp"))


def layer_by_collectives(
    long_inputs, short_inputs, long_lengths, short_lengths, long_cotangent, short_cotangent, *shards
):
    weights = gathered_by_collectives(shards)
    long_output, long_saved = layer_pass(weights, long_inputs, long_lengths)
    short_output, short_saved = layer_pass(weights, short_inputs, short_lengths)
    long_grad, long_terms = layer_back(weights, long_saved, long_cotangent)
    short_grad, short_terms = layer_back(weights, short_saved, short_cotangent)
    totals = tuple((first + second for first, second in zip(long_terms, short_terms)))
    reduced = reduced_by_collectives(totals)
    return (long_output.astype(bf16), short_output.astype(bf16), long_grad, short_grad, *reduced)


def solution(mesh):
    rows = P(("fsdp", "dp"), None, None)
    count = P(("fsdp", "dp"))
    matrix, vector = P("fsdp", None), P("fsdp")
    params = tuple(matrix if i in (0, 2, 3, 5, 9, 11) else vector for i in range(15))
    by_kernel = mesh.shape["fsdp"] == 16 and mesh.shape["dp"] == 2
    return jax.shard_map(
        layer_by_kernel if by_kernel else layer_by_collectives,
        mesh=mesh,
        in_specs=(rows, rows, count, count, rows, rows, *params),
        out_specs=(rows, rows, rows, rows, *params),
        check_vma=False,
    )
```

```python
import functools
import math

import jax
import jax.numpy as jnp
from jax import lax
from jax.experimental import pallas as pl
from jax.experimental.pallas import tpu as pltpu
from jax.sharding import PartitionSpec as P

HEADS = 12
HEAD_DIM = 64
MESH = pl.DeviceIdType.MESH
DMA = pltpu.SemaphoreType.DMA
f32 = jnp.float32
bf16 = jnp.bfloat16

epsilon = 1e-05
masked_score = -1000000000.0


def matmul(left, right):
    return jnp.dot(left, right, preferred_element_type=f32)


def transposed(left, right):
    return lax.dot_general(left, right, (((0,), (0,)), ((), ())), preferred_element_type=f32)


def against(left, right):
    return lax.dot_general(left, right, (((1,), (1,)), ((), ())), preferred_element_type=f32)


def norm_forward(tensor, scales, offsets):
    centre = jnp.mean(tensor, axis=-1, keepdims=True)
    centred = tensor - centre
    inverse = lax.rsqrt(jnp.mean(centred * centred, axis=-1, keepdims=True) + epsilon)
    scaled = centred * inverse
    return (scaled * scales + offsets, scaled, inverse)


def norm_backward(upstream, scaled, inverse, scales):
    delta_scaled = upstream * scales
    plain_mean = jnp.mean(delta_scaled, axis=-1, keepdims=True)
    cross_mean = jnp.mean(delta_scaled * scaled, axis=-1, keepdims=True)
    delta_input = inverse * (delta_scaled - plain_mean - scaled * cross_mean)
    return (delta_input, jnp.sum(upstream * scaled, axis=0), jnp.sum(upstream, axis=0))


def layer_pass(weights, inputs, lengths):
    (
        query_weight,
        query_bias,
        key_weight,
        value_weight,
        value_bias,
        out_weight,
        out_bias,
        first_gain,
        first_shift,
        up_weight,
        up_bias,
        down_weight,
        down_bias,
        second_gain,
        second_shift,
    ) = weights
    count, length, width = inputs.shape
    heads_shape = (count, length, HEADS, HEAD_DIM)
    rows = inputs.reshape(count * length, width)
    queries = (matmul(rows, query_weight) + query_bias).astype(bf16).reshape(heads_shape)
    key_rows = matmul(rows, key_weight).astype(bf16).reshape(heads_shape)
    value_rows = (matmul(rows, value_weight) + value_bias).astype(bf16).reshape(heads_shape)
    score_scale = HEAD_DIM ** (-0.5)
    scores = jnp.einsum("bqhd,bkhd->bhqk", queries, key_rows, preferred_element_type=f32) * score_scale
    live = lax.broadcasted_iota(jnp.int32, (count, length), 1) < lengths[:, None]
    scores = jnp.where(live[:, None, None, :], scores, masked_score)
    highest = jnp.max(scores, axis=-1, keepdims=True)
    raised = jnp.exp(scores - highest)
    attention = raised / jnp.sum(raised, axis=-1, keepdims=True)
    attention_low = attention.astype(bf16)
    mixed = jnp.einsum("bhqk,bkhd->bqhd", attention_low, value_rows, preferred_element_type=f32)
    mixed = mixed.reshape(count * length, width).astype(bf16)
    branch = matmul(mixed, out_weight) + out_bias
    normed, scaled_one, inverse_one = norm_forward(rows.astype(f32) + branch, first_gain, first_shift)
    normed_low = normed.astype(bf16)
    inner = matmul(normed_low, up_weight) + up_bias
    hidden = jax.nn.gelu(inner, approximate=False).astype(bf16)
    update = matmul(hidden, down_weight) + down_bias
    final, scaled_two, inverse_two = norm_forward(normed + update, second_gain, second_shift)
    saved = (
        rows,
        queries,
        key_rows,
        value_rows,
        attention,
        attention_low,
        mixed,
        scaled_one,
        inverse_one,
        normed_low,
        inner,
        hidden,
        scaled_two,
        inverse_two,
    )
    return (final.reshape(count, length, width), saved)


def layer_back(weights, saved, cotangent):
    (
        query_weight,
        query_bias,
        key_weight,
        value_weight,
        value_bias,
        out_weight,
        out_bias,
        first_gain,
        first_shift,
        up_weight,
        up_bias,
        down_weight,
        down_bias,
        second_gain,
        second_shift,
    ) = weights
    (
        rows,
        queries,
        key_rows,
        value_rows,
        attention,
        attention_low,
        mixed,
        scaled_one,
        inverse_one,
        normed_low,
        inner,
        hidden,
        scaled_two,
        inverse_two,
    ) = saved
    count, length, width = cotangent.shape
    heads_shape = (count, length, HEADS, HEAD_DIM)
    score_scale = HEAD_DIM ** (-0.5)
    upstream = cotangent.reshape(count * length, width).astype(f32)
    grad_two, second_gain_term, second_shift_term = norm_backward(upstream, scaled_two, inverse_two, second_gain)
    delta_update = grad_two.astype(bf16)
    down_weight_term = transposed(hidden, delta_update)
    down_bias_term = jnp.sum(delta_update.astype(f32), axis=0)
    _, gelu_pull = jax.vjp(functools.partial(jax.nn.gelu, approximate=False), inner)
    delta_inner = gelu_pull(against(delta_update, down_weight))[0].astype(bf16)
    up_weight_term = transposed(normed_low, delta_inner)
    up_bias_term = jnp.sum(delta_inner.astype(f32), axis=0)
    grad_normed = against(delta_inner, up_weight) + grad_two
    grad_one, first_gain_term, first_shift_term = norm_backward(grad_normed, scaled_one, inverse_one, first_gain)
    delta_branch = grad_one.astype(bf16)
    out_weight_term = transposed(mixed, delta_branch)
    out_bias_term = jnp.sum(delta_branch.astype(f32), axis=0)
    delta_mixed = against(delta_branch, out_weight).astype(bf16).reshape(heads_shape)
    delta_values = jnp.einsum("bhqk,bqhd->bkhd", attention_low, delta_mixed, preferred_element_type=f32)
    delta_values = delta_values.astype(bf16).reshape(count * length, width)
    grad_attention = jnp.einsum("bqhd,bkhd->bhqk", delta_mixed, value_rows, preferred_element_type=f32)
    row_total = jnp.sum(attention * grad_attention, axis=-1, keepdims=True)
    delta_scores = (attention * (grad_attention - row_total)).astype(bf16)
    delta_queries = jnp.einsum("bhqk,bkhd->bqhd", delta_scores, key_rows, preferred_element_type=f32) * score_scale
    delta_queries = delta_queries.astype(bf16).reshape(count * length, width)
    delta_keys = jnp.einsum("bhqk,bqhd->bkhd", delta_scores, queries, preferred_element_type=f32) * score_scale
    delta_keys = delta_keys.astype(bf16).reshape(count * length, width)
    query_weight_term = transposed(rows, delta_queries)
    query_bias_term = jnp.sum(delta_queries.astype(f32), axis=0)
    key_weight_term = transposed(rows, delta_keys)
    value_weight_term = transposed(rows, delta_values)
    value_bias_term = jnp.sum(delta_values.astype(f32), axis=0)
    input_grad = (
        grad_one
        + against(delta_queries, query_weight)
        + against(delta_keys, key_weight)
        + against(delta_values, value_weight)
    )
    terms = (
        query_weight_term,
        query_bias_term,
        key_weight_term,
        value_weight_term,
        value_bias_term,
        out_weight_term,
        out_bias_term,
        first_gain_term,
        first_shift_term,
        up_weight_term,
        up_bias_term,
        down_weight_term,
        down_bias_term,
        second_gain_term,
        second_shift_term,
    )
    return (input_grad.reshape(count, length, width), terms)


class Place:
    def __init__(self):
        chip = lax.axis_index("fsdp")
        core = lax.axis_index("dp")
        z, y, x = chip // 4, (chip // 2) % 2, chip % 2
        self.z, self.y, self.x, self.core = z, y, x, core
        first = 1 - core
        self.own = (y, x)
        self.near = (jnp.where(core == 0, y, 1 - y), jnp.where(core == 0, 1 - x, x))
        self.far = (jnp.where(core == 0, 1 - y, y), jnp.where(core == 0, x, 1 - x))
        self.across = (1 - y, 1 - x)
        self.up = [(z + d) % 4 for d in (1, 2, 3)]
        self.down = [(z + 4 - d) % 4 for d in (1, 2, 3)]
        self.column = [self.device(q, y, x, core) for q in self.up]
        self.near_device = self.device(z, *self.near, core)
        self.far_device = self.device(z, *self.far, core)
        self.partner = self.device(z, y, x, 1 - core)

    def device(self, z, y, x, core):
        return (z * 4 + y * 2 + x, core)

    def greet(self):
        barrier = pltpu.get_barrier_semaphore()
        for peer in self.column + [self.near_device, self.far_device, self.partner]:
            pl.semaphore_signal(barrier, 1, device_id=peer, device_id_type=MESH)
        return barrier


def half(kind, core):
    if kind == "w":
        return (slice(None), pl.ds(pl.multiple_of(core * 384, 128), 384))
    if kind == "d":
        return (slice(None), pl.ds(pl.multiple_of(core * 128, 128), 128))
    return (pl.ds(pl.multiple_of(core * 8, 8), 8), slice(None))


UNIT = {"w": (48, 768), "d": (192, 256), "v": (16, 128)}
HALF = {"w": (48, 384), "d": (192, 128), "v": (8, 128)}
TYPE = {"w": bf16, "d": bf16, "v": f32}
COUNT = {"w": 8, "d": 3, "v": 1}
GATHER = [("v", 0)] + [("w", i) for i in range(8)] + [("d", i) for i in range(3)]
REDUCE = [("d", i) for i in range(3)] + [("w", i) for i in (4, 5, 6, 7, 3, 2, 1, 0)] + [("v", 0)]
JOBS = len(GATHER)
SMALL = (1, 4, 6, 7, 8, 12, 13, 14)
QUERY_BIAS, VALUE_BIAS, OUT_BIAS, FIRST_GAIN, FIRST_SHIFT, DOWN_BIAS, SECOND_GAIN, SECOND_SHIFT = range(8)
ORDER = (
    "g1.0", "g1.1", "g2.0", "g1.2", "g2.1", "g1.3", "g2.2", "g3.0", "g4.0", "g1.4",
    "g2.3", "g3.1", "g4.1", "g1.5", "g2.4", "g3.2", "g4.2", "g5.0", "g1.6", "g2.5",
    "g3.3", "g4.3", "g5.1", "g6.0", "spread.0", "g1.7", "g2.6", "g3.4", "g4.4", "g5.2",
    "g6.1", "project.0", "g1.8", "g2.7", "g3.5", "g4.5", "g5.3", "g6.2", "project.1", "g1.9",
    "g2.8", "g3.6", "g4.6", "g5.4", "g6.3", "project.2", "attend.0", "g1.10", "g2.9", "g3.7",
    "g4.7", "attend.1", "g5.5", "g6.4", "g1.11", "g2.10", "attend.2", "g3.8", "g4.8", "g5.6",
    "g6.5", "first_norm.0", "expand.0", "g2.11", "g3.9", "g4.9", "g5.7", "g6.6", "expand.1", "g3.10",
    "g4.10", "g5.8", "g6.7", "expand.2", "g3.11", "g4.11", "g5.9", "g6.8", "expand.3", "g5.10",
    "g6.9", "contract.0", "g5.11", "g6.10", "contract.1", "g6.11", "contract.2", "second_norm.0", "down_grad.0", "r0.0",
    "down_grad.1", "r0.1", "down_grad.2", "r0.2", "inner_grad.0", "up_grad.0", "r1.0", "r0.3", "inner_grad.1", "up_grad.1",
    "r1.1", "r0.4", "inner_grad.2", "up_grad.2", "r1.2", "r2.0", "r0.5", "inner_grad.3", "up_grad.3", "r1.3",
    "r2.1", "r0.6", "up_pull.0", "r1.4", "r2.2", "r3.0", "first_pull.0", "out_grad.0", "r0.7", "mixed_pull.0",
    "attend_pull.0", "r1.5", "r2.3", "r3.1", "r4.0", "attend_pull.1", "attend_pull.2", "attend_pull.3", "attend_pull.4", "attend_pull.5",
    "head_grad.0", "r0.8", "head_grad.1", "r1.6", "r2.4", "r3.2", "r4.1", "r0.9", "head_grad.2", "r1.7",
    "r2.5", "r3.3", "r4.2", "r0.10", "vectors.0", "r1.8", "r2.6", "r3.4", "r4.3", "r0.11",
    "input_pull.0", "r1.9", "r2.7", "r3.5", "r4.4", "input_pull.1", "r1.10", "r2.8", "r3.6", "r4.5",
    "r1.11", "r2.9", "r3.7", "r4.6", "r2.10", "r3.8", "r4.7", "r2.11", "r3.9", "r4.8",
    "r3.10", "r4.9", "r3.11", "r4.10", "r4.11",
)
D = 768
TILE = 192
PAIRS = HEADS // 2
BLOCK = 128


class Sender:
    def __init__(self, place):
        self.place = place
        self.started = []

    def copy(self, source, target, send, receive, device):
        return pltpu.make_async_remote_copy(
            source, target, send, receive, device_id=device, device_id_type=MESH
        )

    def send(self, source, target, send, receive, device):
        copy = self.copy(source, target, send, receive, device)
        copy.start()
        self.started.append(copy)

    def arrived(self, target, send, receive):
        self.copy(target, target, send, receive, self.place.partner).wait_recv()

    def finish(self):
        for copy in self.started:
            copy.wait_send()


def gather_steps(place, sender, given, whole, own_s, z_s, z_r, h_s, h_r, p_s, p_r):
    z, core = place.z, place.core
    local = [
        pltpu.make_async_copy(
            given(kind, i, half(kind, core)),
            whole[kind].at[(i, z, *place.own, *half(kind, core))],
            own_s.at[n],
        )
        for n, (kind, i) in enumerate(GATHER)
    ]
    for copy in local:
        copy.start()

    def unit(n, q):
        kind, i = GATHER[n]
        return whole[kind].at[(i, q, *place.own, *half(kind, core))]

    def column(n, spot, core=core):
        kind, i = GATHER[n]
        return whole[kind].at[(i, slice(None), *spot, *half(kind, core))]

    def pass_on(n, spot, j, to):
        part = column(n, spot)
        sender.send(part, part, h_s.at[n, j], h_r.at[n, j], to)

    def share(n, spot, j):
        part = column(n, spot)
        sender.send(part, part, p_s.at[n, j], p_r.at[n, j], place.partner)

    def first(n):
        local[n].wait()
        for j in range(3):
            sender.send(unit(n, z), unit(n, z), z_s.at[n, j], z_r.at[n, j], place.column[j])

    def second(n):
        for j in range(3):
            sender.arrived(unit(n, place.down[j]), z_s.at[n, j], z_r.at[n, j])
        pass_on(n, place.own, 0, place.near_device)
        pass_on(n, place.own, 1, place.far_device)
        share(n, place.own, 0)

    def third(n):
        sender.arrived(column(n, place.near), h_s.at[n, 0], h_r.at[n, 0])
        pass_on(n, place.near, 2, place.far_device)
        share(n, place.near, 1)

    def fourth(n):
        sender.arrived(column(n, place.far), h_s.at[n, 1], h_r.at[n, 1])
        share(n, place.far, 2)

    def fifth(n):
        sender.arrived(column(n, place.across), h_s.at[n, 2], h_r.at[n, 2])
        share(n, place.across, 3)

    def complete(n):
        for j, spot in enumerate((place.own, place.far, place.near, place.across)):
            sender.arrived(column(n, spot, 1 - core), p_s.at[n, j], p_r.at[n, j])

    return {"g1": first, "g2": second, "g3": third, "g4": fourth, "g5": fifth, "g6": complete}


def reduce_steps(place, sender, total, shared, far, near, high, final, out, p_s, p_r, h_s, h_r, z_s, z_r, f_s, f_r, o_s):
    z, core = place.z, place.core

    def add(n, spot, more):
        kind, i = REDUCE[n]
        ref = total(kind, i)

        def one(q, _):
            at = (core, q, *spot)
            ref[at] = (ref[at].astype(f32) + more[q].astype(f32)).astype(TYPE[kind])
            return 0

        lax.fori_loop(0, 4, one, 0)

    def column(n, spot):
        return total(*REDUCE[n]).at[(core, slice(None), *spot)]

    def give(n):
        kind, i = REDUCE[n]
        sender.send(total(kind, i).at[1 - core], shared[kind].at[i], p_s.at[n], p_r.at[n], place.partner)

    def first(n):
        kind, i = REDUCE[n]
        sender.arrived(shared[kind].at[i], p_s.at[n], p_r.at[n])
        for j, spot in enumerate((place.across, place.far)):
            add(n, spot, shared[kind].at[(i, slice(None), *spot)])
            sender.send(column(n, spot), far[kind].at[i, j], h_s.at[n, j], h_r.at[n, j], place.far_device)
        for spot in (place.near, place.own):
            add(n, spot, shared[kind].at[(i, slice(None), *spot)])

    def second(n):
        kind, i = REDUCE[n]
        sender.arrived(far[kind].at[i, 0], h_s.at[n, 0], h_r.at[n, 0])
        add(n, place.near, far[kind].at[i, 0])
        sender.send(column(n, place.near), near[kind].at[i], h_s.at[n, 2], h_r.at[n, 2], place.near_device)

    def third(n):
        kind, i = REDUCE[n]
        sender.arrived(far[kind].at[i, 1], h_s.at[n, 1], h_r.at[n, 1])
        add(n, place.own, far[kind].at[i, 1])
        sender.arrived(near[kind].at[i], h_s.at[n, 2], h_r.at[n, 2])
        add(n, place.own, near[kind].at[i])
        for j in range(3):
            part = total(kind, i).at[(core, place.up[j], *place.own)]
            sender.send(part, high[kind].at[i, j], z_s.at[n, j], z_r.at[n, j], place.column[j])

    def fourth(n):
        kind, i = REDUCE[n]
        mine = total(kind, i)[(core, z, *place.own)].astype(f32)
        for j in range(3):
            sender.arrived(high[kind].at[i, j], z_s.at[n, j], z_r.at[n, j])
            mine = mine + high[kind][i, j].astype(f32)
        final[kind][i] = mine
        mine_out = out(kind, i, core)
        sender.send(final[kind].at[i], mine_out, f_s.at[n], f_r.at[n], place.partner)
        pltpu.make_async_copy(final[kind].at[i], mine_out, o_s.at[n]).start()

    def stored(n):
        kind, i = REDUCE[n]
        pltpu.make_async_copy(final[kind].at[i], out(kind, i, core), o_s.at[n]).wait()
        sender.arrived(out(kind, i, 1 - core), f_s.at[n], f_r.at[n])

    return {"r0": give, "r1": first, "r2": second, "r3": third, "r4": fourth, "r5": stored}


def iota(shape, axis):
    return lax.broadcasted_iota(jnp.int32, shape, axis)


def loop(count, body):
    def step(i, _):
        body(i)
        return 0

    lax.fori_loop(0, count, step, 0)


def tile_rows(i):
    return pl.ds(pl.multiple_of(i * TILE, TILE), TILE)


def flat(value):
    return value.reshape(math.prod(value.shape[:-1]), value.shape[-1])


def spread_table():
    return jnp.where(iota((128, D), 1) % 48 == iota((128, D), 0), 1.0, 0.0)


def spread_tables_wide():
    l = iota((128, D), 1) % 192
    j = iota((128, D), 0)
    return jnp.where(l == j, 1.0, 0.0), jnp.where(l == j + 128, 1.0, 0.0)


def wide_rows():
    row = iota((64, D), 0)
    mine = iota((64, D), 1) // 192 == row // 16
    return mine & (row % 16 == 8), mine & (row % 16 == 9)


def total_over(mask, value):
    return jnp.sum(jnp.where(mask, value, 0.0), axis=0, keepdims=True)


def fused_kernel(
    long_lengths,
    short_lengths,
    long_inputs,
    short_inputs,
    long_cotangent,
    short_cotangent,
    wq_in,
    wk_in,
    wv_in,
    wo_in,
    up_in,
    down_in,
    v_in,
    long_output,
    short_output,
    long_grad,
    short_grad,
    wq_out,
    wk_out,
    wv_out,
    wo_out,
    up_out,
    down_out,
    v_out,
    w,
    d,
    v,
    shared_w,
    shared_d,
    shared_v,
    far_w,
    far_d,
    far_v,
    near_w,
    near_d,
    near_v,
    high_w,
    high_d,
    high_v,
    final_w,
    final_d,
    final_v,
    total_d,
    total_v,
    x,
    c,
    q,
    k,
    vl,
    mixed,
    xhat,
    inverse,
    low,
    hidden,
    slope,
    acc,
    delta,
    vec,
    stats,
    up_bias,
    small,
    up_bias_sum,
    own_s,
    gz_s,
    gz_r,
    gh_s,
    gh_r,
    gp_s,
    gp_r,
    p_s,
    p_r,
    h_s,
    h_r,
    z_s,
    z_r,
    f_s,
    f_r,
    o_s,
    in_s,
    out_s,
):
    place = Place()
    barrier = place.greet()
    sender = Sender(place)
    matrices_in = (wq_in, wk_in, wv_in, wo_in)
    matrices_out = (wq_out, wk_out, wv_out, wo_out)

    def given(kind, i, at):
        rows, cols = at
        if kind == "v":
            return v_in.at[rows, cols]
        core = place.core
        if kind == "d":
            return down_in.at[:, pl.ds(pl.multiple_of(256 * i + core * 128, 128), 128)]
        if i < 4:
            return matrices_in[i].at[rows, cols]
        return up_in.at[:, pl.ds(pl.multiple_of(D * (i - 4) + core * 384, 128), 384)]

    def out(kind, i, core):
        rows, cols = half(kind, core)
        if kind == "v":
            return v_out.at[rows, cols]
        if kind == "d":
            return down_out.at[:, pl.ds(pl.multiple_of(256 * i + core * 128, 128), 128)]
        if i < 4:
            return matrices_out[i].at[rows, cols]
        return up_out.at[:, pl.ds(pl.multiple_of(D * (i - 4) + core * 384, 128), 384)]

    def total(kind, i):
        if kind == "d":
            return total_d.at[i]
        if kind == "v":
            return total_v
        return hidden.at[i - 4] if i >= 4 else slope.at[i]

    steps = gather_steps(
        place, sender, given, {"w": w, "d": d, "v": v}, own_s, gz_s, gz_r, gh_s, gh_r, gp_s, gp_r
    )
    steps |= reduce_steps(
        place,
        sender,
        total,
        {"w": shared_w, "d": shared_d, "v": shared_v},
        {"w": far_w, "d": far_d, "v": far_v},
        {"w": near_w, "d": near_d, "v": near_v},
        {"w": high_w, "d": high_d, "v": high_v},
        {"w": final_w, "d": final_d, "v": final_v},
        out,
        p_s,
        p_r,
        h_s,
        h_r,
        z_s,
        z_r,
        f_s,
        f_r,
        o_s,
    )

    count, length, _ = long_inputs.shape
    short = short_inputs.shape[1]

    def groups(buffer, long_ref, short_ref, outward, s):
        copies = []
        for i in range(count):
            copies.append((buffer.at[i * length : (i + 1) * length], long_ref.at[i]))
        for i in range(count):
            start = count * length + i * short
            copies.append((buffer.at[start : start + short], short_ref.at[i]))
        return [
            pltpu.make_async_copy(*((a, b) if outward else (b, a)), s.at[i]) for i, (a, b) in enumerate(copies)
        ]

    x_copies = groups(x, long_inputs, short_inputs, False, in_s.at[0])
    c_copies = groups(c, long_cotangent, short_cotangent, False, in_s.at[1])
    for copy in x_copies + c_copies:
        copy.start()
    small[...] = jnp.zeros_like(small)
    up_bias_sum[...] = jnp.zeros_like(up_bias_sum)
    total_v[...] = jnp.zeros_like(total_v)
    pl.semaphore_wait(barrier, 6)

    def weight(i):
        return flat(w[i])

    def row(at):
        return vec[at : at + 1, :]


    def spread():
        wide = matmul(flat(v[0]).astype(bf16), spread_table().astype(bf16))
        mine = iota((256, D), 1) // 48 == iota((256, D), 0) // 16
        vec[...] = jnp.sum(jnp.where(mine, wide, 0.0).reshape(16, 16, D), axis=0)
        table_a, table_b = spread_tables_wide()
        mask_a, mask_b = wide_rows()
        for j in range(4):
            unit = flat(v[0, j]).astype(bf16)
            up_bias[j : j + 1, :] = total_over(mask_a, matmul(unit, table_a.astype(bf16))) + total_over(
                mask_b, matmul(unit, table_b.astype(bf16))
            )

    def project(i, target, bias, scale=1.0):
        result = matmul(x[...], weight(i))
        if bias is not None:
            result = result + row(bias)
        result = (result.astype(bf16) * scale).astype(bf16)
        for p in range(PAIRS):
            target[p] = result[:, 128 * p : 128 * p + 128]

    left_lanes = iota((BLOCK, BLOCK), 1) < HEAD_DIM

    def stacked(value):
        none = jnp.zeros_like(value)
        return jnp.concatenate([jnp.where(left_lanes, value, none), jnp.where(left_lanes, none, value)], axis=0)

    def picked(value):
        return jnp.where(left_lanes, value[:BLOCK], value[BLOCK:])

    def live_keys(b, is_long):
        key = iota((BLOCK, BLOCK), 0)
        if is_long:
            return key < long_lengths[b]
        left = key < short
        limit = jnp.where(left, short_lengths[2 * b], short + short_lengths[2 * b + 1])
        return (key < limit) & (left == (iota((BLOCK, BLOCK), 1) < short))

    def block_rows(b, is_long):
        start = b * BLOCK if is_long else count * length + b * BLOCK
        return pl.ds(pl.multiple_of(start, BLOCK), BLOCK)

    def block_scores(p, rows, live):
        scores = against(stacked(k[p, rows, :]), q[p, rows, :])
        return [jnp.where(live, scores[BLOCK * head : BLOCK * head + BLOCK], masked_score) for head in range(2)]

    def attend(b, is_long):
        rows = block_rows(b, is_long)
        live = live_keys(b, is_long)
        at = b if is_long else b + count
        results = []
        for p in range(PAIRS):
            parts = []
            for head, part in enumerate(block_scores(p, rows, live)):
                highest = jnp.max(part, axis=0, keepdims=True)
                raised = jnp.exp(part - highest)
                scale = 1.0 / jnp.sum(raised, axis=0, keepdims=True)
                stats[at, 2 * p + head : 2 * p + head + 1, :] = highest
                stats[at, HEADS + 2 * p + head : HEADS + 2 * p + head + 1, :] = scale
                parts.append((raised * scale).astype(bf16))
            both = jnp.concatenate(parts, axis=0)
            results.append(transposed(both, stacked(vl[p, rows, :])).astype(bf16))
        mixed[rows, :] = jnp.concatenate(results, axis=1)

    def branch():
        acc[...] = matmul(mixed[...], weight(3)) + row(OUT_BIAS)

    def first_norm(t):
        rows = tile_rows(t)
        normed, scaled, inv = norm_forward(x[rows, :].astype(f32) + acc[rows, :], row(FIRST_GAIN), row(FIRST_SHIFT))
        xhat[rows, :] = scaled
        inverse[rows, :] = inv
        low[rows, :] = normed.astype(bf16)

    def put(buffer, j, value):
        for side in range(2):
            buffer[j, side] = value[:, 384 * side : 384 * side + 384].reshape(4, 2, 2, 48, 384)

    def take(buffer, j):
        return jnp.concatenate([flat(buffer[j, side]) for side in range(2)], axis=1)

    def expand(j):
        inner = matmul(low[...], weight(4 + j)) + up_bias[j : j + 1, :]
        phi = 0.5 + 0.5 * lax.erf(inner * 0.5**0.5)
        put(hidden, j, (inner * phi).astype(bf16))
        density = jnp.exp(-0.5 * inner * inner) * (2 * math.pi) ** -0.5
        put(slope, j, (phi + inner * density).astype(bf16))

    def contract(n):
        update = row(DOWN_BIAS)[:, 256 * n : 256 * n + 256]
        for j in range(4):
            update = update + matmul(take(hidden, j), flat(d[n, j]))
        acc[:, 256 * n : 256 * n + 256] = update

    def tally(at, value):
        small[at : at + 1, :] += jnp.sum(value, axis=0, keepdims=True)

    def norm_pull(upstream, scaled, inv, gain):
        g = upstream * gain
        plain = jnp.mean(g, axis=-1, keepdims=True)
        cross = jnp.mean(g * scaled, axis=-1, keepdims=True)
        return inv * (g - plain - scaled * cross)

    def second_norm(t):
        rows = tile_rows(t)
        normed = xhat[rows, :] * row(FIRST_GAIN) + row(FIRST_SHIFT)
        final, scaled, inv = norm_forward(normed + acc[rows, :], row(SECOND_GAIN), row(SECOND_SHIFT))
        upstream = c[rows, :].astype(f32)
        c[rows, :] = final.astype(bf16)
        tally(SECOND_GAIN, upstream * scaled)
        tally(SECOND_SHIFT, upstream)
        grad = norm_pull(upstream, scaled, inv, row(SECOND_GAIN))
        acc[rows, :] = grad
        lowered = grad.astype(bf16)
        delta[rows, :] = lowered
        tally(DOWN_BIAS, lowered.astype(f32))


    def down_grad(n):
        for j in range(4):
            grad = transposed(take(hidden, j), delta[:, 256 * n : 256 * n + 256]).astype(bf16)
            for side in range(2):
                total_d[n, side, j] = grad[:, 128 * side : 128 * side + 128].reshape(2, 2, 192, 128)

    def inner_grad(j):
        pulled = against(delta[...], jnp.concatenate([flat(d[n, j]) for n in range(3)], axis=1))
        inner = (pulled * take(slope, j).astype(f32)).astype(bf16)
        put(slope, j, inner)
        up_bias_sum[j : j + 1, :] = jnp.sum(inner.astype(f32), axis=0, keepdims=True)

    def weight_grad(left, right, buffer, slot):
        put(buffer, slot, transposed(left[...], right()).astype(bf16))

    def up_pull():
        grad = acc[...]
        for j in range(4):
            grad = grad + against(take(slope, j), weight(4 + j))
        acc[...] = grad

    def first_pull(t):
        rows = tile_rows(t)
        upstream = acc[rows, :]
        scaled = xhat[rows, :]
        tally(FIRST_GAIN, upstream * scaled)
        tally(FIRST_SHIFT, upstream)
        grad = norm_pull(upstream, scaled, inverse[rows, :], row(FIRST_GAIN))
        acc[rows, :] = grad
        lowered = grad.astype(bf16)
        delta[rows, :] = lowered
        tally(OUT_BIAS, lowered.astype(f32))

    def mixed_pull():
        mixed[...] = against(delta[...], weight(3)).astype(bf16)

    def attend_pull(b, is_long):
        rows = block_rows(b, is_long)
        live = live_keys(b, is_long)
        at = b if is_long else b + count
        results = []
        for p in range(PAIRS):
            down = mixed[rows, 128 * p : 128 * p + 128]
            probs = []
            for head, part in enumerate(block_scores(p, rows, live)):
                highest = stats[at, 2 * p + head : 2 * p + head + 1, :]
                scale = stats[at, HEADS + 2 * p + head : HEADS + 2 * p + head + 1, :]
                probs.append(jnp.exp(part - highest) * scale)
            both = jnp.concatenate(probs, axis=0).astype(bf16)
            grad_values = picked(matmul(both, down))
            grad_probs = against(stacked(vl[p, rows, :]), down)
            parts = []
            for head in range(2):
                part = grad_probs[BLOCK * head : BLOCK * head + BLOCK]
                mean = jnp.sum(probs[head] * part, axis=0, keepdims=True)
                parts.append((probs[head] * (part - mean)).astype(bf16))
            grad_scores = jnp.concatenate(parts, axis=0)
            grad_queries = transposed(grad_scores, stacked(k[p, rows, :])) * HEAD_DIM**-0.5
            grad_keys = picked(matmul(grad_scores, q[p, rows, :]))
            results.append((grad_queries.astype(bf16), grad_keys.astype(bf16), grad_values.astype(bf16)))
        for p, (grad_queries, grad_keys, grad_values) in enumerate(results):
            q[p, rows, :] = grad_queries
            k[p, rows, :] = grad_keys
            vl[p, rows, :] = grad_values

    def joined(heads):
        return lambda: jnp.concatenate([heads[p] for p in range(PAIRS)], axis=1)

    def head_sum(at, heads):
        for p in range(PAIRS):
            small[at : at + 1, 128 * p : 128 * p + 128] = jnp.sum(heads[p].astype(f32), axis=0, keepdims=True)

    def input_pull(t):
        rows = slice(384 * t, 384 * t + 384)
        grad = acc[rows, :]
        for i, heads in enumerate((q, k, vl)):
            grad = grad + against(jnp.concatenate([heads[p, rows, :] for p in range(PAIRS)], axis=1), weight(i))
        acc[rows, :] = grad

    def exact(left, right):
        return lax.dot_general(
            left, right, (((1,), (1,)), ((), ())), precision=lax.Precision.HIGHEST, preferred_element_type=f32
        )

    def vectors_out():
        mine = iota((16, 8, D), 2) // 48 == iota((16, 8, D), 0)
        pieces = jnp.where(mine, jnp.broadcast_to(small[...][None], (16, 8, D)), 0.0).reshape(128, D)
        total_v[0] = exact(pieces, spread_table()).reshape(4, 2, 2, 8, 128)
        table_a, table_b = spread_tables_wide()
        mask_a, mask_b = wide_rows()
        for j in range(4):
            sums = jnp.broadcast_to(up_bias_sum[j : j + 1, :], (64, D))
            wide = exact(jnp.where(mask_a, sums, 0.0), table_a) + exact(jnp.where(mask_b, sums, 0.0), table_b)
            total_v[1, j] = wide.reshape(2, 2, 16, 128)[:, :, 8:, :]


    def wait_all(copies):
        for copy in copies:
            copy.wait()

    def start_all(copies):
        for copy in copies:
            copy.start()

    final_copies = groups(c, long_output, short_output, True, out_s.at[0])
    grad_copies = groups(acc, long_grad, short_grad, True, out_s.at[1])

    def project_all(i):
        if i == 0:
            wait_all(x_copies)
        project(i, (q, k, vl)[i], (QUERY_BIAS, None, VALUE_BIAS)[i], HEAD_DIM**-0.5 if i == 0 else 1.0)

    def attend_all(i):
        if 2 * i < count:
            loop(2, lambda b: attend(2 * i + b, True))
        else:
            loop(count // 2, lambda b: attend(b, False))

    def normalise():
        branch()
        loop(4, first_norm)

    def finish():
        wait_all(c_copies)
        loop(4, second_norm)
        start_all(final_copies)

    def attend_pull_all(b):
        attend_pull(b % count, b < count)

    def head_grad(i):
        weight_grad(x, joined((vl, k, q)[i]), slope, 2 - i)

    def vector_grads():
        head_sum(QUERY_BIAS, q)
        head_sum(VALUE_BIAS, vl)
        vectors_out()

    def input_pull_all(t):
        input_pull(t)
        if t == 1:
            start_all(grad_copies)

    steps |= {
        "spread": lambda _: spread(),
        "project": project_all,
        "attend": attend_all,
        "first_norm": lambda _: normalise(),
        "expand": expand,
        "contract": contract,
        "second_norm": lambda _: finish(),
        "down_grad": down_grad,
        "inner_grad": inner_grad,
        "up_grad": lambda j: weight_grad(low, lambda: take(slope, j), hidden, j),
        "up_pull": lambda _: up_pull(),
        "first_pull": lambda _: loop(4, first_pull),
        "out_grad": lambda _: weight_grad(mixed, lambda: delta[...], slope, 3),
        "mixed_pull": lambda _: mixed_pull(),
        "attend_pull": attend_pull_all,
        "head_grad": head_grad,
        "vectors": lambda _: vector_grads(),
        "input_pull": input_pull_all,
    }
    for entry in ORDER:
        name, at = entry.split(".")
        steps[name](int(at))
    sender.finish()
    wait_all(final_copies + grad_copies)
    for n in range(JOBS):
        steps["r5"](n)


def fused(lengths, rows, matrices, vectors):
    long_inputs, short_inputs = rows[:2]
    count = long_inputs.shape[0]
    tokens = count * (long_inputs.shape[1] + short_inputs.shape[1])
    n = JOBS
    anywhere = pl.BlockSpec(memory_space=pl.ANY)
    scalar = pl.BlockSpec(memory_space=pltpu.SMEM)
    spots = (4, 2, 2)
    scratch = [pltpu.VMEM((COUNT[kind], *spots, *UNIT[kind]), TYPE[kind]) for kind in "wdv"]
    for lead in (spots, (2, 4), (4,), (3,)):
        scratch += [pltpu.VMEM((COUNT[kind], *lead, *HALF[kind]), TYPE[kind]) for kind in "wdv"]
    scratch += [pltpu.VMEM((COUNT[kind], *HALF[kind]), f32) for kind in "wdv"]
    scratch += [pltpu.VMEM((3, 2, *spots, *HALF["d"]), bf16), pltpu.VMEM((2, *spots, *HALF["v"]), f32)]
    heads = pltpu.VMEM((PAIRS, tokens, 128), bf16)
    low = pltpu.VMEM((tokens, D), bf16)
    high = pltpu.VMEM((tokens, D), f32)
    wide = pltpu.VMEM((4, 2, *spots, *HALF["w"]), bf16)
    scratch += [low, low, heads, heads, heads, low, high, pltpu.VMEM((tokens, 1), f32), low, wide, wide, high, low]
    scratch += [pltpu.VMEM((16, D), f32), pltpu.VMEM((count + count // 2, 2 * HEADS, BLOCK), f32), pltpu.VMEM((4, D), f32), pltpu.VMEM((8, D), f32), pltpu.VMEM((4, D), f32)]
    scratch += [DMA((n,))] + [DMA((n, 3))] * 4 + [DMA((n, 4))] * 2
    scratch += [DMA((n,))] * 2 + [DMA((n, 3))] * 4 + [DMA((n,))] * 2 + [DMA((n,)), DMA((2, 2 * count)), DMA((2, 2 * count))]
    results = [jax.ShapeDtypeStruct(a.shape, bf16) for a in rows[:2]]
    results += [jax.ShapeDtypeStruct(a.shape, f32) for a in rows[:2]]
    results += [jax.ShapeDtypeStruct(a.shape, f32) for a in matrices]
    results += [jax.ShapeDtypeStruct((16, 128), f32)]
    return pl.pallas_call(
        fused_kernel,
        out_shape=results,
        in_specs=[scalar] * 2 + [anywhere] * 11,
        out_specs=[anywhere] * 11,
        scratch_shapes=scratch,
        compiler_params=pltpu.CompilerParams(
            collective_id=0, has_side_effects=True, vmem_limit_bytes=61 << 20
        ),
        name="layer",
    )(*lengths, *rows, *matrices, vectors)


def deliver_kernel(*refs):
    sources, targets, held = refs[:11], refs[11:30], refs[30:41]
    in_s, out_s = refs[41:]
    loads = [pltpu.make_async_copy(sources[at], held[at], in_s.at[at]) for at in range(11)]
    stores = [pltpu.make_async_copy(held[at], targets[at], out_s.at[at]) for at in range(10)]
    for load in loads:
        load.start()
    for load, store in zip(loads, stores):
        load.wait()
        store.start()
    loads[10].wait()
    v = held[10]
    for at in range(8):
        targets[10 + at][...] = v[at, :48]
    targets[18][0:128] = v[8]
    targets[18][128:192] = v[9, :64]
    for store in stores:
        store.wait()


def deliver(results):
    anywhere = pl.BlockSpec(memory_space=pl.ANY)
    vmem = pl.BlockSpec(memory_space=pltpu.VMEM)
    vectors = [jax.ShapeDtypeStruct((48,), f32)] * 8 + [jax.ShapeDtypeStruct((192,), f32)]
    return pl.pallas_call(
        deliver_kernel,
        out_shape=[jax.ShapeDtypeStruct(a.shape, a.dtype) for a in results[:10]] + vectors,
        in_specs=[anywhere] * 11,
        out_specs=[anywhere] * 10 + [vmem] * 9,
        scratch_shapes=[pltpu.VMEM(a.shape, a.dtype) for a in results] + [DMA((11,)), DMA((10,))],
        compiler_params=pltpu.CompilerParams(vmem_limit_bytes=60 << 20),
        name="deliver",
    )(*results)


def layer_by_kernel(long_inputs, short_inputs, long_lengths, short_lengths, long_cotangent, short_cotangent, *shards):
    small = jnp.pad(jnp.stack([shards[i] for i in SMALL]), ((0, 0), (0, 80)))
    tail = jnp.pad(shards[10], (0, 64)).reshape(2, 128)
    vectors = jnp.pad(jnp.concatenate([small, tail]), ((0, 6), (0, 0))).astype(f32)
    results = fused(
        (long_lengths, short_lengths),
        (long_inputs, short_inputs, long_cotangent, short_cotangent),
        tuple(shards[i] for i in (0, 2, 3, 5, 9, 11)),
        vectors,
    )
    results = deliver(results)
    *rows, wq, wk, wv, wo, up, down = results[:10]
    *small, up_bias = results[10:]
    done = {0: wq, 2: wk, 3: wv, 5: wo, 9: up, 11: down, 10: up_bias, **dict(zip(SMALL, small))}
    return (*rows, *(done[i] for i in range(15)))


def gathered_by_collectives(shards):
    full = tuple(lax.all_gather(shard, "fsdp", axis=0, tiled=True) for shard in shards)
    return tuple(a.astype(f32) if a.ndim == 1 else a for a in full)


def reduced_by_collectives(totals):
    reduced = lax.psum_scatter(totals, "fsdp", scatter_dimension=0, tiled=True)
    low = jax.tree.map(lambda a: a.astype(bf16), reduced)
    return jax.tree.map(lambda a: a.astype(f32), lax.psum(low, "dp"))


def layer_by_collectives(
    long_inputs, short_inputs, long_lengths, short_lengths, long_cotangent, short_cotangent, *shards
):
    weights = gathered_by_collectives(shards)
    long_output, long_saved = layer_pass(weights, long_inputs, long_lengths)
    short_output, short_saved = layer_pass(weights, short_inputs, short_lengths)
    long_grad, long_terms = layer_back(weights, long_saved, long_cotangent)
    short_grad, short_terms = layer_back(weights, short_saved, short_cotangent)
    totals = tuple((first + second for first, second in zip(long_terms, short_terms)))
    reduced = reduced_by_collectives(totals)
    return (long_output.astype(bf16), short_output.astype(bf16), long_grad, short_grad, *reduced)


def solution(mesh):
    rows = P(("fsdp", "dp"), None, None)
    count = P(("fsdp", "dp"))
    matrix, vector = P("fsdp", None), P("fsdp")
    params = tuple(matrix if i in (0, 2, 3, 5, 9, 11) else vector for i in range(15))
    by_kernel = mesh.shape["fsdp"] == 16 and mesh.shape["dp"] == 2
    return jax.shard_map(
        layer_by_kernel if by_kernel else layer_by_collectives,
        mesh=mesh,
        in_specs=(rows, rows, count, count, rows, rows, *params),
        out_specs=(rows, rows, rows, rows, *params),
        check_vma=False,
    )
```

```python
import functools
import math

import jax
import jax.numpy as jnp
from jax import lax
from jax.experimental import pallas as pl
from jax.experimental.pallas import tpu as pltpu
from jax.sharding import PartitionSpec as P

HEADS = 12
HEAD_DIM = 64
MESH = pl.DeviceIdType.MESH
DMA = pltpu.SemaphoreType.DMA
f32 = jnp.float32
bf16 = jnp.bfloat16

epsilon = 1e-05
masked_score = -1000000000.0


def matmul(left, right):
    return jnp.dot(left, right, preferred_element_type=f32)


def transposed(left, right):
    return lax.dot_general(left, right, (((0,), (0,)), ((), ())), preferred_element_type=f32)


def against(left, right):
    return lax.dot_general(left, right, (((1,), (1,)), ((), ())), preferred_element_type=f32)


def norm_forward(tensor, scales, offsets):
    centre = jnp.mean(tensor, axis=-1, keepdims=True)
    centred = tensor - centre
    inverse = lax.rsqrt(jnp.mean(centred * centred, axis=-1, keepdims=True) + epsilon)
    scaled = centred * inverse
    return (scaled * scales + offsets, scaled, inverse)


def norm_backward(upstream, scaled, inverse, scales):
    delta_scaled = upstream * scales
    plain_mean = jnp.mean(delta_scaled, axis=-1, keepdims=True)
    cross_mean = jnp.mean(delta_scaled * scaled, axis=-1, keepdims=True)
    delta_input = inverse * (delta_scaled - plain_mean - scaled * cross_mean)
    return (delta_input, jnp.sum(upstream * scaled, axis=0), jnp.sum(upstream, axis=0))


def layer_pass(weights, inputs, lengths):
    (
        query_weight,
        query_bias,
        key_weight,
        value_weight,
        value_bias,
        out_weight,
        out_bias,
        first_gain,
        first_shift,
        up_weight,
        up_bias,
        down_weight,
        down_bias,
        second_gain,
        second_shift,
    ) = weights
    count, length, width = inputs.shape
    heads_shape = (count, length, HEADS, HEAD_DIM)
    rows = inputs.reshape(count * length, width)
    queries = (matmul(rows, query_weight) + query_bias).astype(bf16).reshape(heads_shape)
    key_rows = matmul(rows, key_weight).astype(bf16).reshape(heads_shape)
    value_rows = (matmul(rows, value_weight) + value_bias).astype(bf16).reshape(heads_shape)
    score_scale = HEAD_DIM ** (-0.5)
    scores = jnp.einsum("bqhd,bkhd->bhqk", queries, key_rows, preferred_element_type=f32) * score_scale
    live = lax.broadcasted_iota(jnp.int32, (count, length), 1) < lengths[:, None]
    scores = jnp.where(live[:, None, None, :], scores, masked_score)
    highest = jnp.max(scores, axis=-1, keepdims=True)
    raised = jnp.exp(scores - highest)
    attention = raised / jnp.sum(raised, axis=-1, keepdims=True)
    attention_low = attention.astype(bf16)
    mixed = jnp.einsum("bhqk,bkhd->bqhd", attention_low, value_rows, preferred_element_type=f32)
    mixed = mixed.reshape(count * length, width).astype(bf16)
    branch = matmul(mixed, out_weight) + out_bias
    normed, scaled_one, inverse_one = norm_forward(rows.astype(f32) + branch, first_gain, first_shift)
    normed_low = normed.astype(bf16)
    inner = matmul(normed_low, up_weight) + up_bias
    hidden = jax.nn.gelu(inner, approximate=False).astype(bf16)
    update = matmul(hidden, down_weight) + down_bias
    final, scaled_two, inverse_two = norm_forward(normed + update, second_gain, second_shift)
    saved = (
        rows,
        queries,
        key_rows,
        value_rows,
        attention,
        attention_low,
        mixed,
        scaled_one,
        inverse_one,
        normed_low,
        inner,
        hidden,
        scaled_two,
        inverse_two,
    )
    return (final.reshape(count, length, width), saved)


def layer_back(weights, saved, cotangent):
    (
        query_weight,
        query_bias,
        key_weight,
        value_weight,
        value_bias,
        out_weight,
        out_bias,
        first_gain,
        first_shift,
        up_weight,
        up_bias,
        down_weight,
        down_bias,
        second_gain,
        second_shift,
    ) = weights
    (
        rows,
        queries,
        key_rows,
        value_rows,
        attention,
        attention_low,
        mixed,
        scaled_one,
        inverse_one,
        normed_low,
        inner,
        hidden,
        scaled_two,
        inverse_two,
    ) = saved
    count, length, width = cotangent.shape
    heads_shape = (count, length, HEADS, HEAD_DIM)
    score_scale = HEAD_DIM ** (-0.5)
    upstream = cotangent.reshape(count * length, width).astype(f32)
    grad_two, second_gain_term, second_shift_term = norm_backward(upstream, scaled_two, inverse_two, second_gain)
    delta_update = grad_two.astype(bf16)
    down_weight_term = transposed(hidden, delta_update)
    down_bias_term = jnp.sum(delta_update.astype(f32), axis=0)
    _, gelu_pull = jax.vjp(functools.partial(jax.nn.gelu, approximate=False), inner)
    delta_inner = gelu_pull(against(delta_update, down_weight))[0].astype(bf16)
    up_weight_term = transposed(normed_low, delta_inner)
    up_bias_term = jnp.sum(delta_inner.astype(f32), axis=0)
    grad_normed = against(delta_inner, up_weight) + grad_two
    grad_one, first_gain_term, first_shift_term = norm_backward(grad_normed, scaled_one, inverse_one, first_gain)
    delta_branch = grad_one.astype(bf16)
    out_weight_term = transposed(mixed, delta_branch)
    out_bias_term = jnp.sum(delta_branch.astype(f32), axis=0)
    delta_mixed = against(delta_branch, out_weight).astype(bf16).reshape(heads_shape)
    delta_values = jnp.einsum("bhqk,bqhd->bkhd", attention_low, delta_mixed, preferred_element_type=f32)
    delta_values = delta_values.astype(bf16).reshape(count * length, width)
    grad_attention = jnp.einsum("bqhd,bkhd->bhqk", delta_mixed, value_rows, preferred_element_type=f32)
    row_total = jnp.sum(attention * grad_attention, axis=-1, keepdims=True)
    delta_scores = (attention * (grad_attention - row_total)).astype(bf16)
    delta_queries = jnp.einsum("bhqk,bkhd->bqhd", delta_scores, key_rows, preferred_element_type=f32) * score_scale
    delta_queries = delta_queries.astype(bf16).reshape(count * length, width)
    delta_keys = jnp.einsum("bhqk,bqhd->bkhd", delta_scores, queries, preferred_element_type=f32) * score_scale
    delta_keys = delta_keys.astype(bf16).reshape(count * length, width)
    query_weight_term = transposed(rows, delta_queries)
    query_bias_term = jnp.sum(delta_queries.astype(f32), axis=0)
    key_weight_term = transposed(rows, delta_keys)
    value_weight_term = transposed(rows, delta_values)
    value_bias_term = jnp.sum(delta_values.astype(f32), axis=0)
    input_grad = (
        grad_one
        + against(delta_queries, query_weight)
        + against(delta_keys, key_weight)
        + against(delta_values, value_weight)
    )
    terms = (
        query_weight_term,
        query_bias_term,
        key_weight_term,
        value_weight_term,
        value_bias_term,
        out_weight_term,
        out_bias_term,
        first_gain_term,
        first_shift_term,
        up_weight_term,
        up_bias_term,
        down_weight_term,
        down_bias_term,
        second_gain_term,
        second_shift_term,
    )
    return (input_grad.reshape(count, length, width), terms)


class Place:
    def __init__(self):
        chip = lax.axis_index("fsdp")
        core = lax.axis_index("dp")
        z, y, x = chip // 4, (chip // 2) % 2, chip % 2
        self.z, self.y, self.x, self.core = z, y, x, core
        first = 1 - core
        self.own = (y, x)
        self.near = (jnp.where(core == 0, y, 1 - y), jnp.where(core == 0, 1 - x, x))
        self.far = (jnp.where(core == 0, 1 - y, y), jnp.where(core == 0, x, 1 - x))
        self.across = (1 - y, 1 - x)
        self.up = [(z + d) % 4 for d in (1, 2, 3)]
        self.down = [(z + 4 - d) % 4 for d in (1, 2, 3)]
        self.column = [self.device(q, y, x, core) for q in self.up]
        self.near_device = self.device(z, *self.near, core)
        self.far_device = self.device(z, *self.far, core)
        self.partner = self.device(z, y, x, 1 - core)

    def device(self, z, y, x, core):
        return (z * 4 + y * 2 + x, core)

    def greet(self):
        barrier = pltpu.get_barrier_semaphore()
        for peer in self.column + [self.near_device, self.far_device, self.partner]:
            pl.semaphore_signal(barrier, 1, device_id=peer, device_id_type=MESH)
        return barrier


def half(kind, core):
    if kind == "w":
        return (slice(None), pl.ds(pl.multiple_of(core * 384, 128), 384))
    if kind == "d":
        return (slice(None), pl.ds(pl.multiple_of(core * 128, 128), 128))
    return (pl.ds(pl.multiple_of(core * 8, 8), 8), slice(None))


UNIT = {"w": (48, 768), "d": (192, 256), "v": (16, 128)}
HALF = {"w": (48, 384), "d": (192, 128), "v": (8, 128)}
TYPE = {"w": bf16, "d": bf16, "v": f32}
COUNT = {"w": 8, "d": 3, "v": 1}
GATHER = [("v", 0)] + [("w", i) for i in range(8)] + [("d", i) for i in range(3)]
REDUCE = [("d", i) for i in range(3)] + [("w", i) for i in (4, 5, 6, 7, 3, 2, 1, 0)] + [("v", 0)]
JOBS = len(GATHER)
SMALL = (1, 4, 6, 7, 8, 12, 13, 14)
QUERY_BIAS, VALUE_BIAS, OUT_BIAS, FIRST_GAIN, FIRST_SHIFT, DOWN_BIAS, SECOND_GAIN, SECOND_SHIFT = range(8)
ORDER = (
    "g1.0", "g1.1", "g2.0", "g1.2", "g2.1", "g1.3", "g2.2", "g3.0", "g4.0", "g1.4",
    "g2.3", "g3.1", "g4.1", "g1.5", "g2.4", "g3.2", "g4.2", "g5.0", "g1.6", "g2.5",
    "g3.3", "g4.3", "g5.1", "g6.0", "spread.0", "g1.7", "g2.6", "g3.4", "g4.4", "g5.2",
    "g6.1", "project.0", "g1.8", "g2.7", "g3.5", "g4.5", "g5.3", "g6.2", "project.1", "g1.9",
    "g2.8", "g3.6", "g4.6", "g5.4", "g6.3", "project.2", "attend.0", "g1.10", "g2.9", "g3.7",
    "g4.7", "attend.1", "g5.5", "g6.4", "g1.11", "g2.10", "attend.2", "g3.8", "g4.8", "g5.6",
    "g6.5", "first_norm.0", "expand.0", "g2.11", "g3.9", "g4.9", "g5.7", "g6.6", "expand.1", "g3.10",
    "g4.10", "g5.8", "g6.7", "expand.2", "g3.11", "g4.11", "g5.9", "g6.8", "expand.3", "g5.10",
    "g6.9", "contract.0", "g5.11", "g6.10", "contract.1", "g6.11", "contract.2", "second_norm.0", "down_grad.0", "r0.0",
    "down_grad.1", "r0.1", "down_grad.2", "r0.2", "inner_grad.0", "up_grad.0", "r1.0", "r0.3", "inner_grad.1", "up_grad.1",
    "r1.1", "r0.4", "inner_grad.2", "up_grad.2", "r1.2", "r0.5", "inner_grad.3", "up_grad.3", "r1.3", "r2.0",
    "r0.6", "up_pull.0", "r1.4", "r2.1", "first_pull.0", "out_grad.0", "r0.7", "mixed_pull.0", "attend_pull.0", "r1.5",
    "r2.2", "r3.0", "attend_pull.1", "attend_pull.2", "attend_pull.3", "attend_pull.4", "attend_pull.5", "head_grad.0", "r0.8", "head_grad.1",
    "r1.6", "r2.3", "r3.1", "r0.9", "head_grad.2", "r1.7", "r2.4", "r3.2", "r4.0", "r0.10",
    "vectors.0", "r1.8", "r2.5", "r3.3", "r4.1", "r0.11", "input_pull.0", "r1.9", "r2.6", "r3.4",
    "r4.2", "input_pull.1", "r1.10", "r2.7", "r3.5", "r4.3", "r1.11", "r2.8", "r3.6", "r4.4",
    "r2.9", "r3.7", "r4.5", "r2.10", "r3.8", "r4.6", "r2.11", "r3.9", "r4.7", "r3.10",
    "r4.8", "r3.11", "r4.9", "r4.10", "r4.11",
)
D = 768
TILE = 192
PAIRS = HEADS // 2
BLOCK = 128


class Sender:
    def __init__(self, place):
        self.place = place
        self.started = []

    def copy(self, source, target, send, receive, device):
        return pltpu.make_async_remote_copy(
            source, target, send, receive, device_id=device, device_id_type=MESH
        )

    def send(self, source, target, send, receive, device):
        copy = self.copy(source, target, send, receive, device)
        copy.start()
        self.started.append(copy)

    def arrived(self, target, send, receive):
        self.copy(target, target, send, receive, self.place.partner).wait_recv()

    def finish(self):
        for copy in self.started:
            copy.wait_send()


def gather_steps(place, sender, given, whole, own_s, z_s, z_r, h_s, h_r, p_s, p_r):
    z, core = place.z, place.core
    local = [
        pltpu.make_async_copy(
            given(kind, i, half(kind, core)),
            whole[kind].at[(i, z, *place.own, *half(kind, core))],
            own_s.at[n],
        )
        for n, (kind, i) in enumerate(GATHER)
    ]
    for copy in local:
        copy.start()

    def unit(n, q):
        kind, i = GATHER[n]
        return whole[kind].at[(i, q, *place.own, *half(kind, core))]

    def column(n, spot, core=core):
        kind, i = GATHER[n]
        return whole[kind].at[(i, slice(None), *spot, *half(kind, core))]

    def pass_on(n, spot, j, to):
        part = column(n, spot)
        sender.send(part, part, h_s.at[n, j], h_r.at[n, j], to)

    def share(n, spot, j):
        part = column(n, spot)
        sender.send(part, part, p_s.at[n, j], p_r.at[n, j], place.partner)

    def first(n):
        local[n].wait()
        for j in range(3):
            sender.send(unit(n, z), unit(n, z), z_s.at[n, j], z_r.at[n, j], place.column[j])

    def second(n):
        for j in range(3):
            sender.arrived(unit(n, place.down[j]), z_s.at[n, j], z_r.at[n, j])
        pass_on(n, place.own, 0, place.near_device)
        pass_on(n, place.own, 1, place.far_device)
        share(n, place.own, 0)

    def third(n):
        sender.arrived(column(n, place.near), h_s.at[n, 0], h_r.at[n, 0])
        pass_on(n, place.near, 2, place.far_device)
        share(n, place.near, 1)

    def fourth(n):
        sender.arrived(column(n, place.far), h_s.at[n, 1], h_r.at[n, 1])
        share(n, place.far, 2)

    def fifth(n):
        sender.arrived(column(n, place.across), h_s.at[n, 2], h_r.at[n, 2])
        share(n, place.across, 3)

    def complete(n):
        for j, spot in enumerate((place.own, place.far, place.near, place.across)):
            sender.arrived(column(n, spot, 1 - core), p_s.at[n, j], p_r.at[n, j])

    return {"g1": first, "g2": second, "g3": third, "g4": fourth, "g5": fifth, "g6": complete}


def reduce_steps(place, sender, total, shared, far, near, high, final, out, p_s, p_r, h_s, h_r, z_s, z_r, f_s, f_r, o_s):
    z, core = place.z, place.core

    def add(n, spot, more):
        kind, i = REDUCE[n]
        ref = total(kind, i)

        at = (core, slice(None), *spot)
        ref[at] = (ref[at].astype(f32) + more[...].astype(f32)).astype(TYPE[kind])

    def column(n, spot):
        return total(*REDUCE[n]).at[(core, slice(None), *spot)]

    def give(n):
        kind, i = REDUCE[n]
        sender.send(total(kind, i).at[1 - core], shared[kind].at[i], p_s.at[n], p_r.at[n], place.partner)

    def first(n):
        kind, i = REDUCE[n]
        sender.arrived(shared[kind].at[i], p_s.at[n], p_r.at[n])
        for j, spot in enumerate((place.across, place.far)):
            add(n, spot, shared[kind].at[(i, slice(None), *spot)])
            sender.send(column(n, spot), far[kind].at[i, j], h_s.at[n, j], h_r.at[n, j], place.far_device)
        for spot in (place.near, place.own):
            add(n, spot, shared[kind].at[(i, slice(None), *spot)])

    def second(n):
        kind, i = REDUCE[n]
        sender.arrived(far[kind].at[i, 0], h_s.at[n, 0], h_r.at[n, 0])
        add(n, place.near, far[kind].at[i, 0])
        sender.send(column(n, place.near), near[kind].at[i], h_s.at[n, 2], h_r.at[n, 2], place.near_device)

    def third(n):
        kind, i = REDUCE[n]
        sender.arrived(far[kind].at[i, 1], h_s.at[n, 1], h_r.at[n, 1])
        add(n, place.own, far[kind].at[i, 1])
        sender.arrived(near[kind].at[i], h_s.at[n, 2], h_r.at[n, 2])
        add(n, place.own, near[kind].at[i])
        for j in range(3):
            part = total(kind, i).at[(core, place.up[j], *place.own)]
            sender.send(part, high[kind].at[i, j], z_s.at[n, j], z_r.at[n, j], place.column[j])

    def fourth(n):
        kind, i = REDUCE[n]
        mine = total(kind, i)[(core, z, *place.own)].astype(f32)
        for j in range(3):
            sender.arrived(high[kind].at[i, j], z_s.at[n, j], z_r.at[n, j])
            mine = mine + high[kind][i, j].astype(f32)
        final[kind][i] = mine
        mine_out = out(kind, i, core)
        sender.send(final[kind].at[i], mine_out, f_s.at[n], f_r.at[n], place.partner)
        pltpu.make_async_copy(final[kind].at[i], mine_out, o_s.at[n]).start()

    def stored(n):
        kind, i = REDUCE[n]
        pltpu.make_async_copy(final[kind].at[i], out(kind, i, core), o_s.at[n]).wait()
        sender.arrived(out(kind, i, 1 - core), f_s.at[n], f_r.at[n])

    return {"r0": give, "r1": first, "r2": second, "r3": third, "r4": fourth, "r5": stored}


def iota(shape, axis):
    return lax.broadcasted_iota(jnp.int32, shape, axis)


def loop(count, body):
    def step(i, _):
        body(i)
        return 0

    lax.fori_loop(0, count, step, 0)


def tile_rows(i):
    return pl.ds(pl.multiple_of(i * TILE, TILE), TILE)


def flat(value):
    return value.reshape(math.prod(value.shape[:-1]), value.shape[-1])


def spread_table():
    return jnp.where(iota((128, D), 1) % 48 == iota((128, D), 0), 1.0, 0.0)


def spread_tables_wide():
    l = iota((128, D), 1) % 192
    j = iota((128, D), 0)
    return jnp.where(l == j, 1.0, 0.0), jnp.where(l == j + 128, 1.0, 0.0)


def wide_rows():
    row = iota((64, D), 0)
    mine = iota((64, D), 1) // 192 == row // 16
    return mine & (row % 16 == 8), mine & (row % 16 == 9)


def total_over(mask, value):
    return jnp.sum(jnp.where(mask, value, 0.0), axis=0, keepdims=True)


def fused_kernel(
    long_lengths,
    short_lengths,
    long_inputs,
    short_inputs,
    long_cotangent,
    short_cotangent,
    wq_in,
    wk_in,
    wv_in,
    wo_in,
    up_in,
    down_in,
    v_in,
    long_output,
    short_output,
    long_grad,
    short_grad,
    wq_out,
    wk_out,
    wv_out,
    wo_out,
    up_out,
    down_out,
    v_out,
    w,
    d,
    v,
    shared_w,
    shared_d,
    shared_v,
    far_w,
    far_d,
    far_v,
    near_w,
    near_d,
    near_v,
    high_w,
    high_d,
    high_v,
    final_w,
    final_d,
    final_v,
    total_d,
    total_v,
    x,
    c,
    q,
    k,
    vl,
    mixed,
    xhat,
    inverse,
    low,
    hidden,
    slope,
    acc,
    delta,
    vec,
    stats,
    up_bias,
    small,
    up_bias_sum,
    own_s,
    gz_s,
    gz_r,
    gh_s,
    gh_r,
    gp_s,
    gp_r,
    p_s,
    p_r,
    h_s,
    h_r,
    z_s,
    z_r,
    f_s,
    f_r,
    o_s,
    in_s,
    out_s,
):
    place = Place()
    barrier = place.greet()
    sender = Sender(place)
    matrices_in = (wq_in, wk_in, wv_in, wo_in)
    matrices_out = (wq_out, wk_out, wv_out, wo_out)

    def given(kind, i, at):
        rows, cols = at
        if kind == "v":
            return v_in.at[rows, cols]
        core = place.core
        if kind == "d":
            return down_in.at[:, pl.ds(pl.multiple_of(256 * i + core * 128, 128), 128)]
        if i < 4:
            return matrices_in[i].at[rows, cols]
        return up_in.at[:, pl.ds(pl.multiple_of(D * (i - 4) + core * 384, 128), 384)]

    def out(kind, i, core):
        rows, cols = half(kind, core)
        if kind == "v":
            return v_out.at[rows, cols]
        if kind == "d":
            return down_out.at[:, pl.ds(pl.multiple_of(256 * i + core * 128, 128), 128)]
        if i < 4:
            return matrices_out[i].at[rows, cols]
        return up_out.at[:, pl.ds(pl.multiple_of(D * (i - 4) + core * 384, 128), 384)]

    def total(kind, i):
        if kind == "d":
            return total_d.at[i]
        if kind == "v":
            return total_v
        return hidden.at[i - 4] if i >= 4 else slope.at[i]

    steps = gather_steps(
        place, sender, given, {"w": w, "d": d, "v": v}, own_s, gz_s, gz_r, gh_s, gh_r, gp_s, gp_r
    )
    steps |= reduce_steps(
        place,
        sender,
        total,
        {"w": shared_w, "d": shared_d, "v": shared_v},
        {"w": far_w, "d": far_d, "v": far_v},
        {"w": near_w, "d": near_d, "v": near_v},
        {"w": high_w, "d": high_d, "v": high_v},
        {"w": final_w, "d": final_d, "v": final_v},
        out,
        p_s,
        p_r,
        h_s,
        h_r,
        z_s,
        z_r,
        f_s,
        f_r,
        o_s,
    )

    count, length, _ = long_inputs.shape
    short = short_inputs.shape[1]

    def groups(buffer, long_ref, short_ref, outward, s):
        copies = []
        for i in range(count):
            copies.append((buffer.at[i * length : (i + 1) * length], long_ref.at[i]))
        for i in range(count):
            start = count * length + i * short
            copies.append((buffer.at[start : start + short], short_ref.at[i]))
        return [
            pltpu.make_async_copy(*((a, b) if outward else (b, a)), s.at[i]) for i, (a, b) in enumerate(copies)
        ]

    x_copies = groups(x, long_inputs, short_inputs, False, in_s.at[0])
    c_copies = groups(c, long_cotangent, short_cotangent, False, in_s.at[1])
    for copy in x_copies + c_copies:
        copy.start()
    small[...] = jnp.zeros_like(small)
    up_bias_sum[...] = jnp.zeros_like(up_bias_sum)
    total_v[...] = jnp.zeros_like(total_v)
    pl.semaphore_wait(barrier, 6)

    def weight(i):
        return flat(w[i])

    def row(at):
        return vec[at : at + 1, :]


    def spread():
        wide = matmul(flat(v[0]).astype(bf16), spread_table().astype(bf16))
        mine = iota((256, D), 1) // 48 == iota((256, D), 0) // 16
        vec[...] = jnp.sum(jnp.where(mine, wide, 0.0).reshape(16, 16, D), axis=0)
        table_a, table_b = spread_tables_wide()
        mask_a, mask_b = wide_rows()
        for j in range(4):
            unit = flat(v[0, j]).astype(bf16)
            up_bias[j : j + 1, :] = total_over(mask_a, matmul(unit, table_a.astype(bf16))) + total_over(
                mask_b, matmul(unit, table_b.astype(bf16))
            )

    def project(i, target, bias, scale=1.0):
        result = matmul(x[...], weight(i))
        if bias is not None:
            result = result + row(bias)
        result = (result.astype(bf16) * scale).astype(bf16)
        for p in range(PAIRS):
            target[p] = result[:, 128 * p : 128 * p + 128]

    left_lanes = iota((BLOCK, BLOCK), 1) < HEAD_DIM

    def stacked(value):
        none = jnp.zeros_like(value)
        return jnp.concatenate([jnp.where(left_lanes, value, none), jnp.where(left_lanes, none, value)], axis=0)

    def picked(value):
        return jnp.where(left_lanes, value[:BLOCK], value[BLOCK:])

    def live_keys(b, is_long):
        key = iota((BLOCK, BLOCK), 0)
        if is_long:
            return key < long_lengths[b]
        left = key < short
        limit = jnp.where(left, short_lengths[2 * b], short + short_lengths[2 * b + 1])
        return (key < limit) & (left == (iota((BLOCK, BLOCK), 1) < short))

    def block_rows(b, is_long):
        start = b * BLOCK if is_long else count * length + b * BLOCK
        return pl.ds(pl.multiple_of(start, BLOCK), BLOCK)

    def block_scores(p, rows, live):
        scores = against(stacked(k[p, rows, :]), q[p, rows, :])
        return [jnp.where(live, scores[BLOCK * head : BLOCK * head + BLOCK], masked_score) for head in range(2)]

    def attend(b, is_long):
        rows = block_rows(b, is_long)
        live = live_keys(b, is_long)
        at = b if is_long else b + count
        results = []
        for p in range(PAIRS):
            parts = []
            for head, part in enumerate(block_scores(p, rows, live)):
                highest = jnp.max(part, axis=0, keepdims=True)
                raised = jnp.exp(part - highest)
                scale = 1.0 / jnp.sum(raised, axis=0, keepdims=True)
                stats[at, 2 * p + head : 2 * p + head + 1, :] = highest
                stats[at, HEADS + 2 * p + head : HEADS + 2 * p + head + 1, :] = scale
                parts.append((raised * scale).astype(bf16))
            both = jnp.concatenate(parts, axis=0)
            results.append(transposed(both, stacked(vl[p, rows, :])).astype(bf16))
        mixed[rows, :] = jnp.concatenate(results, axis=1)

    def branch():
        acc[...] = matmul(mixed[...], weight(3)) + row(OUT_BIAS)

    def first_norm(t):
        rows = tile_rows(t)
        normed, scaled, inv = norm_forward(x[rows, :].astype(f32) + acc[rows, :], row(FIRST_GAIN), row(FIRST_SHIFT))
        xhat[rows, :] = scaled
        inverse[rows, :] = inv
        low[rows, :] = normed.astype(bf16)

    def put(buffer, j, value):
        for side in range(2):
            buffer[j, side] = value[:, 384 * side : 384 * side + 384].reshape(4, 2, 2, 48, 384)

    def take(buffer, j):
        return jnp.concatenate([flat(buffer[j, side]) for side in range(2)], axis=1)

    def expand(j):
        inner = matmul(low[...], weight(4 + j)) + up_bias[j : j + 1, :]
        phi = 0.5 + 0.5 * lax.erf(inner * 0.5**0.5)
        put(hidden, j, (inner * phi).astype(bf16))
        density = jnp.exp(-0.5 * inner * inner) * (2 * math.pi) ** -0.5
        put(slope, j, (phi + inner * density).astype(bf16))

    def contract(n):
        update = row(DOWN_BIAS)[:, 256 * n : 256 * n + 256]
        for j in range(4):
            update = update + matmul(take(hidden, j), flat(d[n, j]))
        acc[:, 256 * n : 256 * n + 256] = update

    def tally(at, value):
        small[at : at + 1, :] += jnp.sum(value, axis=0, keepdims=True)

    def norm_pull(upstream, scaled, inv, gain):
        g = upstream * gain
        plain = jnp.mean(g, axis=-1, keepdims=True)
        cross = jnp.mean(g * scaled, axis=-1, keepdims=True)
        return inv * (g - plain - scaled * cross)

    def second_norm(t):
        rows = tile_rows(t)
        normed = xhat[rows, :] * row(FIRST_GAIN) + row(FIRST_SHIFT)
        final, scaled, inv = norm_forward(normed + acc[rows, :], row(SECOND_GAIN), row(SECOND_SHIFT))
        upstream = c[rows, :].astype(f32)
        c[rows, :] = final.astype(bf16)
        tally(SECOND_GAIN, upstream * scaled)
        tally(SECOND_SHIFT, upstream)
        grad = norm_pull(upstream, scaled, inv, row(SECOND_GAIN))
        acc[rows, :] = grad
        lowered = grad.astype(bf16)
        delta[rows, :] = lowered
        tally(DOWN_BIAS, lowered.astype(f32))


    def down_grad(n):
        for j in range(4):
            grad = transposed(take(hidden, j), delta[:, 256 * n : 256 * n + 256]).astype(bf16)
            for side in range(2):
                total_d[n, side, j] = grad[:, 128 * side : 128 * side + 128].reshape(2, 2, 192, 128)

    def inner_grad(j):
        pulled = against(delta[...], jnp.concatenate([flat(d[n, j]) for n in range(3)], axis=1))
        inner = (pulled * take(slope, j).astype(f32)).astype(bf16)
        put(slope, j, inner)
        up_bias_sum[j : j + 1, :] = jnp.sum(inner.astype(f32), axis=0, keepdims=True)

    def weight_grad(left, right, buffer, slot):
        put(buffer, slot, transposed(left[...], right()).astype(bf16))

    def up_pull():
        grad = acc[...]
        for j in range(4):
            grad = grad + against(take(slope, j), weight(4 + j))
        acc[...] = grad

    def first_pull(t):
        rows = tile_rows(t)
        upstream = acc[rows, :]
        scaled = xhat[rows, :]
        tally(FIRST_GAIN, upstream * scaled)
        tally(FIRST_SHIFT, upstream)
        grad = norm_pull(upstream, scaled, inverse[rows, :], row(FIRST_GAIN))
        acc[rows, :] = grad
        lowered = grad.astype(bf16)
        delta[rows, :] = lowered
        tally(OUT_BIAS, lowered.astype(f32))

    def mixed_pull():
        mixed[...] = against(delta[...], weight(3)).astype(bf16)

    def attend_pull(b, is_long):
        rows = block_rows(b, is_long)
        live = live_keys(b, is_long)
        at = b if is_long else b + count
        results = []
        for p in range(PAIRS):
            down = mixed[rows, 128 * p : 128 * p + 128]
            probs = []
            for head, part in enumerate(block_scores(p, rows, live)):
                highest = stats[at, 2 * p + head : 2 * p + head + 1, :]
                scale = stats[at, HEADS + 2 * p + head : HEADS + 2 * p + head + 1, :]
                probs.append(jnp.exp(part - highest) * scale)
            both = jnp.concatenate(probs, axis=0).astype(bf16)
            grad_values = picked(matmul(both, down))
            grad_probs = against(stacked(vl[p, rows, :]), down)
            parts = []
            for head in range(2):
                part = grad_probs[BLOCK * head : BLOCK * head + BLOCK]
                mean = jnp.sum(probs[head] * part, axis=0, keepdims=True)
                parts.append((probs[head] * (part - mean)).astype(bf16))
            grad_scores = jnp.concatenate(parts, axis=0)
            grad_queries = transposed(grad_scores, stacked(k[p, rows, :])) * HEAD_DIM**-0.5
            grad_keys = picked(matmul(grad_scores, q[p, rows, :]))
            results.append((grad_queries.astype(bf16), grad_keys.astype(bf16), grad_values.astype(bf16)))
        for p, (grad_queries, grad_keys, grad_values) in enumerate(results):
            q[p, rows, :] = grad_queries
            k[p, rows, :] = grad_keys
            vl[p, rows, :] = grad_values

    def joined(heads):
        return lambda: jnp.concatenate([heads[p] for p in range(PAIRS)], axis=1)

    def head_sum(at, heads):
        for p in range(PAIRS):
            small[at : at + 1, 128 * p : 128 * p + 128] = jnp.sum(heads[p].astype(f32), axis=0, keepdims=True)

    def input_pull(t):
        rows = slice(384 * t, 384 * t + 384)
        grad = acc[rows, :]
        for i, heads in enumerate((q, k, vl)):
            grad = grad + against(jnp.concatenate([heads[p, rows, :] for p in range(PAIRS)], axis=1), weight(i))
        acc[rows, :] = grad

    def exact(left, right):
        return lax.dot_general(
            left, right, (((1,), (1,)), ((), ())), precision=lax.Precision.HIGHEST, preferred_element_type=f32
        )

    def vectors_out():
        mine = iota((16, 8, D), 2) // 48 == iota((16, 8, D), 0)
        pieces = jnp.where(mine, jnp.broadcast_to(small[...][None], (16, 8, D)), 0.0).reshape(128, D)
        total_v[0] = exact(pieces, spread_table()).reshape(4, 2, 2, 8, 128)
        table_a, table_b = spread_tables_wide()
        mask_a, mask_b = wide_rows()
        for j in range(4):
            sums = jnp.broadcast_to(up_bias_sum[j : j + 1, :], (64, D))
            wide = exact(jnp.where(mask_a, sums, 0.0), table_a) + exact(jnp.where(mask_b, sums, 0.0), table_b)
            total_v[1, j] = wide.reshape(2, 2, 16, 128)[:, :, 8:, :]


    def wait_all(copies):
        for copy in copies:
            copy.wait()

    def start_all(copies):
        for copy in copies:
            copy.start()

    final_copies = groups(c, long_output, short_output, True, out_s.at[0])
    grad_copies = groups(acc, long_grad, short_grad, True, out_s.at[1])

    def project_all(i):
        if i == 0:
            wait_all(x_copies)
        project(i, (q, k, vl)[i], (QUERY_BIAS, None, VALUE_BIAS)[i], HEAD_DIM**-0.5 if i == 0 else 1.0)

    def attend_all(i):
        if 2 * i < count:
            loop(2, lambda b: attend(2 * i + b, True))
        else:
            loop(count // 2, lambda b: attend(b, False))

    def normalise():
        branch()
        loop(4, first_norm)

    def finish():
        wait_all(c_copies)
        loop(4, second_norm)
        start_all(final_copies)

    def attend_pull_all(b):
        attend_pull(b % count, b < count)

    def head_grad(i):
        weight_grad(x, joined((vl, k, q)[i]), slope, 2 - i)

    def vector_grads():
        head_sum(QUERY_BIAS, q)
        head_sum(VALUE_BIAS, vl)
        vectors_out()

    def input_pull_all(t):
        input_pull(t)
        if t == 1:
            start_all(grad_copies)

    steps |= {
        "spread": lambda _: spread(),
        "project": project_all,
        "attend": attend_all,
        "first_norm": lambda _: normalise(),
        "expand": expand,
        "contract": contract,
        "second_norm": lambda _: finish(),
        "down_grad": down_grad,
        "inner_grad": inner_grad,
        "up_grad": lambda j: weight_grad(low, lambda: take(slope, j), hidden, j),
        "up_pull": lambda _: up_pull(),
        "first_pull": lambda _: loop(4, first_pull),
        "out_grad": lambda _: weight_grad(mixed, lambda: delta[...], slope, 3),
        "mixed_pull": lambda _: mixed_pull(),
        "attend_pull": attend_pull_all,
        "head_grad": head_grad,
        "vectors": lambda _: vector_grads(),
        "input_pull": input_pull_all,
    }
    for entry in ORDER:
        name, at = entry.split(".")
        steps[name](int(at))
    sender.finish()
    wait_all(final_copies + grad_copies)
    for n in range(JOBS):
        steps["r5"](n)


def fused(lengths, rows, matrices, vectors):
    long_inputs, short_inputs = rows[:2]
    count = long_inputs.shape[0]
    tokens = count * (long_inputs.shape[1] + short_inputs.shape[1])
    n = JOBS
    anywhere = pl.BlockSpec(memory_space=pl.ANY)
    scalar = pl.BlockSpec(memory_space=pltpu.SMEM)
    spots = (4, 2, 2)
    scratch = [pltpu.VMEM((COUNT[kind], *spots, *UNIT[kind]), TYPE[kind]) for kind in "wdv"]
    for lead in (spots, (2, 4), (4,), (3,)):
        scratch += [pltpu.VMEM((COUNT[kind], *lead, *HALF[kind]), TYPE[kind]) for kind in "wdv"]
    scratch += [pltpu.VMEM((COUNT[kind], *HALF[kind]), f32) for kind in "wdv"]
    scratch += [pltpu.VMEM((3, 2, *spots, *HALF["d"]), bf16), pltpu.VMEM((2, *spots, *HALF["v"]), f32)]
    heads = pltpu.VMEM((PAIRS, tokens, 128), bf16)
    low = pltpu.VMEM((tokens, D), bf16)
    high = pltpu.VMEM((tokens, D), f32)
    wide = pltpu.VMEM((4, 2, *spots, *HALF["w"]), bf16)
    scratch += [low, low, heads, heads, heads, low, high, pltpu.VMEM((tokens, 1), f32), low, wide, wide, high, low]
    scratch += [pltpu.VMEM((16, D), f32), pltpu.VMEM((count + count // 2, 2 * HEADS, BLOCK), f32), pltpu.VMEM((4, D), f32), pltpu.VMEM((8, D), f32), pltpu.VMEM((4, D), f32)]
    scratch += [DMA((n,))] + [DMA((n, 3))] * 4 + [DMA((n, 4))] * 2
    scratch += [DMA((n,))] * 2 + [DMA((n, 3))] * 4 + [DMA((n,))] * 2 + [DMA((n,)), DMA((2, 2 * count)), DMA((2, 2 * count))]
    results = [jax.ShapeDtypeStruct(a.shape, bf16) for a in rows[:2]]
    results += [jax.ShapeDtypeStruct(a.shape, f32) for a in rows[:2]]
    results += [jax.ShapeDtypeStruct(a.shape, f32) for a in matrices]
    results += [jax.ShapeDtypeStruct((16, 128), f32)]
    return pl.pallas_call(
        fused_kernel,
        out_shape=results,
        in_specs=[scalar] * 2 + [anywhere] * 11,
        out_specs=[anywhere] * 11,
        scratch_shapes=scratch,
        compiler_params=pltpu.CompilerParams(
            collective_id=0, has_side_effects=True, vmem_limit_bytes=61 << 20
        ),
        name="layer",
    )(*lengths, *rows, *matrices, vectors)


def deliver_kernel(*refs):
    sources, targets, held = refs[:11], refs[11:30], refs[30:41]
    in_s, out_s = refs[41:]
    loads = [pltpu.make_async_copy(sources[at], held[at], in_s.at[at]) for at in range(11)]
    stores = [pltpu.make_async_copy(held[at], targets[at], out_s.at[at]) for at in range(10)]
    for load in loads:
        load.start()
    for load, store in zip(loads, stores):
        load.wait()
        store.start()
    loads[10].wait()
    v = held[10]
    for at in range(8):
        targets[10 + at][...] = v[at, :48]
    targets[18][0:128] = v[8]
    targets[18][128:192] = v[9, :64]
    for store in stores:
        store.wait()


def deliver(results):
    anywhere = pl.BlockSpec(memory_space=pl.ANY)
    vmem = pl.BlockSpec(memory_space=pltpu.VMEM)
    vectors = [jax.ShapeDtypeStruct((48,), f32)] * 8 + [jax.ShapeDtypeStruct((192,), f32)]
    return pl.pallas_call(
        deliver_kernel,
        out_shape=[jax.ShapeDtypeStruct(a.shape, a.dtype) for a in results[:10]] + vectors,
        in_specs=[anywhere] * 11,
        out_specs=[anywhere] * 10 + [vmem] * 9,
        scratch_shapes=[pltpu.VMEM(a.shape, a.dtype) for a in results] + [DMA((11,)), DMA((10,))],
        compiler_params=pltpu.CompilerParams(vmem_limit_bytes=60 << 20),
        name="deliver",
    )(*results)


def layer_by_kernel(long_inputs, short_inputs, long_lengths, short_lengths, long_cotangent, short_cotangent, *shards):
    small = jnp.pad(jnp.stack([shards[i] for i in SMALL]), ((0, 0), (0, 80)))
    tail = jnp.pad(shards[10], (0, 64)).reshape(2, 128)
    vectors = jnp.pad(jnp.concatenate([small, tail]), ((0, 6), (0, 0))).astype(f32)
    results = fused(
        (long_lengths, short_lengths),
        (long_inputs, short_inputs, long_cotangent, short_cotangent),
        tuple(shards[i] for i in (0, 2, 3, 5, 9, 11)),
        vectors,
    )
    results = deliver(results)
    *rows, wq, wk, wv, wo, up, down = results[:10]
    *small, up_bias = results[10:]
    done = {0: wq, 2: wk, 3: wv, 5: wo, 9: up, 11: down, 10: up_bias, **dict(zip(SMALL, small))}
    return (*rows, *(done[i] for i in range(15)))


def gathered_by_collectives(shards):
    full = tuple(lax.all_gather(shard, "fsdp", axis=0, tiled=True) for shard in shards)
    return tuple(a.astype(f32) if a.ndim == 1 else a for a in full)


def reduced_by_collectives(totals):
    reduced = lax.psum_scatter(totals, "fsdp", scatter_dimension=0, tiled=True)
    low = jax.tree.map(lambda a: a.astype(bf16), reduced)
    return jax.tree.map(lambda a: a.astype(f32), lax.psum(low, "dp"))


def layer_by_collectives(
    long_inputs, short_inputs, long_lengths, short_lengths, long_cotangent, short_cotangent, *shards
):
    weights = gathered_by_collectives(shards)
    long_output, long_saved = layer_pass(weights, long_inputs, long_lengths)
    short_output, short_saved = layer_pass(weights, short_inputs, short_lengths)
    long_grad, long_terms = layer_back(weights, long_saved, long_cotangent)
    short_grad, short_terms = layer_back(weights, short_saved, short_cotangent)
    totals = tuple((first + second for first, second in zip(long_terms, short_terms)))
    reduced = reduced_by_collectives(totals)
    return (long_output.astype(bf16), short_output.astype(bf16), long_grad, short_grad, *reduced)


def solution(mesh):
    rows = P(("fsdp", "dp"), None, None)
    count = P(("fsdp", "dp"))
    matrix, vector = P("fsdp", None), P("fsdp")
    params = tuple(matrix if i in (0, 2, 3, 5, 9, 11) else vector for i in range(15))
    by_kernel = mesh.shape["fsdp"] == 16 and mesh.shape["dp"] == 2
    return jax.shard_map(
        layer_by_kernel if by_kernel else layer_by_collectives,
        mesh=mesh,
        in_specs=(rows, rows, count, count, rows, rows, *params),
        out_specs=(rows, rows, rows, rows, *params),
        check_vma=False,
    )
```
